512 devices in a mesh: seq: 64 (over y, z), head: 8 (over x, core).
Axes of the slice: x: 4, y: 8, z: 8, core: 2. Of those that a mesh axis runs over, the one named last changes fastest.
Arguments:
- hidden_state: bfloat16 [4, 8192], P(None, 'seq'), may hold values from -70 to 70
- attn_gain: bfloat16 [8192], P('seq'), may hold values from 0.099609375 to 1.8984375
- query_key_value_weight: bfloat16 [8192, 10240], P('seq', 'head'), may hold values from -0.0625 to 0.0625
- key_page_cache: bfloat16 [1024, 128, 1024], P('seq', None, 'head'), may hold values from -200 to 200
- value_page_cache: bfloat16 [1024, 128, 1024], P('seq', None, 'head'), may hold values from -11 to 11
- page_table: int32 [4, 256], replicated, may hold values from 0 to 1023, as said below
- lengths: int32 [4], replicated, may hold values from 1 to 32767, as said below
- out_weight: bfloat16 [8192, 8192], P('head', 'seq'), may hold values from -0.0625 to 0.0625
- ffn_gain: bfloat16 [8192], P('seq'), may hold values from 0.099609375 to 1.8984375
- gate_weight: bfloat16 [8192, 28672], P('seq', 'head'), may hold values from -0.0625 to 0.0625
- up_weight: bfloat16 [8192, 28672], P('seq', 'head'), may hold values from -0.0625 to 0.0625
- down_weight: bfloat16 [28672, 8192], P('head', 'seq'), may hold values from -0.03125 to 0.03125
Outputs:
- attended: bfloat16 [4, 8192], P(None, 'seq')
- mixed: bfloat16 [4, 8192], P(None, 'seq')
The draws below stay inside these ranges and needn't reach their ends.
Inputs may be any that keep to these rules, and one draw needn't show every extreme that they name: `page_table`: entry [b, j] is the pool page holding positions j * 128 to (j + 1) * 128 - 1 of request b. Request b's pages are owned in turn: page j by (o_b + j) modulo the seq axis's size, for some o_b, so each seq device holds 4 pages of every request. Every pool page appears exactly once in the table. The new token of request b sits at position lengths[b]; in every draw one request has exactly 32767 cached tokens.
All inputs are finite; a program needn't handle non-finite values.
Results may differ from the reference program's by a relative error of at most 0.007.
Values may be sent and summed in bfloat16 or wider, within the bound.
A program may use at most 64 MiB of HBM per device.

```python
import math
import jax
import jax.numpy as jnp
from jax import lax

MODEL_WIDTH = 8192
FF = 28672
QUERY_HEADS = 64
KEY_VALUE_HEADS = 8
HEAD_SIZE = 128
BATCH_REQUESTS = 4
PAGE_TOKENS = 128
PAGES_DEV_REQ = 4
DEVICE_PAGES = 16
MAXP = 256
CONTEXT = 32768
POOL_PAGES = 1024
N_SEQ = 64


def draw_hidden_state(key, part):
    key = jax.random.fold_in(key, 11)
    child_keys = jax.random.split(key, 3)
    columns = jnp.arange(MODEL_WIDTH, dtype=jnp.float32) / MODEL_WIDTH
    random_base = jax.random.truncated_normal(child_keys[0], -4.0, 4.0, (BATCH_REQUESTS, MODEL_WIDTH), jnp.float32)
    slopes = 3.0 ** columns
    row_scales = jnp.exp(jax.random.uniform(child_keys[1], (BATCH_REQUESTS, 1), jnp.float32, jnp.log(0.3), jnp.log(3.0)))
    col_scales = jnp.exp(jax.random.uniform(child_keys[2], (MODEL_WIDTH,), jnp.float32, 0.0, jnp.log(3.0)))
    return (random_base * row_scales * col_scales * slopes * 0.5).astype(jnp.bfloat16)


def draw_key_page_cache(key, part):
    key = jax.random.fold_in(key, 23)
    child_keys = jax.random.split(key, 1)
    array_shape = (POOL_PAGES, PAGE_TOKENS, KEY_VALUE_HEADS * HEAD_SIZE)
    return jax.random.truncated_normal(child_keys[0], -4.0, 4.0, array_shape, jnp.float32).astype(jnp.bfloat16)


def draw_value_page_cache(key, part):
    key = jax.random.fold_in(key, 29)
    child_keys = jax.random.split(key, 3)
    complete_shape = (POOL_PAGES, PAGE_TOKENS, KEY_VALUE_HEADS, HEAD_SIZE)
    head_piece = jax.random.truncated_normal(child_keys[1], -2.5, 2.5, (1, 1, KEY_VALUE_HEADS, HEAD_SIZE), jnp.float32)
    page_piece = 0.5 * jax.random.truncated_normal(child_keys[2], -2.5, 2.5, (POOL_PAGES, 1, KEY_VALUE_HEADS, HEAD_SIZE), jnp.float32)
    random_base = jax.random.truncated_normal(child_keys[0], -4.0, 4.0, complete_shape, jnp.float32)
    return (random_base + head_piece + page_piece).reshape(POOL_PAGES, PAGE_TOKENS, KEY_VALUE_HEADS * HEAD_SIZE).astype(jnp.bfloat16)


def draw_page_table(key, part):
    key = jax.random.fold_in(key, 37)
    child_keys = jax.random.split(key, 2)
    owner_count = MAXP // PAGES_DEV_REQ
    first_owner = jax.random.randint(child_keys[0], (BATCH_REQUESTS, 1), 0, owner_count)
    logical = jnp.arange(MAXP, dtype=jnp.int32)[None, :]
    owners = (first_owner + logical) % owner_count
    local_slot = jnp.arange(BATCH_REQUESTS, dtype=jnp.int32)[:, None] * PAGES_DEV_REQ + logical // owner_count
    orders = jax.vmap(lambda sub_key: jax.random.permutation(sub_key, DEVICE_PAGES))(jax.random.split(child_keys[1], owner_count))
    return (owners * DEVICE_PAGES + orders[owners, local_slot]).astype(jnp.int32)


def draw_lengths(key, part):
    key = jax.random.fold_in(key, 41)
    child_keys = jax.random.split(key, 2)
    random_len = jax.random.randint(child_keys[0], (BATCH_REQUESTS,), 1, CONTEXT)
    longest = jax.random.randint(child_keys[1], (), 0, BATCH_REQUESTS)
    return jnp.where(jnp.arange(BATCH_REQUESTS) == longest, CONTEXT - 1, random_len).astype(jnp.int32)


def block_levels(stream_key, shape, pieces, least, top_value):
    loudness = 1.0
    for dim, shards_of in pieces:
        steps = jax.random.uniform(jax.random.fold_in(jax.random.fold_in(stream_key, 6), dim), (shards_of,), jnp.float32, least / len(pieces), top_value / len(pieces))
        loudness = loudness * jnp.repeat(jnp.exp(steps), shape[dim] // shards_of).reshape((-1,) + (1,) * (len(shape) - 1 - dim))
    return loudness


def noise(key, dims, width, bound, cuts=(), held_as=jnp.bfloat16):
    level = block_levels(key, dims, cuts, -0.22, 0.18) if cuts else 1.0
    array = jax.random.normal(key, dims, jnp.float32) * width * level
    return jnp.minimum(jnp.maximum(array, -bound), bound).astype(held_as)


def setup_inputs(seed: int = 0) -> dict:
    splits = jax.random.split(jax.random.key(seed), 13)
    hidden_state = draw_hidden_state(jax.random.fold_in(splits[12], 71), 0)
    attn_gain = jnp.clip(1.0 + 0.18 * jax.random.normal(splits[1], (MODEL_WIDTH,), jnp.float32), 0.099609375, 1.8984375).astype(jnp.bfloat16)
    query_key_value_weight = noise(splits[2], (MODEL_WIDTH, KEY_VALUE_HEADS * (QUERY_HEADS // KEY_VALUE_HEADS + 2) * HEAD_SIZE), MODEL_WIDTH ** -0.5, 0.0625, ((0, 64), (1, 8)))
    key_page_cache = draw_key_page_cache(jax.random.fold_in(splits[12], 71), 0)
    value_page_cache = draw_value_page_cache(jax.random.fold_in(splits[12], 71), 0)
    page_table = draw_page_table(jax.random.fold_in(splits[12], 71), 0)
    lengths = draw_lengths(jax.random.fold_in(splits[12], 71), 0)
    out_weight = noise(splits[7], (QUERY_HEADS * HEAD_SIZE, MODEL_WIDTH), (QUERY_HEADS * HEAD_SIZE) ** -0.5, 0.0625, ((0, 8), (1, 64)))
    ffn_gain = jnp.clip(1.0 + 0.18 * jax.random.normal(splits[8], (MODEL_WIDTH,), jnp.float32), 0.099609375, 1.8984375).astype(jnp.bfloat16)
    gate_weight = noise(splits[9], (MODEL_WIDTH, FF), MODEL_WIDTH ** -0.5, 0.0625, ((0, 64), (1, 8)))
    up_weight = noise(splits[10], (MODEL_WIDTH, FF), MODEL_WIDTH ** -0.5, 0.0625, ((0, 64), (1, 8)))
    down_weight = noise(splits[11], (FF, MODEL_WIDTH), FF ** -0.5, 0.03125, ((0, 8), (1, 64)))
    return dict(hidden_state=hidden_state, attn_gain=attn_gain, query_key_value_weight=query_key_value_weight, key_page_cache=key_page_cache, value_page_cache=value_page_cache, page_table=page_table, lengths=lengths, out_weight=out_weight, ffn_gain=ffn_gain, gate_weight=gate_weight, up_weight=up_weight, down_weight=down_weight)


epsilon = 1e-05
rope_base = 500000.0
neg_fill = -1e+30
scale_factor = 8.0
low_factor = 1.0
high_factor = 4.0
native_window = 8192.0

def product(form, left, right):
    return jnp.einsum(form, left.astype(jnp.float32), right.astype(jnp.float32))

def rotate(vectors, position):
    half_width = vectors.shape[-1] // 2
    base_freq = rope_base ** (-jnp.arange(half_width, dtype=jnp.float32) * 2.0 / vectors.shape[-1])
    ratio = native_window * base_freq / (2.0 * math.pi)
    smooth = jnp.clip((ratio - low_factor) / (high_factor - low_factor), 0.0, 1.0)
    frequency = (1.0 - smooth) * base_freq / scale_factor + smooth * base_freq
    angles = position[..., None].astype(jnp.float32) * frequency
    cos_part = jnp.cos(angles)
    sine_part = jnp.sin(angles)
    earlier = vectors[..., :half_width]
    latter = vectors[..., half_width:]
    return jnp.concatenate([earlier * cos_part - latter * sine_part, latter * cos_part + earlier * sine_part], axis=-1)

def owner_partial(key_rows, value_rows, queries, new_key, new_value, page_table, lengths, new_owner, owner):
    slot_count, page_len = (key_rows.shape[0], key_rows.shape[1])
    requests, kv_heads, query_group, head_dim = queries.shape
    score_scale = 1.0 / math.sqrt(head_dim)
    slot_ids = owner * slot_count + jnp.arange(slot_count, dtype=jnp.int32)
    matches = page_table[None, :, :] == slot_ids[:, None, None]
    page_index = jnp.arange(page_table.shape[1], dtype=jnp.int32)
    slot_page = lax.optimization_barrier(jnp.sum(jnp.where(matches, page_index[None, None, :], 0), axis=(1, 2)))
    owned_by = jnp.any(matches, axis=2)
    slot_len = lax.optimization_barrier(jnp.sum(jnp.where(owned_by, lengths[None, :], 0), axis=1))
    positions = slot_page[:, None] * page_len + jnp.arange(page_len, dtype=jnp.int32)[None, :]
    live_key = positions < slot_len[:, None]
    slot_query = lax.optimization_barrier(jnp.sum(jnp.where(owned_by[:, :, None, None, None], queries[None], jnp.zeros((), queries.dtype)), axis=1))
    key_heads = key_rows.reshape(slot_count, page_len, kv_heads, head_dim)
    value_heads = value_rows.reshape(slot_count, page_len, kv_heads, head_dim)
    scores = product('shgd,sthd->shgt', slot_query, key_heads) * score_scale
    masked = jnp.where(live_key[:, None, None, :], scores, neg_fill)
    slot_peak = lax.optimization_barrier(jnp.max(masked, axis=3))
    req_peak = lax.optimization_barrier(jnp.max(jnp.where(owned_by[:, :, None, None], slot_peak[:, None], neg_fill), axis=0))
    is_mine = new_owner == owner
    new_score = lax.optimization_barrier(jnp.sum(queries.astype(jnp.float32) * new_key.astype(jnp.float32)[:, :, None, :], axis=3)) * score_scale
    peak_score = jnp.maximum(req_peak, jnp.where(is_mine[:, None, None], new_score, neg_fill))
    slot_best = lax.optimization_barrier(jnp.sum(jnp.where(owned_by[:, :, None, None], peak_score[None], 0.0), axis=1))
    weights = jnp.where(live_key[:, None, None, :], jnp.exp(masked - slot_best[..., None]), 0.0)
    slot_totals = lax.optimization_barrier(jnp.sum(weights, axis=3))
    slot_accum = product('shgt,sthd->shgd', weights.astype(jnp.bfloat16), value_heads)
    totals = lax.optimization_barrier(jnp.sum(jnp.where(owned_by[:, :, None, None], slot_totals[:, None], 0.0), axis=0))
    accum = lax.optimization_barrier(jnp.sum(jnp.where(owned_by[:, :, None, None, None], slot_accum[:, None], 0.0), axis=0))
    new_weight = jnp.where(is_mine[:, None, None], jnp.exp(new_score - peak_score), 0.0)
    totals = totals + new_weight
    accum = accum + new_weight.astype(jnp.bfloat16).astype(jnp.float32)[..., None] * new_value.astype(jnp.float32)[:, :, None, :]
    return (peak_score, totals, accum)

def reference(hidden_state, attn_gain, query_key_value_weight, key_page_cache, value_page_cache, page_table, lengths, out_weight, ffn_gain, gate_weight, up_weight, down_weight):
    query_group = QUERY_HEADS // KEY_VALUE_HEADS
    stream = hidden_state.astype(jnp.float32)
    scaled = (stream * attn_gain.astype(jnp.float32)).astype(jnp.bfloat16)
    inv_rms = lax.rsqrt(lax.optimization_barrier(jnp.sum(stream * stream, axis=1)) / MODEL_WIDTH + epsilon)
    combined_sum = jnp.dot(scaled, query_key_value_weight, preferred_element_type=jnp.float32) * inv_rms[:, None]
    combined_sum = combined_sum.reshape(BATCH_REQUESTS, KEY_VALUE_HEADS, query_group + 2, HEAD_SIZE)
    queries = rotate(combined_sum[:, :, :query_group], lengths[:, None, None]).astype(jnp.bfloat16)
    new_key = rotate(combined_sum[:, :, query_group], lengths[:, None]).astype(jnp.bfloat16)
    new_value = combined_sum[:, :, query_group + 1].astype(jnp.bfloat16)
    new_page = jnp.take_along_axis(page_table, (lengths // PAGE_TOKENS).astype(jnp.int32)[:, None], axis=1)[:, 0]
    new_owner = (new_page // DEVICE_PAGES).astype(jnp.int32)
    cache_key_list = key_page_cache.reshape(N_SEQ, DEVICE_PAGES, PAGE_TOKENS, KEY_VALUE_HEADS * HEAD_SIZE)
    cache_value_list = value_page_cache.reshape(N_SEQ, DEVICE_PAGES, PAGE_TOKENS, KEY_VALUE_HEADS * HEAD_SIZE)

    def one_owner(packed):
        owner, key_rows, value_rows = packed
        return owner_partial(key_rows, value_rows, queries, new_key, new_value, page_table, lengths, new_owner, owner)
    peaks, totals, accums = lax.map(one_owner, (jnp.arange(N_SEQ, dtype=jnp.int32), cache_key_list, cache_value_list))
    overall = lax.optimization_barrier(jnp.max(peaks, axis=0))
    factors = jnp.exp(peaks - overall[None])
    denominator = lax.optimization_barrier(jnp.sum(totals * factors, axis=0))
    numerator = lax.optimization_barrier(jnp.sum(accums * factors[..., None], axis=0))
    attention = (numerator / denominator[..., None]).astype(jnp.bfloat16).reshape(BATCH_REQUESTS, QUERY_HEADS * HEAD_SIZE)
    projected = jnp.dot(attention, out_weight, preferred_element_type=jnp.float32)
    attended = (stream + projected).astype(jnp.bfloat16)
    after = attended.astype(jnp.float32)
    ffn_scaled = (after * ffn_gain.astype(jnp.float32)).astype(jnp.bfloat16)
    inv_norm = lax.rsqrt(lax.optimization_barrier(jnp.sum(after * after, axis=1)) / MODEL_WIDTH + epsilon)
    gate = jnp.dot(ffn_scaled, gate_weight, preferred_element_type=jnp.float32) * inv_norm[:, None]
    up_proj = jnp.dot(ffn_scaled, up_weight, preferred_element_type=jnp.float32) * inv_norm[:, None]
    hidden = (jax.nn.silu(gate) * up_proj).astype(jnp.bfloat16)
    mixed = (after + jnp.dot(hidden, down_weight, preferred_element_type=jnp.float32)).astype(jnp.bfloat16)
    return (attended, mixed)
```

```python
import functools
import math

import jax
import jax.numpy as jnp
import numpy as np
from jax import lax
from jax.experimental import pallas as pl
from jax.experimental.pallas import tpu as pltpu
from jax.sharding import PartitionSpec as P

MODEL_WIDTH = 8192
QUERY_HEADS = 64
KEY_VALUE_HEADS = 8
HEAD_SIZE = 128
PAGE_TOKENS = 128
REQUESTS = 4
GROUP = QUERY_HEADS // KEY_VALUE_HEADS
ROWS = GROUP * REQUESTS
SLOTS = 16
LANES = 128
SIDE = 8
HEADS = 8
TILES = 28
HALF_TILES = 14

epsilon = 1e-05
neg_fill = -1e30
MESH = pl.DeviceIdType.MESH
f32 = jnp.float32
bf16 = jnp.bfloat16

RING_ORDER = (4, 3, 5, 2, 6, 1, 7)


def rope_frequencies():
    index = np.arange(HEAD_SIZE // 2, dtype=np.float64)
    base = 500000.0 ** (-2.0 * index / HEAD_SIZE)
    ratio = 8192.0 * base / (2.0 * math.pi)
    smooth = np.clip((ratio - 1.0) / 3.0, 0.0, 1.0)
    frequency = (1.0 - smooth) * base / 8.0 + smooth * base
    return np.concatenate([frequency, frequency]).astype(np.float32)[None, :]


def layer(
    len_ref,
    freq_ref,
    hidden_any,
    gain_any,
    wqkv_any,
    keys_any,
    values_any,
    table_any,
    wout_any,
    fgain_any,
    wgate_any,
    wup_any,
    wdown_any,
    attended_ref,
    mixed_ref,
    hidden,
    gain,
    wqkv,
    keys,
    values,
    table,
    wout,
    fgain,
    wgate,
    wup,
    wdown,
    load_sem,
    qkv_out1,
    qkv_in1,
    qkv_out2,
    qkv_in2,
    live_buf,
    part_out1,
    part_in1,
    part_out2,
    part_in2,
    proj_buf,
    gate_rows,
    up_rows,
    chunk_out,
    chunk_in,
    piece_out,
    piece_in,
    act_buf,
    act_rows,
    down_buf,
    send_sem,
    recv_sem,
):
    seq = lax.axis_index("seq")
    head = lax.axis_index("head")
    core = lax.rem(head, 2)
    row_y = seq // SIDE
    row_z = lax.rem(seq, SIDE)
    first = row_y + core * (row_z - row_y)
    second = row_z + core * (row_y - row_z)

    def seq_of(one, two):
        return one * (SIDE - (SIDE - 1) * core) + two * (1 + (SIDE - 1) * core)

    def first_peer(d):
        other = lax.rem(first + d, SIDE)
        return other, (seq_of(other, second), head)

    def second_peer(d):
        other = lax.rem(second + d, SIDE)
        return other, (seq_of(first, other), head)

    def head_peer(d):
        other = lax.rem(head + d, HEADS)
        return other, (seq, other)

    barrier = pltpu.get_barrier_semaphore()
    for d in range(1, 8):
        for peer in (first_peer, second_peer, head_peer):
            pl.semaphore_signal(barrier, inc=1, device_id=peer(d)[1], device_id_type=MESH)

    loads = {}
    for i, (name, src, dst) in enumerate(
        (
            ("hidden", hidden_any, hidden),
            ("gain", gain_any, gain),
            ("wqkv", wqkv_any, wqkv),
            ("table", table_any, table),
            ("keys", keys_any, keys),
            ("values", values_any, values),
            ("wout", wout_any, wout),
            ("fgain", fgain_any, fgain),
            ("wgate", wgate_any, wgate),
            ("wup", wup_any, wup),
            ("wdown", wdown_any, wdown),
        )
    ):
        loads[name] = pltpu.make_async_copy(src, dst, load_sem.at[i])
        loads[name].start()

    started = []

    def exchange(step, peer, src_of, dst_of):
        copies = []
        for d in RING_ORDER:
            other, device = peer(d)
            copy = pltpu.make_async_remote_copy(
                src_ref=src_of(other),
                dst_ref=dst_of(d),
                send_sem=send_sem.at[step, d - 1],
                recv_sem=recv_sem.at[step, d - 1],
                device_id=device,
                device_id_type=MESH,
            )
            copy.start()
            copies.append(copy)
        started.extend(copies)
        return copies

    def arrive(copies):
        for copy in copies:
            copy.wait_recv()

    loads["hidden"].wait()
    loads["gain"].wait()
    stream = hidden[...].astype(f32)
    scaled = (stream * gain[...].astype(f32)).astype(bf16)
    square = jnp.broadcast_to(jnp.sum(stream * stream, axis=1, keepdims=True), (REQUESTS, LANES))
    loads["wqkv"].wait()
    part = jnp.dot(scaled, wqkv[...], preferred_element_type=f32)
    part_rows = jnp.concatenate(
        [part[:, t * LANES : (t + 1) * LANES] for t in range(GROUP + 2)]
        + [square, jnp.zeros((REQUESTS, LANES), f32)],
        axis=0,
    )
    qkv_out1[...] = part_rows.astype(bf16)

    pl.semaphore_wait(barrier, 21)
    copies = exchange(0, first_peer, lambda o: qkv_out1, lambda d: qkv_in1.at[d - 1])

    sub = lax.broadcasted_iota(jnp.int32, (8, 1), 0)
    request = lax.rem(sub, REQUESTS)
    length = jnp.zeros((8, 1), jnp.int32)
    for b in range(REQUESTS):
        length = jnp.where(request == b, len_ref[b], length)
    loads["table"].wait()
    pages = table[...]
    pages = jnp.concatenate([pages, pages], axis=0)
    page_count = pages.shape[1]
    page_index = lax.broadcasted_iota(jnp.int32, (8, page_count), 1)
    lane = lax.broadcasted_iota(jnp.int32, (8, LANES), 1)
    for j in range(SLOTS):
        hit = jnp.sum(
            jnp.where(pages == seq * SLOTS + j, (page_index + 1).astype(f32), 0.0), axis=1, keepdims=True
        ).astype(jnp.int32)
        limit = jnp.where(hit > 0, length - (hit - 1) * PAGE_TOKENS, 0)
        live_buf[:, j * LANES : (j + 1) * LANES] = jnp.where(lane < limit, 1.0, 0.0)
    mine_page = (page_index == length // PAGE_TOKENS) & (pages >= seq * SLOTS) & (pages < (seq + 1) * SLOTS)
    mine = jnp.sum(jnp.where(mine_page, 1.0, 0.0), axis=1, keepdims=True) > 0.5
    angle = length.astype(f32) * freq_ref[...]
    cos_part = jnp.cos(angle)
    sine_part = jnp.where(lane < HEAD_SIZE // 2, -jnp.sin(angle), jnp.sin(angle))

    arrive(copies)
    total = part_rows
    for d in range(7):
        total = total + qkv_in1[d].astype(f32)
    qkv_out2[...] = total.astype(bf16)
    copies = exchange(1, second_peer, lambda o: qkv_out2, lambda d: qkv_in2.at[d - 1])
    loads["keys"].wait()
    loads["values"].wait()
    arrive(copies)
    for d in range(7):
        total = total + qkv_in2[d].astype(f32)

    square_all = total[40:44]
    square_all = jnp.concatenate([square_all, square_all], axis=0)
    inv_rms = lax.rsqrt(square_all / MODEL_WIDTH + epsilon)
    joined = total[0:40].reshape(5, 8, LANES) * inv_rms
    swapped = pltpu.roll(joined.reshape(40, LANES), HEAD_SIZE // 2, 1).reshape(5, 8, LANES)
    turned = joined * cos_part + swapped * sine_part
    queries = turned[0:4].reshape(ROWS, LANES).astype(bf16)
    new_key = turned[4][0:4].astype(bf16).astype(f32)
    new_key = jnp.concatenate([new_key, new_key], axis=0)
    new_value = joined[4][4:8].astype(bf16).astype(f32)
    new_value = jnp.concatenate([new_value, new_value], axis=0)

    scale = 1.0 / math.sqrt(HEAD_SIZE)
    tokens = SLOTS * PAGE_TOKENS
    scores = lax.dot_general(
        queries,
        keys[...].reshape(tokens, HEAD_SIZE),
        (((1,), (1,)), ((), ())),
        preferred_element_type=f32,
    )
    live = live_buf[...] > 0.5
    masked = jnp.where(live, scores.reshape(4, 8, tokens) * scale, neg_fill)
    new_score = (
        jnp.sum(queries.astype(f32).reshape(4, 8, LANES) * new_key, axis=2, keepdims=True) * scale
    )
    peak = jnp.maximum(
        jnp.max(masked, axis=2, keepdims=True), jnp.where(mine, new_score, neg_fill)
    )
    weight = jnp.where(live, jnp.exp(masked - peak), 0.0)
    new_weight = jnp.where(mine, jnp.exp(new_score - peak), 0.0)
    denom = jnp.sum(weight, axis=2, keepdims=True) + new_weight
    accum = jnp.dot(
        weight.reshape(ROWS, tokens).astype(bf16),
        values[...].reshape(tokens, HEAD_SIZE),
        preferred_element_type=f32,
    ).reshape(4, 8, LANES)
    accum = accum + new_weight.astype(bf16).astype(f32) * new_value
    some = denom > 0.0
    safe = jnp.where(some, denom, 1.0)
    mean = (accum / safe).reshape(ROWS, LANES)
    lse = jnp.where(some, peak + jnp.log(safe), neg_fill).reshape(ROWS, 1)

    diagonal = lax.broadcasted_iota(jnp.int32, (ROWS, LANES), 0) == lax.broadcasted_iota(
        jnp.int32, (ROWS, LANES), 1
    )
    lse_row = jnp.sum(jnp.where(diagonal, lse, 0.0), axis=0, keepdims=True)
    stat_row = lax.broadcasted_iota(jnp.int32, (16, LANES), 0)

    def packed(mean, lse_row):
        high = lse_row.astype(bf16).astype(f32)
        rest = lse_row - high
        middle = rest.astype(bf16).astype(f32)
        low = rest - middle
        stats = jnp.where(
            stat_row == 0, high, jnp.where(stat_row == 1, middle, jnp.where(stat_row == 2, low, 0.0))
        )
        return jnp.concatenate([mean, stats], axis=0).astype(bf16)

    def merged(mean, lse_row, arrived):
        means, lses = [mean], [lse_row]
        for d in range(7):
            block = arrived[d].astype(f32)
            means.append(block[0:ROWS])
            lses.append(block[ROWS : ROWS + 1] + block[ROWS + 1 : ROWS + 2] + block[ROWS + 2 : ROWS + 3])
        best = functools.reduce(jnp.maximum, lses)
        factors = [jnp.exp(part - best) for part in lses]
        whole = functools.reduce(jnp.add, factors)
        result = None
        for factor, part in zip(factors, means):
            column = jnp.sum(jnp.where(diagonal, factor / whole, 0.0), axis=1, keepdims=True)
            result = column * part if result is None else result + column * part
        return result, best + jnp.log(whole)

    part_out1[...] = packed(mean, lse_row)
    copies = exchange(2, first_peer, lambda o: part_out1, lambda d: part_in1.at[d - 1])
    loads["wout"].wait()
    loads["fgain"].wait()
    arrive(copies)
    mean, lse_row = merged(mean, lse_row, part_in1)
    part_out2[...] = packed(mean, lse_row)
    copies = exchange(3, second_peer, lambda o: part_out2, lambda d: part_in2.at[d - 1])
    loads["wgate"].wait()
    loads["wup"].wait()
    loads["wdown"].wait()
    arrive(copies)
    mean, _ = merged(mean, lse_row, part_in2)

    attention = jnp.concatenate(
        [mean[g * REQUESTS : (g + 1) * REQUESTS] for g in range(GROUP)], axis=1
    ).astype(bf16)
    proj_buf[head] = jnp.dot(attention, wout[...], preferred_element_type=f32)
    copies = exchange(4, head_peer, lambda o: proj_buf.at[head], lambda d: proj_buf.at[head])
    arrive(copies)
    projected = proj_buf[0]
    for h in range(1, HEADS):
        projected = projected + proj_buf[h]
    attended = (stream + projected).astype(bf16)
    attended_ref[...] = attended
    after = attended.astype(f32)
    ffn = (after * fgain[...].astype(f32)).astype(bf16).astype(f32)
    ffn = jnp.concatenate([ffn, ffn], axis=0).astype(bf16)
    square = jnp.sum(after * after, axis=1, keepdims=True)
    gate_part = jnp.dot(ffn, wgate[...], preferred_element_type=f32)
    up_part = jnp.dot(ffn, wup[...], preferred_element_type=f32)
    for t in range(TILES):
        gate_rows[t * 8 : (t + 1) * 8, :] = gate_part[:, t * LANES : (t + 1) * LANES]
        up_rows[t * 8 : (t + 1) * 8, :] = up_part[:, t * LANES : (t + 1) * LANES]
    blank = jnp.zeros((2, LANES), f32)
    blank_row = lax.broadcasted_iota(jnp.int32, (2, LANES), 0)
    for c in range(SIDE):
        b, half = c // 2, c % 2
        span = pl.ds(half * HALF_TILES * 8 + b, HALF_TILES, stride=8)
        tail = jnp.where(blank_row == 0, square[b : b + 1], 0.0)
        chunk_out[c] = jnp.concatenate([gate_rows[span, :], tail, up_rows[span, :], blank], axis=0).astype(bf16)
    copies = exchange(5, first_peer, lambda o: chunk_out.at[o], lambda d: chunk_in.at[d - 1])
    own = chunk_out[first].astype(f32)
    arrive(copies)
    for d in range(7):
        own = own + chunk_in[d].astype(f32)
    piece_out[...] = own.astype(bf16)
    copies = exchange(6, second_peer, lambda o: piece_out, lambda d: piece_in.at[d - 1])
    arrive(copies)
    for d in range(7):
        own = own + piece_in[d].astype(f32)
    inv_norm = lax.rsqrt(own[HALF_TILES : HALF_TILES + 1] / MODEL_WIDTH + epsilon)
    gate = own[0:16] * inv_norm
    act = gate / (1.0 + jnp.exp(-gate)) * (own[16:32] * inv_norm)
    act_buf[first] = act.astype(bf16)
    copies = exchange(7, first_peer, lambda o: act_buf.at[first], lambda d: act_buf.at[first])
    arrive(copies)
    act_rows[...] = act_buf[...].reshape(SIDE * 16, LANES).astype(f32)
    units = jnp.concatenate(
        [
            act_rows[pl.ds((t // HALF_TILES) * 16 + t % HALF_TILES, REQUESTS, stride=32), :]
            for t in range(TILES)
        ],
        axis=1,
    ).astype(bf16)
    down_buf[head] = jnp.dot(units, wdown[...], preferred_element_type=f32)
    copies = exchange(8, head_peer, lambda o: down_buf.at[head], lambda d: down_buf.at[head])
    arrive(copies)
    down = down_buf[0]
    for h in range(1, HEADS):
        down = down + down_buf[h]
    mixed_ref[...] = (after + down).astype(bf16)

    for copy in started:
        copy.wait_send()


def on_device(
    hidden_state,
    attn_gain,
    query_key_value_weight,
    key_page_cache,
    value_page_cache,
    page_table,
    lengths,
    out_weight,
    ffn_gain,
    gate_weight,
    up_weight,
    down_weight,
):
    requests, width = hidden_state.shape
    arrays = (
        hidden_state,
        attn_gain.reshape(1, width),
        query_key_value_weight,
        key_page_cache,
        value_page_cache,
        page_table,
        out_weight,
        ffn_gain.reshape(1, width),
        gate_weight,
        up_weight,
        down_weight,
    )
    any_spec = pl.BlockSpec(memory_space=pl.ANY)
    vmem_spec = pl.BlockSpec(memory_space=pltpu.VMEM)
    out = jax.ShapeDtypeStruct((requests, width), bf16)
    rows = 48
    return pl.pallas_call(
        layer,
        out_shape=(out, out),
        in_specs=[pl.BlockSpec(memory_space=pltpu.SMEM), vmem_spec] + [any_spec] * len(arrays),
        out_specs=(vmem_spec, vmem_spec),
        scratch_shapes=[pltpu.VMEM(a.shape, a.dtype) for a in arrays]
        + [
            pltpu.SemaphoreType.DMA((len(arrays),)),
            pltpu.VMEM((rows, LANES), bf16),
            pltpu.VMEM((7, rows, LANES), bf16),
            pltpu.VMEM((rows, LANES), bf16),
            pltpu.VMEM((7, rows, LANES), bf16),
            pltpu.VMEM((8, SLOTS * PAGE_TOKENS), f32),
            pltpu.VMEM((rows, LANES), bf16),
            pltpu.VMEM((7, rows, LANES), bf16),
            pltpu.VMEM((rows, LANES), bf16),
            pltpu.VMEM((7, rows, LANES), bf16),
            pltpu.VMEM((HEADS, REQUESTS, LANES), f32),
            pltpu.VMEM((TILES * 8, LANES), f32),
            pltpu.VMEM((TILES * 8, LANES), f32),
            pltpu.VMEM((SIDE, 32, LANES), bf16),
            pltpu.VMEM((7, 32, LANES), bf16),
            pltpu.VMEM((32, LANES), bf16),
            pltpu.VMEM((7, 32, LANES), bf16),
            pltpu.VMEM((SIDE, 16, LANES), bf16),
            pltpu.VMEM((SIDE * 16, LANES), f32),
            pltpu.VMEM((HEADS, REQUESTS, LANES), f32),
            pltpu.SemaphoreType.DMA((9, 7)),
            pltpu.SemaphoreType.DMA((9, 7)),
        ],
        compiler_params=pltpu.CompilerParams(
            collective_id=0, has_side_effects=True, vmem_limit_bytes=48 * 1024 * 1024
        ),
    )(lengths, jnp.asarray(rope_frequencies()), *arrays)


def solution(mesh):
    in_specs = (
        P(None, "seq"),
        P("seq"),
        P("seq", "head"),
        P("seq", None, "head"),
        P("seq", None, "head"),
        P(),
        P(),
        P("head", "seq"),
        P("seq"),
        P("seq", "head"),
        P("seq", "head"),
        P("head", "seq"),
    )
    out_specs = (P(None, "seq"), P(None, "seq"))
    return jax.shard_map(
        on_device, mesh=mesh, in_specs=in_specs, out_specs=out_specs, check_vma=False
    )
```

```python
import functools
import math

import jax
import jax.numpy as jnp
import numpy as np
from jax import lax
from jax.experimental import pallas as pl
from jax.experimental.pallas import tpu as pltpu
from jax.sharding import PartitionSpec as P

MODEL_WIDTH = 8192
QUERY_HEADS = 64
KEY_VALUE_HEADS = 8
HEAD_SIZE = 128
PAGE_TOKENS = 128
REQUESTS = 4
GROUP = QUERY_HEADS // KEY_VALUE_HEADS
ROWS = GROUP * REQUESTS
SLOTS = 16
LANES = 128
SIDE = 8
HEADS = 8
TILES = 28
HALF_TILES = 14

epsilon = 1e-05
neg_fill = -1e30
MESH = pl.DeviceIdType.MESH
f32 = jnp.float32
bf16 = jnp.bfloat16

RING_ORDER = (4, 3, 5, 2, 6, 1, 7)


def rope_frequencies():
    index = np.arange(HEAD_SIZE // 2, dtype=np.float64)
    base = 500000.0 ** (-2.0 * index / HEAD_SIZE)
    ratio = 8192.0 * base / (2.0 * math.pi)
    smooth = np.clip((ratio - 1.0) / 3.0, 0.0, 1.0)
    frequency = (1.0 - smooth) * base / 8.0 + smooth * base
    return np.concatenate([frequency, frequency]).astype(np.float32)[None, :]


def layer(
    hidden_any,
    gain_any,
    wqkv_any,
    keys_any,
    values_any,
    table_any,
    wout_any,
    fgain_any,
    wgate_any,
    wup_any,
    wdown_any,
    len_any,
    freq_any,
    both_ref,
    hidden,
    gain,
    wqkv,
    keys,
    values,
    table,
    wout,
    fgain,
    wgate,
    wup,
    wdown,
    len_ref,
    freq_ref,
    load_sem,
    qkv_out1,
    qkv_in1,
    qkv_out2,
    qkv_in2,
    live_buf,
    part_out1,
    part_in1,
    part_out2,
    part_in2,
    proj_buf,
    gate_rows,
    up_rows,
    chunk_out,
    chunk_in,
    piece_out,
    piece_in,
    act_buf,
    act_rows,
    down_buf,
    send_sem,
    recv_sem,
):
    seq = lax.axis_index("seq")
    head = lax.axis_index("head")
    core = lax.rem(head, 2)
    row_y = seq // SIDE
    row_z = lax.rem(seq, SIDE)
    first = row_y + core * (row_z - row_y)
    second = row_z + core * (row_y - row_z)

    def seq_of(one, two):
        return one * (SIDE - (SIDE - 1) * core) + two * (1 + (SIDE - 1) * core)

    def first_peer(d):
        other = lax.rem(first + d, SIDE)
        return other, (seq_of(other, second), head)

    def second_peer(d):
        other = lax.rem(second + d, SIDE)
        return other, (seq_of(first, other), head)

    def head_peer(d):
        other = lax.rem(head + d, HEADS)
        return other, (seq, other)

    loads = {}

    def load(index, name, src, dst):
        loads[name] = pltpu.make_async_copy(src, dst, load_sem.at[index])
        loads[name].start()

    load(0, "hidden", hidden_any, hidden)
    load(1, "gain", gain_any, gain)
    load(2, "wqkv", wqkv_any, wqkv)

    barrier = pltpu.get_barrier_semaphore()
    for d in RING_ORDER:
        for peer in (first_peer, second_peer, head_peer):
            pl.semaphore_signal(barrier, inc=1, device_id=peer(d)[1], device_id_type=MESH)

    load(3, "table", table_any, table)
    load(4, "lengths", len_any, len_ref)
    load(5, "freq", freq_any, freq_ref)
    load(6, "keys", keys_any, keys)
    load(7, "values", values_any, values)
    load(8, "wout", wout_any, wout)
    load(9, "fgain", fgain_any, fgain)
    load(10, "wgate", wgate_any, wgate)
    load(11, "wup", wup_any, wup)
    load(12, "wdown", wdown_any, wdown)

    def exchange(step, peer, src_of, dst_of):
        for d in RING_ORDER:
            other, device = peer(d)
            pltpu.make_async_remote_copy(
                src_ref=src_of(other),
                dst_ref=dst_of(d),
                send_sem=send_sem.at[step],
                recv_sem=recv_sem.at[step],
                device_id=device,
                device_id_type=MESH,
            ).start()

    def arrive(step, blocks):
        seven = blocks.at[pl.ds(0, 7)]
        pltpu.make_async_copy(seven, seven, recv_sem.at[step]).wait()

    def departed(step, blocks):
        seven = blocks.at[pl.ds(0, 7)]
        pltpu.make_async_copy(seven, seven, send_sem.at[step]).wait()

    loads["hidden"].wait()
    loads["gain"].wait()
    stream = hidden[...].astype(f32)
    scaled = (stream * gain[...].astype(f32)).astype(bf16)
    square = jnp.broadcast_to(jnp.sum(stream * stream, axis=1, keepdims=True), (REQUESTS, LANES))
    loads["wqkv"].wait()
    part = jnp.dot(scaled, wqkv[...], preferred_element_type=f32)
    part_rows = jnp.concatenate(
        [part[:, t * LANES : (t + 1) * LANES] for t in range(GROUP + 2)]
        + [square, jnp.zeros((REQUESTS, LANES), f32)],
        axis=0,
    )
    qkv_out1[...] = part_rows.astype(bf16)

    pl.semaphore_wait(barrier, 21)
    exchange(0, first_peer, lambda o: qkv_out1, lambda d: qkv_in1.at[d - 1])

    sub = lax.broadcasted_iota(jnp.int32, (8, 1), 0)
    request = lax.rem(sub, REQUESTS)
    length = jnp.zeros((8, 1), jnp.int32)
    loads["lengths"].wait()
    for b in range(REQUESTS):
        length = jnp.where(request == b, len_ref[b], length)
    loads["table"].wait()
    pages = table[...]
    pages = jnp.concatenate([pages, pages], axis=0)
    page_count = pages.shape[1]
    page_index = lax.broadcasted_iota(jnp.int32, (8, page_count), 1)
    lane = lax.broadcasted_iota(jnp.int32, (8, LANES), 1)
    for j in range(SLOTS):
        hit = jnp.sum(
            jnp.where(pages == seq * SLOTS + j, (page_index + 1).astype(f32), 0.0), axis=1, keepdims=True
        ).astype(jnp.int32)
        limit = jnp.where(hit > 0, length - (hit - 1) * PAGE_TOKENS, 0)
        live_buf[:, j * LANES : (j + 1) * LANES] = jnp.where(lane < limit, 1.0, 0.0)
    mine_page = (page_index == length // PAGE_TOKENS) & (pages >= seq * SLOTS) & (pages < (seq + 1) * SLOTS)
    mine = jnp.sum(jnp.where(mine_page, 1.0, 0.0), axis=1, keepdims=True) > 0.5

    arrive(0, qkv_in1)
    total = part_rows
    for d in range(7):
        total = total + qkv_in1[d].astype(f32)
    qkv_out2[...] = total.astype(bf16)
    exchange(1, second_peer, lambda o: qkv_out2, lambda d: qkv_in2.at[d - 1])
    loads["freq"].wait()
    angle = length.astype(f32) * freq_ref[...]
    cos_part = jnp.cos(angle)
    sine_part = jnp.sin(angle)
    sine_part = jnp.where(lane < HEAD_SIZE // 2, -sine_part, sine_part)
    loads["keys"].wait()
    loads["values"].wait()
    arrive(1, qkv_in2)
    for d in range(7):
        total = total + qkv_in2[d].astype(f32)

    square_all = total[40:44]
    square_all = jnp.concatenate([square_all, square_all], axis=0)
    inv_rms = lax.rsqrt(square_all / MODEL_WIDTH + epsilon)
    joined = total[0:40].reshape(5, 8, LANES) * inv_rms
    swapped = pltpu.roll(joined.reshape(40, LANES), HEAD_SIZE // 2, 1).reshape(5, 8, LANES)
    turned = joined * cos_part + swapped * sine_part
    queries = turned[0:4].reshape(ROWS, LANES).astype(bf16)
    new_key = turned[4][0:4].astype(bf16).astype(f32)
    new_key = jnp.concatenate([new_key, new_key], axis=0)
    new_value = joined[4][4:8].astype(bf16).astype(f32)
    new_value = jnp.concatenate([new_value, new_value], axis=0)

    scale = 1.0 / math.sqrt(HEAD_SIZE)
    tokens = SLOTS * PAGE_TOKENS
    scores = lax.dot_general(
        queries,
        keys[...].reshape(tokens, HEAD_SIZE),
        (((1,), (1,)), ((), ())),
        preferred_element_type=f32,
    )
    live = live_buf[...] > 0.5
    masked = jnp.where(live, scores.reshape(4, 8, tokens) * scale, neg_fill)
    new_score = (
        jnp.sum(queries.astype(f32).reshape(4, 8, LANES) * new_key, axis=2, keepdims=True) * scale
    )
    peak = jnp.maximum(
        jnp.max(masked, axis=2, keepdims=True), jnp.where(mine, new_score, neg_fill)
    )
    weight = jnp.where(live, jnp.exp(masked - peak), 0.0)
    new_weight = jnp.where(mine, jnp.exp(new_score - peak), 0.0)
    denom = jnp.sum(weight, axis=2, keepdims=True) + new_weight
    accum = jnp.dot(
        weight.reshape(ROWS, tokens).astype(bf16),
        values[...].reshape(tokens, HEAD_SIZE),
        preferred_element_type=f32,
    ).reshape(4, 8, LANES)
    accum = accum + new_weight.astype(bf16).astype(f32) * new_value
    some = denom > 0.0
    safe = jnp.where(some, denom, 1.0)
    mean = (accum / safe).reshape(ROWS, LANES)
    lse = jnp.where(some, peak + jnp.log(safe), neg_fill).reshape(ROWS, 1)

    diagonal = lax.broadcasted_iota(jnp.int32, (ROWS, LANES), 0) == lax.broadcasted_iota(
        jnp.int32, (ROWS, LANES), 1
    )
    lse_row = jnp.sum(jnp.where(diagonal, lse, 0.0), axis=0, keepdims=True)
    stat_row = lax.broadcasted_iota(jnp.int32, (16, LANES), 0)

    def packed(mean, lse_row):
        high = lse_row.astype(bf16).astype(f32)
        rest = lse_row - high
        middle = rest.astype(bf16).astype(f32)
        low = rest - middle
        stats = jnp.where(
            stat_row == 0, high, jnp.where(stat_row == 1, middle, jnp.where(stat_row == 2, low, 0.0))
        )
        return jnp.concatenate([mean, stats], axis=0).astype(bf16)

    def merged(mean, lse_row, arrived):
        means, lses = [mean], [lse_row]
        for d in range(7):
            block = arrived[d].astype(f32)
            means.append(block[0:ROWS])
            lses.append(block[ROWS : ROWS + 1] + block[ROWS + 1 : ROWS + 2] + block[ROWS + 2 : ROWS + 3])
        best = functools.reduce(jnp.maximum, lses)
        factors = [jnp.exp(part - best) for part in lses]
        whole = functools.reduce(jnp.add, factors)
        result = None
        for factor, part in zip(factors, means):
            column = jnp.sum(jnp.where(diagonal, factor / whole, 0.0), axis=1, keepdims=True)
            result = column * part if result is None else result + column * part
        return result, best + jnp.log(whole)

    part_out1[...] = packed(mean, lse_row)
    exchange(2, first_peer, lambda o: part_out1, lambda d: part_in1.at[d - 1])
    loads["wout"].wait()
    loads["fgain"].wait()
    arrive(2, part_in1)
    mean, lse_row = merged(mean, lse_row, part_in1)
    part_out2[...] = packed(mean, lse_row)
    exchange(3, second_peer, lambda o: part_out2, lambda d: part_in2.at[d - 1])
    loads["wgate"].wait()
    loads["wup"].wait()
    loads["wdown"].wait()
    arrive(3, part_in2)
    mean, _ = merged(mean, lse_row, part_in2)

    attention = jnp.concatenate(
        [mean[g * REQUESTS : (g + 1) * REQUESTS] for g in range(GROUP)], axis=1
    ).astype(bf16)
    proj_buf[head] = jnp.dot(attention, wout[...], preferred_element_type=f32)
    exchange(4, head_peer, lambda o: proj_buf.at[head], lambda d: proj_buf.at[head])
    arrive(4, proj_buf)
    projected = proj_buf[0]
    for h in range(1, HEADS):
        projected = projected + proj_buf[h]
    attended = (stream + projected).astype(bf16)
    after = attended.astype(f32)
    ffn = (after * fgain[...].astype(f32)).astype(bf16).astype(f32)
    ffn = jnp.concatenate([ffn, ffn], axis=0).astype(bf16)
    square = jnp.sum(after * after, axis=1, keepdims=True)
    gate_part = jnp.dot(ffn, wgate[...], preferred_element_type=f32)
    up_part = jnp.dot(ffn, wup[...], preferred_element_type=f32)
    for t in range(TILES):
        gate_rows[t * 8 : (t + 1) * 8, :] = gate_part[:, t * LANES : (t + 1) * LANES]
        up_rows[t * 8 : (t + 1) * 8, :] = up_part[:, t * LANES : (t + 1) * LANES]
    blank = jnp.zeros((2, LANES), f32)
    blank_row = lax.broadcasted_iota(jnp.int32, (2, LANES), 0)
    for c in range(SIDE):
        b, half = c // 2, c % 2
        span = pl.ds(half * HALF_TILES * 8 + b, HALF_TILES, stride=8)
        tail = jnp.where(blank_row == 0, square[b : b + 1], 0.0)
        chunk_out[c] = jnp.concatenate([gate_rows[span, :], tail, up_rows[span, :], blank], axis=0).astype(bf16)
    exchange(5, first_peer, lambda o: chunk_out.at[o], lambda d: chunk_in.at[d - 1])
    own = chunk_out[first].astype(f32)
    arrive(5, chunk_in)
    for d in range(7):
        own = own + chunk_in[d].astype(f32)
    piece_out[...] = own.astype(bf16)
    exchange(6, second_peer, lambda o: piece_out, lambda d: piece_in.at[d - 1])
    arrive(6, piece_in)
    for d in range(7):
        own = own + piece_in[d].astype(f32)
    inv_norm = lax.rsqrt(own[HALF_TILES : HALF_TILES + 1] / MODEL_WIDTH + epsilon)
    gate = own[0:16] * inv_norm
    act = gate / (1.0 + jnp.exp(-gate)) * (own[16:32] * inv_norm)
    act_buf[first] = act.astype(bf16)
    exchange(7, first_peer, lambda o: act_buf.at[first], lambda d: act_buf.at[first])
    arrive(7, act_buf)
    act_rows[...] = act_buf[...].reshape(SIDE * 16, LANES).astype(f32)
    units = jnp.concatenate(
        [
            act_rows[pl.ds((t // HALF_TILES) * 16 + t % HALF_TILES, REQUESTS, stride=32), :]
            for t in range(TILES)
        ],
        axis=1,
    ).astype(bf16)
    down_buf[head] = jnp.dot(units, wdown[...], preferred_element_type=f32)
    exchange(8, head_peer, lambda o: down_buf.at[head], lambda d: down_buf.at[head])
    arrive(8, down_buf)
    down = down_buf[0]
    for h in range(1, HEADS):
        down = down + down_buf[h]
    both_ref[...] = jnp.concatenate([after, after + down], axis=0).astype(bf16)

    for step, blocks in enumerate(
        (qkv_in1, qkv_in2, part_in1, part_in2, proj_buf, chunk_in, piece_in, act_buf, down_buf)
    ):
        departed(step, blocks)


def on_device(
    hidden_state,
    attn_gain,
    query_key_value_weight,
    key_page_cache,
    value_page_cache,
    page_table,
    lengths,
    out_weight,
    ffn_gain,
    gate_weight,
    up_weight,
    down_weight,
):
    requests, width = hidden_state.shape
    arrays = (
        hidden_state,
        attn_gain.reshape(1, width),
        query_key_value_weight,
        key_page_cache,
        value_page_cache,
        page_table,
        out_weight,
        ffn_gain.reshape(1, width),
        gate_weight,
        up_weight,
        down_weight,
        lengths,
        jnp.asarray(rope_frequencies()),
    )
    hbm_spec = pl.BlockSpec(memory_space=pltpu.HBM)
    vmem_spec = pl.BlockSpec(memory_space=pltpu.VMEM)
    out = pltpu.VMEM((2 * requests, width), bf16)
    rows = 48
    both = pl.pallas_call(
        layer,
        out_shape=out,
        in_specs=[hbm_spec] * len(arrays),
        out_specs=vmem_spec,
        scratch_shapes=[
            pltpu.SMEM(a.shape, a.dtype) if a is lengths else pltpu.VMEM(a.shape, a.dtype) for a in arrays
        ]
        + [
            pltpu.SemaphoreType.DMA((len(arrays),)),
            pltpu.VMEM((rows, LANES), bf16),
            pltpu.VMEM((7, rows, LANES), bf16),
            pltpu.VMEM((rows, LANES), bf16),
            pltpu.VMEM((7, rows, LANES), bf16),
            pltpu.VMEM((8, SLOTS * PAGE_TOKENS), f32),
            pltpu.VMEM((rows, LANES), bf16),
            pltpu.VMEM((7, rows, LANES), bf16),
            pltpu.VMEM((rows, LANES), bf16),
            pltpu.VMEM((7, rows, LANES), bf16),
            pltpu.VMEM((HEADS, REQUESTS, LANES), f32),
            pltpu.VMEM((TILES * 8, LANES), f32),
            pltpu.VMEM((TILES * 8, LANES), f32),
            pltpu.VMEM((SIDE, 32, LANES), bf16),
            pltpu.VMEM((7, 32, LANES), bf16),
            pltpu.VMEM((32, LANES), bf16),
            pltpu.VMEM((7, 32, LANES), bf16),
            pltpu.VMEM((SIDE, 16, LANES), bf16),
            pltpu.VMEM((SIDE * 16, LANES), f32),
            pltpu.VMEM((HEADS, REQUESTS, LANES), f32),
            pltpu.SemaphoreType.DMA((9,)),
            pltpu.SemaphoreType.DMA((9,)),
        ],
        compiler_params=pltpu.CompilerParams(
            collective_id=0, has_side_effects=True, vmem_limit_bytes=48 * 1024 * 1024
        ),
    )(*[pltpu.with_memory_space_constraint(a, pltpu.HBM) for a in arrays])
    return both[:requests], both[requests:]


def solution(mesh):
    in_specs = (
        P(None, "seq"),
        P("seq"),
        P("seq", "head"),
        P("seq", None, "head"),
        P("seq", None, "head"),
        P(),
        P(),
        P("head", "seq"),
        P("seq"),
        P("seq", "head"),
        P("seq", "head"),
        P("head", "seq"),
    )
    out_specs = (P(None, "seq"), P(None, "seq"))
    return jax.shard_map(
        on_device, mesh=mesh, in_specs=in_specs, out_specs=out_specs, check_vma=False
    )
```

```python
import functools
import math

import jax
import jax.numpy as jnp
import numpy as np
from jax import lax
from jax.experimental import pallas as pl
from jax.experimental.pallas import tpu as pltpu
from jax.sharding import PartitionSpec as P

MODEL_WIDTH = 8192
QUERY_HEADS = 64
KEY_VALUE_HEADS = 8
HEAD_SIZE = 128
PAGE_TOKENS = 128
REQUESTS = 4
GROUP = QUERY_HEADS // KEY_VALUE_HEADS
ROWS = GROUP * REQUESTS
SLOTS = 16
LANES = 128
SIDE = 8
HEADS = 8

epsilon = 1e-05
neg_fill = -1e30
MESH = pl.DeviceIdType.MESH
f32 = jnp.float32
bf16 = jnp.bfloat16

PEERS = 7
RING_ORDER = (4, 3, 5, 2, 6, 1, 7)
OWNERS = 7
CHUNK = 512


def ring_distance(i):
    return 4 + ((i + 1) // 2) * (1 - 2 * lax.rem(i, 2))


def rope_frequencies():
    index = np.arange(HEAD_SIZE // 2, dtype=np.float64)
    base = 500000.0 ** (-2.0 * index / HEAD_SIZE)
    ratio = 8192.0 * base / (2.0 * math.pi)
    smooth = np.clip((ratio - 1.0) / 3.0, 0.0, 1.0)
    frequency = (1.0 - smooth) * base / 8.0 + smooth * base
    return np.concatenate([frequency, frequency]).astype(np.float32)[None, :]


def layer(
    hidden_any,
    gain_any,
    wqkv_any,
    keys_any,
    values_any,
    table_any,
    wout_any,
    fgain_any,
    wgate_any,
    wup_any,
    wdown_any,
    len_any,
    freq_any,
    both_ref,
    hidden,
    gain,
    wqkv,
    keys,
    values,
    table,
    wout,
    fgain,
    wgate,
    wup,
    wdown,
    len_ref,
    freq_ref,
    load_sem,
    qkv_out1,
    qkv_in1,
    qkv_out2,
    qkv_in2,
    live_buf,
    keys_turned,
    part_out1,
    part_in1,
    part_out2,
    part_in2,
    proj_buf,
    chunk_sum,
    chunk_out,
    chunk_in,
    piece_out,
    piece_in,
    act_buf,
    down_sum,
    down_buf,
    send_sem,
    recv_sem,
    act_sem,
):
    seq = lax.axis_index("seq")
    head = lax.axis_index("head")
    core = lax.rem(head, 2)
    row_y = seq // SIDE
    row_z = lax.rem(seq, SIDE)
    first = row_y + core * (row_z - row_y)
    second = row_z + core * (row_y - row_z)

    def seq_of(one, two):
        return one * (SIDE - (SIDE - 1) * core) + two * (1 + (SIDE - 1) * core)

    def first_peer(d):
        other = lax.rem(first + d, SIDE)
        return other, (seq_of(other, second), head)

    def second_peer(d):
        other = lax.rem(second + d, SIDE)
        return other, (seq_of(first, other), head)

    def head_peer(d):
        other = lax.rem(head + d, HEADS)
        return other, (seq, other)

    loads = {}

    def load(index, name, src, dst):
        loads[name] = pltpu.make_async_copy(src, dst, load_sem.at[index])
        loads[name].start()

    load(0, "hidden", hidden_any, hidden)
    load(1, "gain", gain_any, gain)
    load(2, "wqkv", wqkv_any, wqkv)

    barrier = pltpu.get_barrier_semaphore()

    @pl.loop(0, PEERS)
    def announce(i):
        pl.semaphore_signal(barrier, inc=1, device_id=first_peer(i + 1)[1], device_id_type=MESH)

    @pl.loop(0, PEERS)
    def announce_more(i):
        for peer in (second_peer, head_peer):
            pl.semaphore_signal(barrier, inc=1, device_id=peer(i + 1)[1], device_id_type=MESH)

    load(3, "table", table_any, table)
    load(4, "lengths", len_any, len_ref)
    load(5, "freq", freq_any, freq_ref)
    load(6, "keys", keys_any, keys)
    load(7, "values", values_any, values)
    load(8, "wout", wout_any, wout)
    load(9, "fgain", fgain_any, fgain)
    load(10, "wgate", wgate_any, wgate)
    load(11, "wup", wup_any, wup)
    load(12, "wdown", wdown_any, wdown)

    def exchange(step, peer, src_of, dst_of):
        @pl.loop(0, PEERS)
        def send(i):
            d = ring_distance(i)
            other, device = peer(d)
            pltpu.make_async_remote_copy(
                src_ref=src_of(other),
                dst_ref=dst_of(d),
                send_sem=send_sem.at[step],
                recv_sem=recv_sem.at[step],
                device_id=device,
                device_id_type=MESH,
            ).start()

    def arrive(step, blocks):
        some = blocks.at[pl.ds(0, PEERS)]
        pltpu.make_async_copy(some, some, recv_sem.at[step]).wait()

    def departed(step, blocks, count=PEERS):
        some = blocks.at[pl.ds(0, count)]
        pltpu.make_async_copy(some, some, send_sem.at[step]).wait()

    loads["hidden"].wait()
    loads["gain"].wait()
    stream = hidden[...].astype(f32)
    scaled = (stream * gain[...].astype(f32)).astype(bf16)
    square = jnp.broadcast_to(jnp.sum(stream * stream, axis=1, keepdims=True), (REQUESTS, LANES))
    loads["wqkv"].wait()
    part = jnp.dot(scaled, wqkv[...], preferred_element_type=f32)
    part_rows = jnp.concatenate(
        [part[:, t * LANES : (t + 1) * LANES] for t in range(GROUP + 2)]
        + [square, jnp.zeros((REQUESTS, LANES), f32)],
        axis=0,
    )
    qkv_out1[...] = part_rows.astype(bf16)

    pl.semaphore_wait(barrier, 21)
    exchange(0, first_peer, lambda o: qkv_out1, lambda d: qkv_in1.at[d - 1])

    sub = lax.broadcasted_iota(jnp.int32, (8, 1), 0)
    request = lax.rem(sub, REQUESTS)
    length = jnp.zeros((8, 1), jnp.int32)
    loads["lengths"].wait()
    for b in range(REQUESTS):
        length = jnp.where(request == b, len_ref[b], length)
    loads["table"].wait()
    pages = table[...]
    pages = jnp.concatenate([pages, pages], axis=0)
    page_count = pages.shape[1]
    page_index = lax.broadcasted_iota(jnp.int32, (8, page_count), 1)
    lane = lax.broadcasted_iota(jnp.int32, (8, LANES), 1)
    for j in range(SLOTS):
        hit = jnp.sum(
            jnp.where(pages == seq * SLOTS + j, (page_index + 1).astype(f32), 0.0), axis=1, keepdims=True
        ).astype(jnp.int32)
        limit = jnp.where(hit > 0, length - (hit - 1) * PAGE_TOKENS, 0)
        live_buf[:, j * LANES : (j + 1) * LANES] = jnp.where(lane < limit, 1.0, 0.0)
    mine_page = (page_index == length // PAGE_TOKENS) & (pages >= seq * SLOTS) & (pages < (seq + 1) * SLOTS)
    mine = jnp.sum(jnp.where(mine_page, 1.0, 0.0), axis=1, keepdims=True) > 0.5
    loads["freq"].wait()
    angle = length.astype(f32) * freq_ref[...]
    cos_part = jnp.cos(angle)
    sine_part = jnp.sin(angle)
    sine_part = jnp.where(lane < HEAD_SIZE // 2, -sine_part, sine_part)

    arrive(0, qkv_in1)
    total = part_rows
    for d in range(7):
        total = total + qkv_in1[d].astype(f32)
    qkv_out2[...] = total.astype(bf16)
    exchange(1, second_peer, lambda o: qkv_out2, lambda d: qkv_in2.at[d - 1])
    loads["keys"].wait()

    @pl.loop(0, SLOTS // 4)
    def turn(step):
        for k in range(4):
            j = step * 4 + k
            span = pl.ds(pl.multiple_of(j * PAGE_TOKENS, PAGE_TOKENS), PAGE_TOKENS)
            keys_turned[:, span] = keys[j].T

    loads["values"].wait()
    departed(0, qkv_in1)
    arrive(1, qkv_in2)
    for d in range(7):
        total = total + qkv_in2[d].astype(f32)

    square_all = total[40:44]
    square_all = jnp.concatenate([square_all, square_all], axis=0)
    inv_rms = lax.rsqrt(square_all / MODEL_WIDTH + epsilon)
    joined = total[0:40].reshape(5, 8, LANES) * inv_rms
    swapped = pltpu.roll(joined.reshape(40, LANES), HEAD_SIZE // 2, 1).reshape(5, 8, LANES)
    turned = joined * cos_part + swapped * sine_part
    queries = turned[0:4].reshape(ROWS, LANES).astype(bf16)
    new_key = turned[4][0:4].astype(bf16).astype(f32)
    new_key = jnp.concatenate([new_key, new_key], axis=0)
    new_value = joined[4][4:8].astype(bf16).astype(f32)
    new_value = jnp.concatenate([new_value, new_value], axis=0)

    scale = 1.0 / math.sqrt(HEAD_SIZE)
    tokens = SLOTS * PAGE_TOKENS
    scores = jnp.dot(queries, keys_turned[...], preferred_element_type=f32)
    live = live_buf[...] > 0.5
    masked = jnp.where(live, scores.reshape(4, 8, tokens) * scale, neg_fill)
    new_score = (
        jnp.sum(queries.astype(f32).reshape(4, 8, LANES) * new_key, axis=2, keepdims=True) * scale
    )
    peak = jnp.maximum(
        jnp.max(masked, axis=2, keepdims=True), jnp.where(mine, new_score, neg_fill)
    )
    weight = jnp.where(live, jnp.exp(masked - peak), 0.0)
    new_weight = jnp.where(mine, jnp.exp(new_score - peak), 0.0)
    denom = jnp.sum(weight, axis=2, keepdims=True) + new_weight
    accum = jnp.dot(
        weight.reshape(ROWS, tokens).astype(bf16),
        values[...].reshape(tokens, HEAD_SIZE),
        preferred_element_type=f32,
    ).reshape(4, 8, LANES)
    accum = accum + new_weight.astype(bf16).astype(f32) * new_value
    some = denom > 0.0
    safe = jnp.where(some, denom, 1.0)
    mean = (accum / safe).reshape(ROWS, LANES)
    lse = jnp.where(some, peak + jnp.log(safe), neg_fill).reshape(ROWS, 1)

    diagonal = lax.broadcasted_iota(jnp.int32, (ROWS, LANES), 0) == lax.broadcasted_iota(
        jnp.int32, (ROWS, LANES), 1
    )
    lse_row = jnp.sum(jnp.where(diagonal, lse, 0.0), axis=0, keepdims=True)
    stat_row = lax.broadcasted_iota(jnp.int32, (16, LANES), 0)

    def packed(mean, lse_row):
        high = lse_row.astype(bf16).astype(f32)
        rest = lse_row - high
        middle = rest.astype(bf16).astype(f32)
        low = rest - middle
        stats = jnp.where(
            stat_row == 0, high, jnp.where(stat_row == 1, middle, jnp.where(stat_row == 2, low, 0.0))
        )
        return jnp.concatenate([mean, stats], axis=0).astype(bf16)

    def merged(mean, lse_row, arrived):
        means, lses = [mean], [lse_row]
        for d in range(7):
            block = arrived[d].astype(f32)
            means.append(block[0:ROWS])
            lses.append(block[ROWS : ROWS + 1] + block[ROWS + 1 : ROWS + 2] + block[ROWS + 2 : ROWS + 3])
        best = functools.reduce(jnp.maximum, lses)
        factors = [jnp.exp(part - best) for part in lses]
        whole = functools.reduce(jnp.add, factors)
        result = None
        for factor, part in zip(factors, means):
            column = jnp.sum(jnp.where(diagonal, factor / whole, 0.0), axis=1, keepdims=True)
            result = column * part if result is None else result + column * part
        return result, best + jnp.log(whole)

    part_out1[...] = packed(mean, lse_row)
    exchange(2, first_peer, lambda o: part_out1, lambda d: part_in1.at[d - 1])
    loads["wout"].wait()
    loads["fgain"].wait()
    departed(1, qkv_in2)
    arrive(2, part_in1)
    mean, lse_row = merged(mean, lse_row, part_in1)
    part_out2[...] = packed(mean, lse_row)
    exchange(3, second_peer, lambda o: part_out2, lambda d: part_in2.at[d - 1])
    loads["wgate"].wait()
    loads["wup"].wait()
    loads["wdown"].wait()
    departed(2, part_in1)
    arrive(3, part_in2)
    mean, _ = merged(mean, lse_row, part_in2)

    attention = jnp.concatenate(
        [mean[g * REQUESTS : (g + 1) * REQUESTS] for g in range(GROUP)], axis=1
    ).astype(bf16)
    proj_buf[head] = jnp.dot(attention, wout[...], preferred_element_type=f32)
    exchange(4, head_peer, lambda o: proj_buf.at[head], lambda d: proj_buf.at[head])
    departed(3, part_in2)
    arrive(4, proj_buf)
    projected = proj_buf[0]
    for h in range(1, HEADS):
        projected = projected + proj_buf[h]
    attended = (stream + projected).astype(bf16)
    after = attended.astype(f32)
    ffn = (after * fgain[...].astype(f32)).astype(bf16)
    square = jnp.broadcast_to(jnp.sum(after * after, axis=1, keepdims=True), (REQUESTS, LANES))

    def chunk_of(owner):
        span = pl.ds(pl.multiple_of(owner * CHUNK, CHUNK), CHUNK)
        gate_part = jnp.dot(ffn, wgate[:, span], preferred_element_type=f32)
        up_part = jnp.dot(ffn, wup[:, span], preferred_element_type=f32)
        return jnp.concatenate([gate_part, up_part, square], axis=1)

    owns = first < OWNERS
    for d in RING_ORDER:
        other, device = first_peer(d)
        chunk_out[d - 1] = chunk_of(jnp.minimum(other, OWNERS - 1)).astype(bf16)

        @pl.when(other < OWNERS)
        def send_chunk():
            pltpu.make_async_remote_copy(
                src_ref=chunk_out.at[d - 1],
                dst_ref=chunk_in.at[d - 1],
                send_sem=send_sem.at[5],
                recv_sem=recv_sem.at[5],
                device_id=device,
                device_id_type=MESH,
            ).start()

    chunk_sum[...] = chunk_of(jnp.minimum(first, OWNERS - 1))
    down_sum[...] = jnp.zeros((REQUESTS, LANES), f32)
    departed(4, proj_buf)

    def down_of(owner):
        span = pl.ds(pl.multiple_of(owner * CHUNK, CHUNK), CHUNK)
        down_sum[...] += jnp.dot(act_buf[owner], wdown[span, :], preferred_element_type=f32)

    @pl.when(owns)
    def own_chunk():
        total = chunk_sum[...]
        arrive(5, chunk_in)
        for d in range(PEERS):
            total = total + chunk_in[d].astype(f32)
        piece_out[...] = total.astype(bf16)
        exchange(6, second_peer, lambda o: piece_out, lambda d: piece_in.at[d - 1])
        departed(5, chunk_in, OWNERS - 1)
        arrive(6, piece_in)
        for d in range(PEERS):
            total = total + piece_in[d].astype(f32)
        inv_norm = lax.rsqrt(total[:, 2 * CHUNK : 2 * CHUNK + 1] / MODEL_WIDTH + epsilon)
        gate = total[:, :CHUNK] * inv_norm
        act = gate / (1.0 + jnp.exp(-gate)) * (total[:, CHUNK : 2 * CHUNK] * inv_norm)
        act_buf[first] = act.astype(bf16)

        @pl.loop(0, PEERS)
        def send_act(i):
            d = ring_distance(i)
            other, device = first_peer(d)
            pltpu.make_async_remote_copy(
                src_ref=act_buf.at[first],
                dst_ref=act_buf.at[first],
                send_sem=send_sem.at[7],
                recv_sem=act_sem.at[d - 1],
                device_id=device,
                device_id_type=MESH,
            ).start()

        departed(6, piece_in)
        down_of(first)

    @pl.when(jnp.logical_not(owns))
    def no_chunk():
        departed(5, chunk_in, OWNERS)

    for d in reversed(RING_ORDER):
        owner = lax.rem(first + SIDE - d, SIDE)

        @pl.when(owner < OWNERS)
        def take_act():
            block = act_buf.at[owner]
            pltpu.make_async_copy(block, block, act_sem.at[d - 1]).wait()
            down_of(owner)

    down_buf[head] = down_sum[...]
    exchange(8, head_peer, lambda o: down_buf.at[head], lambda d: down_buf.at[head])

    @pl.when(owns)
    def act_sent():
        departed(7, act_buf)

    arrive(8, down_buf)
    down = down_buf[0]
    for h in range(1, HEADS):
        down = down + down_buf[h]
    both_ref[...] = jnp.concatenate([after, after + down], axis=0).astype(bf16)
    departed(8, down_buf)


def on_device(
    hidden_state,
    attn_gain,
    query_key_value_weight,
    key_page_cache,
    value_page_cache,
    page_table,
    lengths,
    out_weight,
    ffn_gain,
    gate_weight,
    up_weight,
    down_weight,
):
    requests, width = hidden_state.shape
    arrays = (
        hidden_state,
        attn_gain.reshape(1, width),
        query_key_value_weight,
        key_page_cache,
        value_page_cache,
        page_table,
        out_weight,
        ffn_gain.reshape(1, width),
        gate_weight,
        up_weight,
        down_weight,
        lengths,
        jnp.asarray(rope_frequencies()),
    )
    hbm_spec = pl.BlockSpec(memory_space=pltpu.HBM)
    vmem_spec = pl.BlockSpec(memory_space=pltpu.VMEM)
    out = pltpu.VMEM((2 * requests, width), bf16)
    rows = 48
    both = pl.pallas_call(
        layer,
        out_shape=out,
        in_specs=[hbm_spec] * len(arrays),
        out_specs=vmem_spec,
        scratch_shapes=[
            pltpu.SMEM(a.shape, a.dtype) if a is lengths else pltpu.VMEM(a.shape, a.dtype) for a in arrays
        ]
        + [
            pltpu.SemaphoreType.DMA((len(arrays),)),
            pltpu.VMEM((rows, LANES), bf16),
            pltpu.VMEM((7, rows, LANES), bf16),
            pltpu.VMEM((rows, LANES), bf16),
            pltpu.VMEM((7, rows, LANES), bf16),
            pltpu.VMEM((8, SLOTS * PAGE_TOKENS), f32),
            pltpu.VMEM((HEAD_SIZE, SLOTS * PAGE_TOKENS), bf16),
            pltpu.VMEM((rows, LANES), bf16),
            pltpu.VMEM((7, rows, LANES), bf16),
            pltpu.VMEM((rows, LANES), bf16),
            pltpu.VMEM((7, rows, LANES), bf16),
            pltpu.VMEM((HEADS, REQUESTS, LANES), f32),
            pltpu.VMEM((REQUESTS, 2 * CHUNK + LANES), f32),
            pltpu.VMEM((PEERS, REQUESTS, 2 * CHUNK + LANES), bf16),
            pltpu.VMEM((PEERS, REQUESTS, 2 * CHUNK + LANES), bf16),
            pltpu.VMEM((REQUESTS, 2 * CHUNK + LANES), bf16),
            pltpu.VMEM((PEERS, REQUESTS, 2 * CHUNK + LANES), bf16),
            pltpu.VMEM((SIDE, REQUESTS, CHUNK), bf16),
            pltpu.VMEM((REQUESTS, LANES), f32),
            pltpu.VMEM((HEADS, REQUESTS, LANES), f32),
            pltpu.SemaphoreType.DMA((9,)),
            pltpu.SemaphoreType.DMA((9,)),
            pltpu.SemaphoreType.DMA((PEERS,)),
        ],
        compiler_params=pltpu.CompilerParams(
            collective_id=0, has_side_effects=True, vmem_limit_bytes=48 * 1024 * 1024
        ),
    )(*[pltpu.with_memory_space_constraint(a, pltpu.HBM) for a in arrays])
    return both[:requests], both[requests:]


def solution(mesh):
    in_specs = (
        P(None, "seq"),
        P("seq"),
        P("seq", "head"),
        P("seq", None, "head"),
        P("seq", None, "head"),
        P(),
        P(),
        P("head", "seq"),
        P("seq"),
        P("seq", "head"),
        P("seq", "head"),
        P("head", "seq"),
    )
    out_specs = (P(None, "seq"), P(None, "seq"))
    return jax.shard_map(
        on_device, mesh=mesh, in_specs=in_specs, out_specs=out_specs, check_vma=False
    )
```

```python
import functools
import math

import jax
import jax.numpy as jnp
import numpy as np
from jax import lax
from jax.experimental import pallas as pl
from jax.experimental.pallas import tpu as pltpu
from jax.sharding import PartitionSpec as P

MODEL_WIDTH = 8192
QUERY_HEADS = 64
KEY_VALUE_HEADS = 8
HEAD_SIZE = 128
PAGE_TOKENS = 128
REQUESTS = 4
GROUP = QUERY_HEADS // KEY_VALUE_HEADS
ROWS = GROUP * REQUESTS
SLOTS = 16
LANES = 128
SIDE = 8
HEADS = 8

epsilon = 1e-05
neg_fill = -1e30
MESH = pl.DeviceIdType.MESH
f32 = jnp.float32
bf16 = jnp.bfloat16

PEERS = 7
OWNERS = 28
DEVICES = 64


def ring_distance(i):
    return 4 + ((i + 1) // 2) * (1 - 2 * lax.rem(i, 2))


def rope_frequencies():
    index = np.arange(HEAD_SIZE // 2, dtype=np.float64)
    base = 500000.0 ** (-2.0 * index / HEAD_SIZE)
    ratio = 8192.0 * base / (2.0 * math.pi)
    smooth = np.clip((ratio - 1.0) / 3.0, 0.0, 1.0)
    frequency = (1.0 - smooth) * base / 8.0 + smooth * base
    return np.concatenate([frequency, frequency]).astype(np.float32)[None, :]


def layer(
    hidden_any,
    gain_any,
    wqkv_any,
    keys_any,
    values_any,
    table_any,
    wout_any,
    fgain_any,
    wgate_any,
    wup_any,
    wdown_any,
    len_any,
    freq_any,
    both_ref,
    hidden,
    gain,
    wqkv,
    keys,
    values,
    table,
    wout,
    fgain,
    wgate,
    wup,
    wdown,
    len_ref,
    freq_ref,
    load_sem,
    qkv_out1,
    qkv_in1,
    qkv_out2,
    qkv_in2,
    live_buf,
    keys_turned,
    part_out1,
    part_in1,
    part_out2,
    part_in2,
    proj_buf,
    chunk_sum,
    chunk_out,
    chunk_in,
    act_buf,
    down_buf,
    send_sem,
    recv_sem,
):
    seq = lax.axis_index("seq")
    head = lax.axis_index("head")
    core = lax.rem(head, 2)
    row_y = seq // SIDE
    row_z = lax.rem(seq, SIDE)
    first = row_y + core * (row_z - row_y)
    second = row_z + core * (row_y - row_z)

    def seq_of(one, two):
        return one * (SIDE - (SIDE - 1) * core) + two * (1 + (SIDE - 1) * core)

    def first_peer(d):
        other = lax.rem(first + d, SIDE)
        return other, (seq_of(other, second), head)

    def second_peer(d):
        other = lax.rem(second + d, SIDE)
        return other, (seq_of(first, other), head)

    def head_peer(d):
        other = lax.rem(head + d, HEADS)
        return other, (seq, other)

    loads = {}

    def load(index, name, src, dst):
        loads[name] = pltpu.make_async_copy(src, dst, load_sem.at[index])
        loads[name].start()

    load(0, "hidden", hidden_any, hidden)
    load(1, "gain", gain_any, gain)
    load(2, "wqkv", wqkv_any, wqkv)

    barrier = pltpu.get_barrier_semaphore()

    @pl.loop(0, PEERS)
    def announce(i):
        pl.semaphore_signal(barrier, inc=1, device_id=first_peer(i + 1)[1], device_id_type=MESH)

    @pl.loop(0, PEERS)
    def announce_more(i):
        for peer in (second_peer, head_peer):
            pl.semaphore_signal(barrier, inc=1, device_id=peer(i + 1)[1], device_id_type=MESH)

    load(3, "table", table_any, table)
    load(4, "lengths", len_any, len_ref)
    load(5, "freq", freq_any, freq_ref)
    load(6, "keys", keys_any, keys)
    load(7, "values", values_any, values)
    load(8, "wout", wout_any, wout)
    load(9, "fgain", fgain_any, fgain)
    load(10, "wgate", wgate_any, wgate)
    load(11, "wup", wup_any, wup)
    load(12, "wdown", wdown_any, wdown)

    def exchange(step, peer, src_of, dst_of):
        @pl.loop(0, PEERS)
        def send(i):
            d = ring_distance(i)
            other, device = peer(d)
            pltpu.make_async_remote_copy(
                src_ref=src_of(other),
                dst_ref=dst_of(d),
                send_sem=send_sem.at[step],
                recv_sem=recv_sem.at[step],
                device_id=device,
                device_id_type=MESH,
            ).start()

    def arrive(step, blocks, count=PEERS):
        some = blocks.at[pl.ds(0, count)]
        pltpu.make_async_copy(some, some, recv_sem.at[step]).wait()

    def departed(step, blocks, count=PEERS):
        some = blocks.at[pl.ds(0, count)]
        pltpu.make_async_copy(some, some, send_sem.at[step]).wait()

    loads["hidden"].wait()
    loads["gain"].wait()
    stream = hidden[...].astype(f32)
    scaled = (stream * gain[...].astype(f32)).astype(bf16)
    square = jnp.broadcast_to(jnp.sum(stream * stream, axis=1, keepdims=True), (REQUESTS, LANES))
    loads["wqkv"].wait()
    part = jnp.dot(scaled, wqkv[...], preferred_element_type=f32)
    part_rows = jnp.concatenate(
        [part[:, t * LANES : (t + 1) * LANES] for t in range(GROUP + 2)]
        + [square, jnp.zeros((REQUESTS, LANES), f32)],
        axis=0,
    )
    qkv_out1[...] = part_rows.astype(bf16)

    pl.semaphore_wait(barrier, 21)
    exchange(0, first_peer, lambda o: qkv_out1, lambda d: qkv_in1.at[d - 1])

    sub = lax.broadcasted_iota(jnp.int32, (8, 1), 0)
    request = lax.rem(sub, REQUESTS)
    length = jnp.zeros((8, 1), jnp.int32)
    loads["lengths"].wait()
    for b in range(REQUESTS):
        length = jnp.where(request == b, len_ref[b], length)
    loads["table"].wait()
    pages = table[...]
    pages = jnp.concatenate([pages, pages], axis=0)
    page_count = pages.shape[1]
    page_index = lax.broadcasted_iota(jnp.int32, (8, page_count), 1)
    lane = lax.broadcasted_iota(jnp.int32, (8, LANES), 1)
    for j in range(SLOTS):
        hit = jnp.sum(
            jnp.where(pages == seq * SLOTS + j, (page_index + 1).astype(f32), 0.0), axis=1, keepdims=True
        ).astype(jnp.int32)
        limit = jnp.where(hit > 0, length - (hit - 1) * PAGE_TOKENS, 0)
        live_buf[:, j * LANES : (j + 1) * LANES] = jnp.where(lane < limit, 1.0, 0.0)
    mine_page = (page_index == length // PAGE_TOKENS) & (pages >= seq * SLOTS) & (pages < (seq + 1) * SLOTS)
    mine = jnp.sum(jnp.where(mine_page, 1.0, 0.0), axis=1, keepdims=True) > 0.5
    loads["freq"].wait()
    angle = length.astype(f32) * freq_ref[...]
    cos_part = jnp.cos(angle)
    sine_part = jnp.sin(angle)
    sine_part = jnp.where(lane < HEAD_SIZE // 2, -sine_part, sine_part)

    arrive(0, qkv_in1)
    total = part_rows
    for d in range(7):
        total = total + qkv_in1[d].astype(f32)
    qkv_out2[...] = total.astype(bf16)
    exchange(1, second_peer, lambda o: qkv_out2, lambda d: qkv_in2.at[d - 1])
    loads["keys"].wait()

    @pl.loop(0, SLOTS // 4)
    def turn(step):
        for k in range(4):
            j = step * 4 + k
            span = pl.ds(pl.multiple_of(j * PAGE_TOKENS, PAGE_TOKENS), PAGE_TOKENS)
            keys_turned[:, span] = keys[j].T

    loads["values"].wait()
    departed(0, qkv_in1)
    arrive(1, qkv_in2)
    for d in range(7):
        total = total + qkv_in2[d].astype(f32)

    square_all = total[40:44]
    square_all = jnp.concatenate([square_all, square_all], axis=0)
    inv_rms = lax.rsqrt(square_all / MODEL_WIDTH + epsilon)
    joined = total[0:40].reshape(5, 8, LANES) * inv_rms
    swapped = pltpu.roll(joined.reshape(40, LANES), HEAD_SIZE // 2, 1).reshape(5, 8, LANES)
    turned = joined * cos_part + swapped * sine_part
    queries = turned[0:4].reshape(ROWS, LANES).astype(bf16)
    new_key = turned[4][0:4].astype(bf16).astype(f32)
    new_key = jnp.concatenate([new_key, new_key], axis=0)
    new_value = joined[4][4:8].astype(bf16).astype(f32)
    new_value = jnp.concatenate([new_value, new_value], axis=0)

    scale = 1.0 / math.sqrt(HEAD_SIZE)
    tokens = SLOTS * PAGE_TOKENS
    scores = jnp.dot(queries, keys_turned[...], preferred_element_type=f32)
    live = live_buf[...] > 0.5
    masked = jnp.where(live, scores.reshape(4, 8, tokens) * scale, neg_fill)
    new_score = (
        jnp.sum(queries.astype(f32).reshape(4, 8, LANES) * new_key, axis=2, keepdims=True) * scale
    )
    peak = jnp.maximum(
        jnp.max(masked, axis=2, keepdims=True), jnp.where(mine, new_score, neg_fill)
    )
    weight = jnp.where(live, jnp.exp(masked - peak), 0.0)
    new_weight = jnp.where(mine, jnp.exp(new_score - peak), 0.0)
    denom = jnp.sum(weight, axis=2, keepdims=True) + new_weight
    accum = jnp.dot(
        weight.reshape(ROWS, tokens).astype(bf16),
        values[...].reshape(tokens, HEAD_SIZE),
        preferred_element_type=f32,
    ).reshape(4, 8, LANES)
    accum = accum + new_weight.astype(bf16).astype(f32) * new_value
    some = denom > 0.0
    safe = jnp.where(some, denom, 1.0)
    mean = (accum / safe).reshape(ROWS, LANES)
    lse = jnp.where(some, peak + jnp.log(safe), neg_fill).reshape(ROWS, 1)

    diagonal = lax.broadcasted_iota(jnp.int32, (ROWS, LANES), 0) == lax.broadcasted_iota(
        jnp.int32, (ROWS, LANES), 1
    )
    lse_row = jnp.sum(jnp.where(diagonal, lse, 0.0), axis=0, keepdims=True)
    stat_row = lax.broadcasted_iota(jnp.int32, (16, LANES), 0)

    def packed(mean, lse_row):
        high = lse_row.astype(bf16).astype(f32)
        rest = lse_row - high
        middle = rest.astype(bf16).astype(f32)
        low = rest - middle
        stats = jnp.where(
            stat_row == 0, high, jnp.where(stat_row == 1, middle, jnp.where(stat_row == 2, low, 0.0))
        )
        return jnp.concatenate([mean, stats], axis=0).astype(bf16)

    def merged(mean, lse_row, arrived):
        means, lses = [mean], [lse_row]
        for d in range(7):
            block = arrived[d].astype(f32)
            means.append(block[0:ROWS])
            lses.append(block[ROWS : ROWS + 1] + block[ROWS + 1 : ROWS + 2] + block[ROWS + 2 : ROWS + 3])
        best = functools.reduce(jnp.maximum, lses)
        factors = [jnp.exp(part - best) for part in lses]
        whole = functools.reduce(jnp.add, factors)
        result = None
        for factor, part in zip(factors, means):
            column = jnp.sum(jnp.where(diagonal, factor / whole, 0.0), axis=1, keepdims=True)
            result = column * part if result is None else result + column * part
        return result, best + jnp.log(whole)

    part_out1[...] = packed(mean, lse_row)
    exchange(2, first_peer, lambda o: part_out1, lambda d: part_in1.at[d - 1])
    loads["wout"].wait()
    loads["fgain"].wait()
    departed(1, qkv_in2)
    arrive(2, part_in1)
    mean, lse_row = merged(mean, lse_row, part_in1)
    part_out2[...] = packed(mean, lse_row)
    exchange(3, second_peer, lambda o: part_out2, lambda d: part_in2.at[d - 1])
    loads["wgate"].wait()
    loads["wup"].wait()
    loads["wdown"].wait()
    departed(2, part_in1)
    arrive(3, part_in2)
    mean, _ = merged(mean, lse_row, part_in2)

    attention = jnp.concatenate(
        [mean[g * REQUESTS : (g + 1) * REQUESTS] for g in range(GROUP)], axis=1
    ).astype(bf16)
    proj_buf[head] = jnp.dot(attention, wout[...], preferred_element_type=f32)
    exchange(4, head_peer, lambda o: proj_buf.at[head], lambda d: proj_buf.at[head])
    departed(3, part_in2)
    arrive(4, proj_buf)
    projected = proj_buf[0]
    for h in range(1, HEADS):
        projected = projected + proj_buf[h]
    attended = (stream + projected).astype(bf16)
    after = attended.astype(f32)
    ffn = (after * fgain[...].astype(f32)).astype(bf16)
    square = jnp.broadcast_to(jnp.sum(after * after, axis=1, keepdims=True), (REQUESTS, LANES))
    gate_part = jnp.dot(ffn, wgate[...], preferred_element_type=f32)
    up_part = jnp.dot(ffn, wup[...], preferred_element_type=f32)
    for p in range(OWNERS):
        span = slice(p * LANES, (p + 1) * LANES)
        chunk_out[p] = jnp.concatenate([gate_part[:, span], up_part[:, span], square], axis=1).astype(bf16)

    mine_p = seq // 2
    owns = (lax.rem(seq, 2) == core) & (mine_p < OWNERS)

    @pl.loop(0, OWNERS)
    def send_chunk(i):
        p = lax.rem(mine_p + 1 + i, OWNERS)
        owner = 2 * p + core

        @pl.when(owner != seq)
        def start():
            pltpu.make_async_remote_copy(
                src_ref=chunk_out.at[p],
                dst_ref=chunk_in.at[seq],
                send_sem=send_sem.at[5],
                recv_sem=recv_sem.at[5],
                device_id=(owner, head),
                device_id_type=MESH,
            ).start()

    departed(4, proj_buf)

    @pl.when(owns)
    def own_chunk():
        chunk_in[seq] = chunk_out[mine_p]
        arrive(5, chunk_in, DEVICES - 1)
        chunk_sum[...] = jnp.zeros((REQUESTS, 3 * LANES), f32)

        @pl.loop(0, DEVICES // 8)
        def add(i):
            total = chunk_sum[...]
            for k in range(8):
                total = total + chunk_in[i * 8 + k].astype(f32)
            chunk_sum[...] = total

        total = chunk_sum[...]
        inv_norm = lax.rsqrt(total[:, 2 * LANES :] / MODEL_WIDTH + epsilon)
        gate = total[:, :LANES] * inv_norm
        act = gate / (1.0 + jnp.exp(-gate)) * (total[:, LANES : 2 * LANES] * inv_norm)
        act_buf[mine_p] = act.astype(bf16)

        @pl.loop(1, DEVICES)
        def send_act(i):
            other = lax.rem(seq + i, DEVICES)
            pltpu.make_async_remote_copy(
                src_ref=act_buf.at[mine_p],
                dst_ref=act_buf.at[mine_p],
                send_sem=send_sem.at[6],
                recv_sem=recv_sem.at[6],
                device_id=(other, head),
                device_id_type=MESH,
            ).start()

        departed(5, chunk_in, OWNERS - 1)
        arrive(6, act_buf, OWNERS - 1)

    @pl.when(jnp.logical_not(owns))
    def no_chunk():
        departed(5, chunk_in, OWNERS)
        arrive(6, act_buf, OWNERS)

    units = jnp.concatenate([act_buf[p] for p in range(OWNERS)], axis=1)
    down_buf[head] = jnp.dot(units, wdown[...], preferred_element_type=f32)
    exchange(7, head_peer, lambda o: down_buf.at[head], lambda d: down_buf.at[head])

    @pl.when(owns)
    def act_sent():
        departed(6, act_buf, DEVICES - 1)

    arrive(7, down_buf)
    down = down_buf[0]
    for h in range(1, HEADS):
        down = down + down_buf[h]
    both_ref[...] = jnp.concatenate([after, after + down], axis=0).astype(bf16)
    departed(7, down_buf)


def on_device(
    hidden_state,
    attn_gain,
    query_key_value_weight,
    key_page_cache,
    value_page_cache,
    page_table,
    lengths,
    out_weight,
    ffn_gain,
    gate_weight,
    up_weight,
    down_weight,
):
    requests, width = hidden_state.shape
    arrays = (
        hidden_state,
        attn_gain.reshape(1, width),
        query_key_value_weight,
        key_page_cache,
        value_page_cache,
        page_table,
        out_weight,
        ffn_gain.reshape(1, width),
        gate_weight,
        up_weight,
        down_weight,
        lengths,
        jnp.asarray(rope_frequencies()),
    )
    hbm_spec = pl.BlockSpec(memory_space=pltpu.HBM)
    vmem_spec = pl.BlockSpec(memory_space=pltpu.VMEM)
    out = pltpu.VMEM((2 * requests, width), bf16)
    rows = 48
    both = pl.pallas_call(
        layer,
        out_shape=out,
        in_specs=[hbm_spec] * len(arrays),
        out_specs=vmem_spec,
        scratch_shapes=[
            pltpu.SMEM(a.shape, a.dtype) if a is lengths else pltpu.VMEM(a.shape, a.dtype) for a in arrays
        ]
        + [
            pltpu.SemaphoreType.DMA((len(arrays),)),
            pltpu.VMEM((rows, LANES), bf16),
            pltpu.VMEM((7, rows, LANES), bf16),
            pltpu.VMEM((rows, LANES), bf16),
            pltpu.VMEM((7, rows, LANES), bf16),
            pltpu.VMEM((8, SLOTS * PAGE_TOKENS), f32),
            pltpu.VMEM((HEAD_SIZE, SLOTS * PAGE_TOKENS), bf16),
            pltpu.VMEM((rows, LANES), bf16),
            pltpu.VMEM((7, rows, LANES), bf16),
            pltpu.VMEM((rows, LANES), bf16),
            pltpu.VMEM((7, rows, LANES), bf16),
            pltpu.VMEM((HEADS, REQUESTS, LANES), f32),
            pltpu.VMEM((REQUESTS, 3 * LANES), f32),
            pltpu.VMEM((OWNERS, REQUESTS, 3 * LANES), bf16),
            pltpu.VMEM((DEVICES, REQUESTS, 3 * LANES), bf16),
            pltpu.VMEM((DEVICES, REQUESTS, LANES), bf16),
            pltpu.VMEM((HEADS, REQUESTS, LANES), f32),
            pltpu.SemaphoreType.DMA((8,)),
            pltpu.SemaphoreType.DMA((8,)),
        ],
        compiler_params=pltpu.CompilerParams(
            collective_id=0, has_side_effects=True, vmem_limit_bytes=48 * 1024 * 1024
        ),
    )(*[pltpu.with_memory_space_constraint(a, pltpu.HBM) for a in arrays])
    return both[:requests], both[requests:]


def solution(mesh):
    in_specs = (
        P(None, "seq"),
        P("seq"),
        P("seq", "head"),
        P("seq", None, "head"),
        P("seq", None, "head"),
        P(),
        P(),
        P("head", "seq"),
        P("seq"),
        P("seq", "head"),
        P("seq", "head"),
        P("head", "seq"),
    )
    out_specs = (P(None, "seq"), P(None, "seq"))
    return jax.shard_map(
        on_device, mesh=mesh, in_specs=in_specs, out_specs=out_specs, check_vma=False
    )
```

```python
import functools
import math

import jax
import jax.numpy as jnp
import numpy as np
from jax import lax
from jax.experimental import pallas as pl
from jax.experimental.pallas import tpu as pltpu
from jax.sharding import PartitionSpec as P

MODEL_WIDTH = 8192
QUERY_HEADS = 64
KEY_VALUE_HEADS = 8
HEAD_SIZE = 128
PAGE_TOKENS = 128
REQUESTS = 4
GROUP = QUERY_HEADS // KEY_VALUE_HEADS
ROWS = GROUP * REQUESTS
SLOTS = 16
LANES = 128
SIDE = 8
HEADS = 8

epsilon = 1e-05
neg_fill = -1e30
MESH = pl.DeviceIdType.MESH
f32 = jnp.float32
bf16 = jnp.bfloat16

PEERS = 7
RING_ORDER = (4, 3, 5, 2, 6, 1, 7)
OWNERS = 7
CHUNK = 512


def ring_distance(i):
    return 4 + ((i + 1) // 2) * (1 - 2 * lax.rem(i, 2))


def rope_frequencies():
    index = np.arange(HEAD_SIZE // 2, dtype=np.float64)
    base = 500000.0 ** (-2.0 * index / HEAD_SIZE)
    ratio = 8192.0 * base / (2.0 * math.pi)
    smooth = np.clip((ratio - 1.0) / 3.0, 0.0, 1.0)
    frequency = (1.0 - smooth) * base / 8.0 + smooth * base
    return np.concatenate([frequency, frequency]).astype(np.float32)[None, :]


def layer(
    hidden_any,
    gain_any,
    wqkv_any,
    keys_any,
    values_any,
    table_any,
    wout_any,
    fgain_any,
    wgate_any,
    wup_any,
    wdown_any,
    len_any,
    freq_any,
    both_ref,
    hidden,
    gain,
    wqkv,
    keys,
    values,
    table,
    wout,
    fgain,
    wgate,
    wup,
    wdown,
    len_ref,
    freq_ref,
    load_sem,
    qkv_out1,
    qkv_in1,
    qkv_out2,
    qkv_in2,
    live_buf,
    keys_turned,
    part_out1,
    part_in1,
    part_out2,
    part_in2,
    proj_buf,
    chunk_out,
    chunk_in,
    piece_out,
    piece_in,
    act_buf,
    down_sum,
    down_buf,
    send_sem,
    recv_sem,
    act_sem,
):
    seq = lax.axis_index("seq")
    head = lax.axis_index("head")
    core = lax.rem(head, 2)
    row_y = seq // SIDE
    row_z = lax.rem(seq, SIDE)
    first = row_y + core * (row_z - row_y)
    second = row_z + core * (row_y - row_z)

    def seq_of(one, two):
        return one * (SIDE - (SIDE - 1) * core) + two * (1 + (SIDE - 1) * core)

    def first_peer(d):
        other = lax.rem(first + d, SIDE)
        return other, (seq_of(other, second), head)

    def second_peer(d):
        other = lax.rem(second + d, SIDE)
        return other, (seq_of(first, other), head)

    def head_peer(d):
        other = lax.rem(head + d, HEADS)
        return other, (seq, other)

    loads = {}

    def load(index, name, src, dst):
        loads[name] = pltpu.make_async_copy(src, dst, load_sem.at[index])
        loads[name].start()

    barrier = pltpu.get_barrier_semaphore()

    @pl.loop(0, PEERS)
    def announce(i):
        pl.semaphore_signal(barrier, inc=1, device_id=first_peer(i + 1)[1], device_id_type=MESH)

    load(0, "hidden", hidden_any, hidden)
    load(1, "gain", gain_any, gain)
    load(2, "wqkv", wqkv_any, wqkv)

    @pl.loop(0, PEERS)
    def announce_more(i):
        for peer in (second_peer, head_peer):
            pl.semaphore_signal(barrier, inc=1, device_id=peer(i + 1)[1], device_id_type=MESH)

    load(3, "table", table_any, table)
    load(4, "lengths", len_any, len_ref)
    load(5, "freq", freq_any, freq_ref)
    load(6, "keys", keys_any, keys)
    load(7, "values", values_any, values)
    load(8, "wout", wout_any, wout)
    load(9, "fgain", fgain_any, fgain)
    load(10, "wgate", wgate_any, wgate)
    load(11, "wup", wup_any, wup)
    load(12, "wdown", wdown_any, wdown)

    def exchange(step, peer, src_of, dst_of):
        @pl.loop(0, PEERS)
        def send(i):
            d = ring_distance(i)
            other, device = peer(d)
            pltpu.make_async_remote_copy(
                src_ref=src_of(other),
                dst_ref=dst_of(d),
                send_sem=send_sem.at[step],
                recv_sem=recv_sem.at[step],
                device_id=device,
                device_id_type=MESH,
            ).start()

    def arrive(step, blocks):
        some = blocks.at[pl.ds(0, PEERS)]
        pltpu.make_async_copy(some, some, recv_sem.at[step]).wait()

    def departed(step, blocks, count=PEERS):
        some = blocks.at[pl.ds(0, count)]
        pltpu.make_async_copy(some, some, send_sem.at[step]).wait()

    loads["hidden"].wait()
    loads["gain"].wait()
    stream = hidden[...].astype(f32)
    scaled = (stream * gain[...].astype(f32)).astype(bf16)
    square = jnp.broadcast_to(jnp.sum(stream * stream, axis=1, keepdims=True), (REQUESTS, LANES))
    loads["wqkv"].wait()
    part = jnp.dot(scaled, wqkv[...], preferred_element_type=f32)
    total = jnp.concatenate([part, square], axis=1)
    qkv_out1[...] = total.astype(bf16)

    pl.semaphore_wait(barrier, 21)
    exchange(0, first_peer, lambda o: qkv_out1, lambda d: qkv_in1.at[d - 1])

    sub = lax.broadcasted_iota(jnp.int32, (8, 1), 0)
    request = lax.rem(sub, REQUESTS)
    length = jnp.zeros((8, 1), jnp.int32)
    loads["lengths"].wait()
    for b in range(REQUESTS):
        length = jnp.where(request == b, len_ref[b], length)
    loads["table"].wait()
    pages = table[...]
    pages = jnp.concatenate([pages, pages], axis=0)
    page_count = pages.shape[1]
    page_index = lax.broadcasted_iota(jnp.int32, (8, page_count), 1)
    lane = lax.broadcasted_iota(jnp.int32, (8, LANES), 1)
    for j in range(SLOTS):
        hit = jnp.sum(
            jnp.where(pages == seq * SLOTS + j, (page_index + 1).astype(f32), 0.0), axis=1, keepdims=True
        ).astype(jnp.int32)
        limit = jnp.where(hit > 0, length - (hit - 1) * PAGE_TOKENS, 0)
        live_buf[:, j * LANES : (j + 1) * LANES] = jnp.where(lane < limit, 1.0, 0.0)
    mine_page = (page_index == length // PAGE_TOKENS) & (pages >= seq * SLOTS) & (pages < (seq + 1) * SLOTS)
    mine = jnp.sum(jnp.where(mine_page, 1.0, 0.0), axis=1, keepdims=True) > 0.5
    loads["freq"].wait()
    angle = length.astype(f32) * freq_ref[...]
    cos_part = jnp.cos(angle)
    sine_part = jnp.sin(angle)
    sine_part = jnp.where(lane < HEAD_SIZE // 2, -sine_part, sine_part)

    arrive(0, qkv_in1)
    for d in range(7):
        total = total + qkv_in1[d].astype(f32)
    qkv_out2[...] = total.astype(bf16)
    exchange(1, second_peer, lambda o: qkv_out2, lambda d: qkv_in2.at[d - 1])
    loads["keys"].wait()

    @pl.loop(0, SLOTS // 4)
    def turn(step):
        for k in range(4):
            j = step * 4 + k
            span = pl.ds(pl.multiple_of(j * PAGE_TOKENS, PAGE_TOKENS), PAGE_TOKENS)
            keys_turned[:, span] = keys[j].T

    loads["values"].wait()
    departed(0, qkv_in1)
    arrive(1, qkv_in2)
    for d in range(7):
        total = total + qkv_in2[d].astype(f32)

    inv_rms = lax.rsqrt(total[:, (GROUP + 2) * LANES :] / MODEL_WIDTH + epsilon)
    joined = jnp.concatenate(
        [total[:, t * LANES : (t + 1) * LANES] * inv_rms for t in range(GROUP + 2)], axis=0
    ).reshape(5, 8, LANES)
    swapped = pltpu.roll(joined.reshape(40, LANES), HEAD_SIZE // 2, 1).reshape(5, 8, LANES)
    turned = joined * cos_part + swapped * sine_part
    queries = turned[0:4].reshape(ROWS, LANES).astype(bf16)
    new_key = turned[4][0:4].astype(bf16).astype(f32)
    new_key = jnp.concatenate([new_key, new_key], axis=0)
    new_value = joined[4][4:8].astype(bf16).astype(f32)
    new_value = jnp.concatenate([new_value, new_value], axis=0)

    scale = 1.0 / math.sqrt(HEAD_SIZE)
    tokens = SLOTS * PAGE_TOKENS
    scores = jnp.dot(queries, keys_turned[...], preferred_element_type=f32)
    live = live_buf[...] > 0.5
    masked = jnp.where(live, scores.reshape(4, 8, tokens) * scale, neg_fill)
    new_score = (
        jnp.sum(queries.astype(f32).reshape(4, 8, LANES) * new_key, axis=2, keepdims=True) * scale
    )
    peak = jnp.maximum(
        jnp.max(masked, axis=2, keepdims=True), jnp.where(mine, new_score, neg_fill)
    )
    weight = jnp.where(live, jnp.exp(masked - peak), 0.0)
    new_weight = jnp.where(mine, jnp.exp(new_score - peak), 0.0)
    denom = jnp.sum(weight, axis=2, keepdims=True) + new_weight
    accum = jnp.dot(
        weight.reshape(ROWS, tokens).astype(bf16),
        values[...].reshape(tokens, HEAD_SIZE),
        preferred_element_type=f32,
    ).reshape(4, 8, LANES)
    accum = accum + new_weight.astype(bf16).astype(f32) * new_value
    some = denom > 0.0
    safe = jnp.where(some, denom, 1.0)
    mean = (accum / safe).reshape(ROWS, LANES)
    lse = jnp.where(some, peak + jnp.log(safe), neg_fill).reshape(ROWS, 1)

    tiles = [slice(g * REQUESTS, (g + 1) * REQUESTS) for g in range(GROUP)]
    means = [mean[rows] for rows in tiles]
    column = lax.broadcasted_iota(jnp.int32, (REQUESTS, LANES), 1)
    stats = jnp.zeros((REQUESTS, LANES), f32)
    for g, rows in enumerate(tiles):
        stats = jnp.where(column == g, lse[rows], stats)

    def packed(means, stats):
        high = stats.astype(bf16).astype(f32)
        rest = stats - high
        middle = rest.astype(bf16).astype(f32)
        low = rest - middle
        side = high + pltpu.roll(middle, GROUP, 1) + pltpu.roll(low, 2 * GROUP, 1)
        return jnp.concatenate(means + [side], axis=1).astype(bf16)

    def merged(means, stats, arrived):
        blocks = [means]
        lses = [stats]
        for d in range(PEERS):
            block = arrived[d].astype(f32)
            blocks.append([block[:, g * LANES : (g + 1) * LANES] for g in range(GROUP)])
            side = block[:, GROUP * LANES :]
            side = side + pltpu.roll(side, LANES - GROUP, 1) + pltpu.roll(side, LANES - 2 * GROUP, 1)
            lses.append(jnp.where(column < GROUP, side, 0.0))
        best = functools.reduce(jnp.maximum, lses)
        factors = [jnp.exp(part - best) for part in lses]
        whole = functools.reduce(jnp.add, factors)
        factors = [factor / whole for factor in factors]
        means = [
            functools.reduce(
                jnp.add, [factor[:, g : g + 1] * block[g] for factor, block in zip(factors, blocks)]
            )
            for g in range(GROUP)
        ]
        return means, jnp.where(column < GROUP, best + jnp.log(whole), 0.0)

    part_out1[...] = packed(means, stats)
    exchange(2, first_peer, lambda o: part_out1, lambda d: part_in1.at[d - 1])
    loads["wout"].wait()
    loads["fgain"].wait()
    departed(1, qkv_in2)
    arrive(2, part_in1)
    means, stats = merged(means, stats, part_in1)
    part_out2[...] = packed(means, stats)
    exchange(3, second_peer, lambda o: part_out2, lambda d: part_in2.at[d - 1])
    loads["wgate"].wait()
    loads["wup"].wait()
    loads["wdown"].wait()
    departed(2, part_in1)
    arrive(3, part_in2)
    means, _ = merged(means, stats, part_in2)

    attention = jnp.concatenate(means, axis=1).astype(bf16)
    proj_buf[head] = jnp.dot(attention, wout[...], preferred_element_type=f32)
    exchange(4, head_peer, lambda o: proj_buf.at[head], lambda d: proj_buf.at[head])
    departed(3, part_in2)
    arrive(4, proj_buf)
    projected = proj_buf[0]
    for h in range(1, HEADS):
        projected = projected + proj_buf[h]
    attended = (stream + projected).astype(bf16)
    after = attended.astype(f32)
    ffn = (after * fgain[...].astype(f32)).astype(bf16)
    square = jnp.broadcast_to(jnp.sum(after * after, axis=1, keepdims=True), (REQUESTS, LANES))

    gate_part = jnp.dot(ffn, wgate[...], preferred_element_type=f32)
    up_part = jnp.dot(ffn, wup[...], preferred_element_type=f32)
    for c in range(OWNERS):
        span = slice(c * CHUNK, (c + 1) * CHUNK)
        chunk_out[c] = jnp.concatenate([gate_part[:, span], up_part[:, span], square], axis=1).astype(bf16)

    owns = first < OWNERS

    @pl.loop(0, PEERS)
    def send_chunk(i):
        d = ring_distance(i)
        other, device = first_peer(d)

        @pl.when(other < OWNERS)
        def start():
            pltpu.make_async_remote_copy(
                src_ref=chunk_out.at[other],
                dst_ref=chunk_in.at[d - 1],
                send_sem=send_sem.at[5],
                recv_sem=recv_sem.at[5],
                device_id=device,
                device_id_type=MESH,
            ).start()

    down_sum[...] = jnp.zeros((REQUESTS, LANES), f32)
    departed(4, proj_buf)

    def down_of(owner):
        span = pl.ds(pl.multiple_of(owner * CHUNK, CHUNK), CHUNK)
        down_sum[...] += jnp.dot(act_buf[owner], wdown[span, :], preferred_element_type=f32)

    @pl.when(owns)
    def own_chunk():
        total = chunk_out[first].astype(f32)
        arrive(5, chunk_in)
        for d in range(PEERS):
            total = total + chunk_in[d].astype(f32)
        piece_out[...] = total.astype(bf16)
        exchange(6, second_peer, lambda o: piece_out, lambda d: piece_in.at[d - 1])
        departed(5, chunk_in, OWNERS - 1)
        arrive(6, piece_in)
        for d in range(PEERS):
            total = total + piece_in[d].astype(f32)
        inv_norm = lax.rsqrt(total[:, 2 * CHUNK : 2 * CHUNK + 1] / MODEL_WIDTH + epsilon)
        gate = total[:, :CHUNK] * inv_norm
        act = gate / (1.0 + jnp.exp(-gate)) * (total[:, CHUNK : 2 * CHUNK] * inv_norm)
        act_buf[first] = act.astype(bf16)

        @pl.loop(0, PEERS)
        def send_act(i):
            d = ring_distance(i)
            other, device = first_peer(d)
            pltpu.make_async_remote_copy(
                src_ref=act_buf.at[first],
                dst_ref=act_buf.at[first],
                send_sem=send_sem.at[7],
                recv_sem=act_sem.at[d - 1],
                device_id=device,
                device_id_type=MESH,
            ).start()

        departed(6, piece_in)
        down_of(first)

    @pl.when(jnp.logical_not(owns))
    def no_chunk():
        departed(5, chunk_in, OWNERS)

    for d in reversed(RING_ORDER):
        owner = lax.rem(first + SIDE - d, SIDE)

        @pl.when(owner < OWNERS)
        def take_act():
            block = act_buf.at[owner]
            pltpu.make_async_copy(block, block, act_sem.at[d - 1]).wait()
            down_of(owner)

    down_buf[head] = down_sum[...]
    exchange(8, head_peer, lambda o: down_buf.at[head], lambda d: down_buf.at[head])

    @pl.when(owns)
    def act_sent():
        departed(7, act_buf)

    arrive(8, down_buf)
    down = down_buf[0]
    for h in range(1, HEADS):
        down = down + down_buf[h]
    both_ref[...] = jnp.concatenate([after, after + down], axis=0).astype(bf16)
    departed(8, down_buf)


def on_device(
    hidden_state,
    attn_gain,
    query_key_value_weight,
    key_page_cache,
    value_page_cache,
    page_table,
    lengths,
    out_weight,
    ffn_gain,
    gate_weight,
    up_weight,
    down_weight,
):
    requests, width = hidden_state.shape
    arrays = (
        hidden_state,
        attn_gain.reshape(1, width),
        query_key_value_weight,
        key_page_cache,
        value_page_cache,
        page_table,
        out_weight,
        ffn_gain.reshape(1, width),
        gate_weight,
        up_weight,
        down_weight,
        lengths,
        jnp.asarray(rope_frequencies()),
    )
    hbm_spec = pl.BlockSpec(memory_space=pltpu.HBM)
    vmem_spec = pl.BlockSpec(memory_space=pltpu.VMEM)
    out = pltpu.VMEM((2 * requests, width), bf16)
    qkv_width, part_width = (GROUP + 3) * LANES, (GROUP + 1) * LANES
    both = pl.pallas_call(
        layer,
        out_shape=out,
        in_specs=[hbm_spec] * len(arrays),
        out_specs=vmem_spec,
        scratch_shapes=[
            pltpu.SMEM(a.shape, a.dtype) if a is lengths else pltpu.VMEM(a.shape, a.dtype) for a in arrays
        ]
        + [
            pltpu.SemaphoreType.DMA((len(arrays),)),
            pltpu.VMEM((requests, qkv_width), bf16),
            pltpu.VMEM((PEERS, requests, qkv_width), bf16),
            pltpu.VMEM((requests, qkv_width), bf16),
            pltpu.VMEM((PEERS, requests, qkv_width), bf16),
            pltpu.VMEM((8, SLOTS * PAGE_TOKENS), f32),
            pltpu.VMEM((HEAD_SIZE, SLOTS * PAGE_TOKENS), bf16),
            pltpu.VMEM((requests, part_width), bf16),
            pltpu.VMEM((PEERS, requests, part_width), bf16),
            pltpu.VMEM((requests, part_width), bf16),
            pltpu.VMEM((PEERS, requests, part_width), bf16),
            pltpu.VMEM((HEADS, REQUESTS, LANES), f32),
            pltpu.VMEM((SIDE, REQUESTS, 2 * CHUNK + LANES), bf16),
            pltpu.VMEM((PEERS, REQUESTS, 2 * CHUNK + LANES), bf16),
            pltpu.VMEM((REQUESTS, 2 * CHUNK + LANES), bf16),
            pltpu.VMEM((PEERS, REQUESTS, 2 * CHUNK + LANES), bf16),
            pltpu.VMEM((SIDE, REQUESTS, CHUNK), bf16),
            pltpu.VMEM((REQUESTS, LANES), f32),
            pltpu.VMEM((HEADS, REQUESTS, LANES), f32),
            pltpu.SemaphoreType.DMA((9,)),
            pltpu.SemaphoreType.DMA((9,)),
            pltpu.SemaphoreType.DMA((PEERS,)),
        ],
        compiler_params=pltpu.CompilerParams(
            collective_id=0, has_side_effects=True, vmem_limit_bytes=48 * 1024 * 1024
        ),
    )(*[pltpu.with_memory_space_constraint(a, pltpu.HBM) for a in arrays])
    return both[:requests], both[requests:]


def solution(mesh):
    in_specs = (
        P(None, "seq"),
        P("seq"),
        P("seq", "head"),
        P("seq", None, "head"),
        P("seq", None, "head"),
        P(),
        P(),
        P("head", "seq"),
        P("seq"),
        P("seq", "head"),
        P("seq", "head"),
        P("head", "seq"),
    )
    out_specs = (P(None, "seq"), P(None, "seq"))
    return jax.shard_map(
        on_device, mesh=mesh, in_specs=in_specs, out_specs=out_specs, check_vma=False
    )
```

```python
import functools
import math

import jax
import jax.numpy as jnp
import numpy as np
from jax import lax
from jax.experimental import pallas as pl
from jax.experimental.pallas import tpu as pltpu
from jax.sharding import PartitionSpec as P

MODEL_WIDTH = 8192
QUERY_HEADS = 64
KEY_VALUE_HEADS = 8
HEAD_SIZE = 128
PAGE_TOKENS = 128
REQUESTS = 4
GROUP = QUERY_HEADS // KEY_VALUE_HEADS
ROWS = GROUP * REQUESTS
SLOTS = 16
LANES = 128
SIDE = 8
HEADS = 8

epsilon = 1e-05
neg_fill = -1e30
MESH = pl.DeviceIdType.MESH
f32 = jnp.float32
bf16 = jnp.bfloat16

PEERS = 7
CLASSES = 4
CHUNK = 896


def ring_distance(i):
    return 4 + ((i + 1) // 2) * (1 - 2 * lax.rem(i, 2))


def rope_frequencies():
    index = np.arange(HEAD_SIZE // 2, dtype=np.float64)
    base = 500000.0 ** (-2.0 * index / HEAD_SIZE)
    ratio = 8192.0 * base / (2.0 * math.pi)
    smooth = np.clip((ratio - 1.0) / 3.0, 0.0, 1.0)
    frequency = (1.0 - smooth) * base / 8.0 + smooth * base
    return np.concatenate([frequency, frequency]).astype(np.float32)[None, :]


def layer(
    hidden_any,
    gain_any,
    wqkv_any,
    keys_any,
    values_any,
    table_any,
    wout_any,
    fgain_any,
    wgate_any,
    wup_any,
    wdown_any,
    len_any,
    freq_any,
    both_ref,
    hidden,
    gain,
    wqkv,
    keys,
    values,
    table,
    wout,
    fgain,
    wgate,
    wup,
    wdown,
    len_ref,
    freq_ref,
    load_sem,
    qkv_out1,
    qkv_in1,
    qkv_out2,
    qkv_in2,
    live_buf,
    keys_turned,
    part_out1,
    part_in1,
    part_out2,
    part_in2,
    proj_buf,
    chunk_out,
    chunk_in,
    piece_out,
    piece_in,
    act_buf,
    down_buf,
    send_sem,
    recv_sem,
):
    seq = lax.axis_index("seq")
    head = lax.axis_index("head")
    core = lax.rem(head, 2)
    row_y = seq // SIDE
    row_z = lax.rem(seq, SIDE)
    first = row_y + core * (row_z - row_y)
    second = row_z + core * (row_y - row_z)

    def seq_of(one, two):
        return one * (SIDE - (SIDE - 1) * core) + two * (1 + (SIDE - 1) * core)

    def first_peer(d):
        other = lax.rem(first + d, SIDE)
        return other, (seq_of(other, second), head)

    def second_peer(d):
        other = lax.rem(second + d, SIDE)
        return other, (seq_of(first, other), head)

    def head_peer(d):
        other = lax.rem(head + d, HEADS)
        return other, (seq, other)

    loads = {}

    def load(index, name, src, dst):
        loads[name] = pltpu.make_async_copy(src, dst, load_sem.at[index])
        loads[name].start()

    barrier = pltpu.get_barrier_semaphore()

    @pl.loop(0, PEERS)
    def announce(i):
        pl.semaphore_signal(barrier, inc=1, device_id=first_peer(ring_distance(i))[1], device_id_type=MESH)

    load(0, "hidden", hidden_any, hidden)
    load(1, "gain", gain_any, gain)
    load(2, "wqkv", wqkv_any, wqkv)
    load(3, "table", table_any, table)
    load(4, "lengths", len_any, len_ref)
    load(5, "freq", freq_any, freq_ref)

    @pl.loop(0, PEERS)
    def announce_more(i):
        for peer in (second_peer, head_peer):
            pl.semaphore_signal(barrier, inc=1, device_id=peer(ring_distance(i))[1], device_id_type=MESH)

    def exchange(step, peer, src_of, dst_of):
        @pl.loop(0, PEERS)
        def send(i):
            d = ring_distance(i)
            other, device = peer(d)
            pltpu.make_async_remote_copy(
                src_ref=src_of(other),
                dst_ref=dst_of(d),
                send_sem=send_sem.at[step],
                recv_sem=recv_sem.at[step],
                device_id=device,
                device_id_type=MESH,
            ).start()

    def arrive(step, blocks, count=PEERS):
        some = blocks.at[pl.ds(0, count)]
        pltpu.make_async_copy(some, some, recv_sem.at[step]).wait()

    def departed(step, blocks, count=PEERS):
        some = blocks.at[pl.ds(0, count)]
        pltpu.make_async_copy(some, some, send_sem.at[step]).wait()

    loads["hidden"].wait()
    loads["gain"].wait()
    stream = hidden[...].astype(f32)
    scaled = (stream * gain[...].astype(f32)).astype(bf16)
    square = jnp.broadcast_to(jnp.sum(stream * stream, axis=1, keepdims=True), (REQUESTS, LANES))
    loads["wqkv"].wait()
    part = jnp.dot(scaled, wqkv[...], preferred_element_type=f32)
    total = jnp.concatenate([part, square], axis=1)
    qkv_out1[...] = total.astype(bf16)

    pl.semaphore_wait(barrier, 21)
    exchange(0, first_peer, lambda o: qkv_out1, lambda d: qkv_in1.at[d - 1])

    load(6, "keys", keys_any, keys)
    load(7, "values", values_any, values)
    load(8, "wout", wout_any, wout)
    load(9, "fgain", fgain_any, fgain)
    load(10, "wgate", wgate_any, wgate)
    load(11, "wup", wup_any, wup)
    load(12, "wdown", wdown_any, wdown)

    sub = lax.broadcasted_iota(jnp.int32, (8, 1), 0)
    request = lax.rem(sub, REQUESTS)
    length = jnp.zeros((8, 1), jnp.int32)
    loads["lengths"].wait()
    for b in range(REQUESTS):
        length = jnp.where(request == b, len_ref[b], length)
    loads["table"].wait()
    pages = table[...]
    pages = jnp.concatenate([pages, pages], axis=0)
    page_count = pages.shape[1]
    page_index = lax.broadcasted_iota(jnp.int32, (8, page_count), 1)
    lane = lax.broadcasted_iota(jnp.int32, (8, LANES), 1)
    for j in range(SLOTS):
        hit = jnp.sum(
            jnp.where(pages == seq * SLOTS + j, (page_index + 1).astype(f32), 0.0), axis=1, keepdims=True
        ).astype(jnp.int32)
        limit = jnp.where(hit > 0, length - (hit - 1) * PAGE_TOKENS, 0)
        live_buf[:, j * LANES : (j + 1) * LANES] = jnp.where(lane < limit, 1.0, 0.0)
    mine_page = (page_index == length // PAGE_TOKENS) & (pages >= seq * SLOTS) & (pages < (seq + 1) * SLOTS)
    mine = jnp.sum(jnp.where(mine_page, 1.0, 0.0), axis=1, keepdims=True) > 0.5
    loads["freq"].wait()
    angle = length.astype(f32) * freq_ref[...]
    cos_part = jnp.cos(angle)
    sine_part = jnp.sin(angle)
    sine_part = jnp.where(lane < HEAD_SIZE // 2, -sine_part, sine_part)

    arrive(0, qkv_in1)
    for d in range(7):
        total = total + qkv_in1[d].astype(f32)
    qkv_out2[...] = total.astype(bf16)
    exchange(1, second_peer, lambda o: qkv_out2, lambda d: qkv_in2.at[d - 1])
    loads["keys"].wait()

    @pl.loop(0, SLOTS // 4)
    def turn(step):
        for k in range(4):
            j = step * 4 + k
            span = pl.ds(pl.multiple_of(j * PAGE_TOKENS, PAGE_TOKENS), PAGE_TOKENS)
            keys_turned[:, span] = keys[j].T

    loads["values"].wait()
    departed(0, qkv_in1)
    arrive(1, qkv_in2)
    for d in range(7):
        total = total + qkv_in2[d].astype(f32)

    inv_rms = lax.rsqrt(total[:, (GROUP + 2) * LANES :] / MODEL_WIDTH + epsilon)
    joined = jnp.concatenate(
        [total[:, t * LANES : (t + 1) * LANES] * inv_rms for t in range(GROUP + 2)], axis=0
    ).reshape(5, 8, LANES)
    swapped = pltpu.roll(joined.reshape(40, LANES), HEAD_SIZE // 2, 1).reshape(5, 8, LANES)
    turned = joined * cos_part + swapped * sine_part
    queries = turned[0:4].reshape(ROWS, LANES).astype(bf16)
    new_key = turned[4][0:4].astype(bf16).astype(f32)
    new_key = jnp.concatenate([new_key, new_key], axis=0)
    new_value = joined[4][4:8].astype(bf16).astype(f32)
    new_value = jnp.concatenate([new_value, new_value], axis=0)

    scale = 1.0 / math.sqrt(HEAD_SIZE)
    tokens = SLOTS * PAGE_TOKENS
    scores = jnp.dot(queries, keys_turned[...], preferred_element_type=f32)
    live = live_buf[...] > 0.5
    masked = jnp.where(live, scores.reshape(4, 8, tokens) * scale, neg_fill)
    new_score = (
        jnp.sum(queries.astype(f32).reshape(4, 8, LANES) * new_key, axis=2, keepdims=True) * scale
    )
    peak = jnp.maximum(
        jnp.max(masked, axis=2, keepdims=True), jnp.where(mine, new_score, neg_fill)
    )
    weight = jnp.where(live, jnp.exp(masked - peak), 0.0)
    new_weight = jnp.where(mine, jnp.exp(new_score - peak), 0.0)
    denom = jnp.sum(weight, axis=2, keepdims=True) + new_weight
    accum = jnp.dot(
        weight.reshape(ROWS, tokens).astype(bf16),
        values[...].reshape(tokens, HEAD_SIZE),
        preferred_element_type=f32,
    ).reshape(4, 8, LANES)
    accum = accum + new_weight.astype(bf16).astype(f32) * new_value
    some = denom > 0.0
    safe = jnp.where(some, denom, 1.0)
    mean = (accum / safe).reshape(ROWS, LANES)
    lse = jnp.where(some, peak + jnp.log(safe), neg_fill).reshape(ROWS, 1)

    tiles = [slice(g * REQUESTS, (g + 1) * REQUESTS) for g in range(GROUP)]
    means = [mean[rows] for rows in tiles]
    column = lax.broadcasted_iota(jnp.int32, (REQUESTS, LANES), 1)
    stats = jnp.zeros((REQUESTS, LANES), f32)
    for g, rows in enumerate(tiles):
        stats = jnp.where(column == g, lse[rows], stats)

    def packed(means, stats):
        high = stats.astype(bf16).astype(f32)
        rest = stats - high
        middle = rest.astype(bf16).astype(f32)
        low = rest - middle
        side = high + pltpu.roll(middle, GROUP, 1) + pltpu.roll(low, 2 * GROUP, 1)
        return jnp.concatenate(means + [side], axis=1).astype(bf16)

    def merged(means, stats, arrived):
        blocks = [means]
        lses = [stats]
        for d in range(PEERS):
            block = arrived[d].astype(f32)
            blocks.append([block[:, g * LANES : (g + 1) * LANES] for g in range(GROUP)])
            side = block[:, GROUP * LANES :]
            side = side + pltpu.roll(side, LANES - GROUP, 1) + pltpu.roll(side, LANES - 2 * GROUP, 1)
            lses.append(jnp.where(column < GROUP, side, 0.0))
        best = functools.reduce(jnp.maximum, lses)
        factors = [jnp.exp(part - best) for part in lses]
        whole = functools.reduce(jnp.add, factors)
        factors = [factor / whole for factor in factors]
        means = [
            functools.reduce(
                jnp.add, [factor[:, g : g + 1] * block[g] for factor, block in zip(factors, blocks)]
            )
            for g in range(GROUP)
        ]
        return means, jnp.where(column < GROUP, best + jnp.log(whole), 0.0)

    part_out1[...] = packed(means, stats)
    exchange(2, first_peer, lambda o: part_out1, lambda d: part_in1.at[d - 1])
    loads["wout"].wait()
    loads["fgain"].wait()
    departed(1, qkv_in2)
    arrive(2, part_in1)
    means, stats = merged(means, stats, part_in1)
    part_out2[...] = packed(means, stats)
    exchange(3, second_peer, lambda o: part_out2, lambda d: part_in2.at[d - 1])
    loads["wgate"].wait()
    loads["wup"].wait()
    loads["wdown"].wait()
    departed(2, part_in1)
    arrive(3, part_in2)
    means, _ = merged(means, stats, part_in2)

    attention = jnp.concatenate(means, axis=1).astype(bf16)
    proj_buf[head] = jnp.dot(attention, wout[...], preferred_element_type=f32)
    exchange(4, head_peer, lambda o: proj_buf.at[head], lambda d: proj_buf.at[head])
    departed(3, part_in2)
    arrive(4, proj_buf)
    projected = proj_buf[0]
    for h in range(1, HEADS):
        projected = projected + proj_buf[h]
    attended = (stream + projected).astype(bf16)
    after = attended.astype(f32)
    ffn = (after * fgain[...].astype(f32)).astype(bf16)
    square = jnp.broadcast_to(jnp.sum(after * after, axis=1, keepdims=True), (REQUESTS, LANES))

    gate_part = jnp.dot(ffn, wgate[...], preferred_element_type=f32)
    up_part = jnp.dot(ffn, wup[...], preferred_element_type=f32)
    for c in range(CLASSES):
        span = slice(c * CHUNK, (c + 1) * CHUNK)
        chunk_out[c] = jnp.concatenate([gate_part[:, span], up_part[:, span], square], axis=1).astype(bf16)

    exchange(
        5, first_peer, lambda o: chunk_out.at[lax.rem(o, CLASSES)], lambda d: chunk_in.at[d - 1]
    )
    mine = lax.rem(first, CLASSES)
    total = chunk_out[mine].astype(f32)
    departed(4, proj_buf)
    arrive(5, chunk_in)
    for d in range(PEERS):
        total = total + chunk_in[d].astype(f32)
    piece_out[...] = total.astype(bf16)
    exchange(6, second_peer, lambda o: piece_out, lambda d: piece_in.at[d - 1])
    departed(5, chunk_in)
    arrive(6, piece_in)
    for d in range(PEERS):
        total = total + piece_in[d].astype(f32)
    inv_norm = lax.rsqrt(total[:, 2 * CHUNK : 2 * CHUNK + 1] / MODEL_WIDTH + epsilon)
    gate = total[:, :CHUNK] * inv_norm
    act = gate / (1.0 + jnp.exp(-gate)) * (total[:, CHUNK : 2 * CHUNK] * inv_norm)
    act_buf[mine] = act.astype(bf16)

    for d in (2, 1, SIDE - 1):
        _, device = first_peer(d)
        pltpu.make_async_remote_copy(
            src_ref=act_buf.at[mine],
            dst_ref=act_buf.at[mine],
            send_sem=send_sem.at[7],
            recv_sem=recv_sem.at[7],
            device_id=device,
            device_id_type=MESH,
        ).start()
    departed(6, piece_in)
    arrive(7, act_buf, CLASSES - 1)
    units = jnp.concatenate([act_buf[c] for c in range(CLASSES)], axis=1)
    down_buf[head] = jnp.dot(units, wdown[...], preferred_element_type=f32)
    exchange(8, head_peer, lambda o: down_buf.at[head], lambda d: down_buf.at[head])
    departed(7, act_buf, CLASSES - 1)
    arrive(8, down_buf)
    down = down_buf[0]
    for h in range(1, HEADS):
        down = down + down_buf[h]
    both_ref[...] = jnp.concatenate([after, after + down], axis=0).astype(bf16)
    departed(8, down_buf)


def on_device(
    hidden_state,
    attn_gain,
    query_key_value_weight,
    key_page_cache,
    value_page_cache,
    page_table,
    lengths,
    out_weight,
    ffn_gain,
    gate_weight,
    up_weight,
    down_weight,
):
    requests, width = hidden_state.shape
    arrays = (
        hidden_state,
        attn_gain.reshape(1, width),
        query_key_value_weight,
        key_page_cache,
        value_page_cache,
        page_table,
        out_weight,
        ffn_gain.reshape(1, width),
        gate_weight,
        up_weight,
        down_weight,
        lengths,
        jnp.asarray(rope_frequencies()),
    )
    hbm_spec = pl.BlockSpec(memory_space=pltpu.HBM)
    vmem_spec = pl.BlockSpec(memory_space=pltpu.VMEM)
    out = pltpu.VMEM((2 * requests, width), bf16)
    qkv_width, part_width = (GROUP + 3) * LANES, (GROUP + 1) * LANES
    both = pl.pallas_call(
        layer,
        out_shape=out,
        in_specs=[hbm_spec] * len(arrays),
        out_specs=vmem_spec,
        scratch_shapes=[
            pltpu.SMEM(a.shape, a.dtype) if a is lengths else pltpu.VMEM(a.shape, a.dtype) for a in arrays
        ]
        + [
            pltpu.SemaphoreType.DMA((len(arrays),)),
            pltpu.VMEM((requests, qkv_width), bf16),
            pltpu.VMEM((PEERS, requests, qkv_width), bf16),
            pltpu.VMEM((requests, qkv_width), bf16),
            pltpu.VMEM((PEERS, requests, qkv_width), bf16),
            pltpu.VMEM((8, SLOTS * PAGE_TOKENS), f32),
            pltpu.VMEM((HEAD_SIZE, SLOTS * PAGE_TOKENS), bf16),
            pltpu.VMEM((requests, part_width), bf16),
            pltpu.VMEM((PEERS, requests, part_width), bf16),
            pltpu.VMEM((requests, part_width), bf16),
            pltpu.VMEM((PEERS, requests, part_width), bf16),
            pltpu.VMEM((HEADS, REQUESTS, LANES), f32),
            pltpu.VMEM((CLASSES, REQUESTS, 2 * CHUNK + LANES), bf16),
            pltpu.VMEM((PEERS, REQUESTS, 2 * CHUNK + LANES), bf16),
            pltpu.VMEM((REQUESTS, 2 * CHUNK + LANES), bf16),
            pltpu.VMEM((PEERS, REQUESTS, 2 * CHUNK + LANES), bf16),
            pltpu.VMEM((CLASSES, REQUESTS, CHUNK), bf16),
            pltpu.VMEM((HEADS, REQUESTS, LANES), f32),
            pltpu.SemaphoreType.DMA((9,)),
            pltpu.SemaphoreType.DMA((9,)),
        ],
        compiler_params=pltpu.CompilerParams(
            collective_id=0, has_side_effects=True, vmem_limit_bytes=48 * 1024 * 1024
        ),
    )(*[pltpu.with_memory_space_constraint(a, pltpu.HBM) for a in arrays])
    return both[:requests], both[requests:]


def solution(mesh):
    in_specs = (
        P(None, "seq"),
        P("seq"),
        P("seq", "head"),
        P("seq", None, "head"),
        P("seq", None, "head"),
        P(),
        P(),
        P("head", "seq"),
        P("seq"),
        P("seq", "head"),
        P("seq", "head"),
        P("head", "seq"),
    )
    out_specs = (P(None, "seq"), P(None, "seq"))
    return jax.shard_map(
        on_device, mesh=mesh, in_specs=in_specs, out_specs=out_specs, check_vma=False
    )
```

```python
import functools
import math

import jax
import jax.numpy as jnp
import numpy as np
from jax import lax
from jax.experimental import pallas as pl
from jax.experimental.pallas import tpu as pltpu
from jax.sharding import PartitionSpec as P

MODEL_WIDTH = 8192
QUERY_HEADS = 64
KEY_VALUE_HEADS = 8
HEAD_SIZE = 128
PAGE_TOKENS = 128
REQUESTS = 4
GROUP = QUERY_HEADS // KEY_VALUE_HEADS
ROWS = GROUP * REQUESTS
SLOTS = 16
LANES = 128
SIDE = 8
HEADS = 8

epsilon = 1e-05
neg_fill = -1e30
MESH = pl.DeviceIdType.MESH
f32 = jnp.float32
bf16 = jnp.bfloat16

PEERS = 7
CLASSES = 4
CHUNK = 896


def ring_distance(i):
    return 4 + ((i + 1) // 2) * (1 - 2 * lax.rem(i, 2))


def rope_frequencies():
    index = np.arange(HEAD_SIZE // 2, dtype=np.float64)
    base = 500000.0 ** (-2.0 * index / HEAD_SIZE)
    ratio = 8192.0 * base / (2.0 * math.pi)
    smooth = np.clip((ratio - 1.0) / 3.0, 0.0, 1.0)
    frequency = (1.0 - smooth) * base / 8.0 + smooth * base
    return np.concatenate([frequency, frequency]).astype(np.float32)[None, :]


def layer(
    hidden_any,
    gain_any,
    wqkv_any,
    keys_any,
    values_any,
    table_any,
    wout_any,
    fgain_any,
    wgate_any,
    wup_any,
    wdown_any,
    len_any,
    freq_any,
    both_ref,
    hidden,
    gain,
    wqkv,
    keys,
    values,
    table,
    wout,
    fgain,
    wgate,
    wup,
    wdown,
    len_ref,
    freq_ref,
    load_sem,
    qkv_out1,
    qkv_in1,
    qkv_out2,
    qkv_in2,
    live_buf,
    keys_turned,
    part_out1,
    part_in1,
    part_out2,
    part_in2,
    proj_buf,
    chunk_sum,
    chunk_out,
    chunk_in,
    piece_out,
    piece_in,
    act_buf,
    down_buf,
    send_sem,
    recv_sem,
    act_sem,
):
    seq = lax.axis_index("seq")
    head = lax.axis_index("head")
    core = lax.rem(head, 2)
    row_y = seq // SIDE
    row_z = lax.rem(seq, SIDE)
    first = row_y + core * (row_z - row_y)
    second = row_z + core * (row_y - row_z)

    def seq_of(one, two):
        return one * (SIDE - (SIDE - 1) * core) + two * (1 + (SIDE - 1) * core)

    def first_peer(d):
        other = lax.rem(first + d, SIDE)
        return other, (seq_of(other, second), head)

    def second_peer(d):
        other = lax.rem(second + d, SIDE)
        return other, (seq_of(first, other), head)

    def head_peer(d):
        other = lax.rem(head + d, HEADS)
        return other, (seq, other)

    loads = {}

    def load(index, name, src, dst):
        loads[name] = pltpu.make_async_copy(src, dst, load_sem.at[index])
        loads[name].start()

    barrier = pltpu.get_barrier_semaphore()

    @pl.loop(0, PEERS)
    def announce(i):
        pl.semaphore_signal(barrier, inc=1, device_id=first_peer(ring_distance(i))[1], device_id_type=MESH)

    load(0, "hidden", hidden_any, hidden)
    load(1, "gain", gain_any, gain)
    load(2, "wqkv", wqkv_any, wqkv)
    load(3, "table", table_any, table)
    load(4, "lengths", len_any, len_ref)
    load(5, "freq", freq_any, freq_ref)

    @pl.loop(0, PEERS)
    def announce_more(i):
        for peer in (second_peer, head_peer):
            pl.semaphore_signal(barrier, inc=1, device_id=peer(ring_distance(i))[1], device_id_type=MESH)

    def exchange(step, peer, src_of, dst_of):
        @pl.loop(0, PEERS)
        def send(i):
            d = ring_distance(i)
            other, device = peer(d)
            pltpu.make_async_remote_copy(
                src_ref=src_of(other),
                dst_ref=dst_of(d),
                send_sem=send_sem.at[step],
                recv_sem=recv_sem.at[step],
                device_id=device,
                device_id_type=MESH,
            ).start()

    def arrive(step, blocks, count=PEERS):
        some = blocks.at[pl.ds(0, count)]
        pltpu.make_async_copy(some, some, recv_sem.at[step]).wait()

    def departed(step, blocks, count=PEERS):
        some = blocks.at[pl.ds(0, count)]
        pltpu.make_async_copy(some, some, send_sem.at[step]).wait()

    loads["hidden"].wait()
    loads["gain"].wait()
    stream = hidden[...].astype(f32)
    scaled = (stream * gain[...].astype(f32)).astype(bf16)
    square = jnp.broadcast_to(jnp.sum(stream * stream, axis=1, keepdims=True), (REQUESTS, LANES))
    loads["wqkv"].wait()
    part = jnp.dot(scaled, wqkv[...], preferred_element_type=f32)
    total = jnp.concatenate([part, square], axis=1)
    qkv_out1[...] = total.astype(bf16)

    pl.semaphore_wait(barrier, 21)
    exchange(0, first_peer, lambda o: qkv_out1, lambda d: qkv_in1.at[d - 1])

    load(6, "keys", keys_any, keys)
    load(7, "values", values_any, values)
    load(8, "wout", wout_any, wout)
    load(9, "fgain", fgain_any, fgain)
    load(10, "wgate", wgate_any, wgate)
    load(11, "wup", wup_any, wup)
    load(12, "wdown", wdown_any, wdown)

    sub = lax.broadcasted_iota(jnp.int32, (8, 1), 0)
    request = lax.rem(sub, REQUESTS)
    length = jnp.zeros((8, 1), jnp.int32)
    loads["lengths"].wait()
    for b in range(REQUESTS):
        length = jnp.where(request == b, len_ref[b], length)
    loads["table"].wait()
    pages = table[...]
    pages = jnp.concatenate([pages, pages], axis=0)
    page_count = pages.shape[1]
    page_index = lax.broadcasted_iota(jnp.int32, (8, page_count), 1)
    lane = lax.broadcasted_iota(jnp.int32, (8, LANES), 1)
    for j in range(SLOTS):
        hit = jnp.sum(
            jnp.where(pages == seq * SLOTS + j, (page_index + 1).astype(f32), 0.0), axis=1, keepdims=True
        ).astype(jnp.int32)
        limit = jnp.where(hit > 0, length - (hit - 1) * PAGE_TOKENS, 0)
        live_buf[:, j * LANES : (j + 1) * LANES] = jnp.where(lane < limit, 1.0, 0.0)
    mine_page = (page_index == length // PAGE_TOKENS) & (pages >= seq * SLOTS) & (pages < (seq + 1) * SLOTS)
    mine = jnp.sum(jnp.where(mine_page, 1.0, 0.0), axis=1, keepdims=True) > 0.5
    loads["freq"].wait()
    angle = length.astype(f32) * freq_ref[...]
    cos_part = jnp.cos(angle)
    sine_part = jnp.sin(angle)
    sine_part = jnp.where(lane < HEAD_SIZE // 2, -sine_part, sine_part)

    arrive(0, qkv_in1)
    for d in range(7):
        total = total + qkv_in1[d].astype(f32)
    qkv_out2[...] = total.astype(bf16)
    exchange(1, second_peer, lambda o: qkv_out2, lambda d: qkv_in2.at[d - 1])
    loads["keys"].wait()

    @pl.loop(0, SLOTS // 4)
    def turn(step):
        for k in range(4):
            j = step * 4 + k
            span = pl.ds(pl.multiple_of(j * PAGE_TOKENS, PAGE_TOKENS), PAGE_TOKENS)
            keys_turned[:, span] = keys[j].T

    loads["values"].wait()
    departed(0, qkv_in1)
    arrive(1, qkv_in2)
    for d in range(7):
        total = total + qkv_in2[d].astype(f32)

    inv_rms = lax.rsqrt(total[:, (GROUP + 2) * LANES :] / MODEL_WIDTH + epsilon)
    joined = jnp.concatenate(
        [total[:, t * LANES : (t + 1) * LANES] * inv_rms for t in range(GROUP + 2)], axis=0
    ).reshape(5, 8, LANES)
    swapped = pltpu.roll(joined.reshape(40, LANES), HEAD_SIZE // 2, 1).reshape(5, 8, LANES)
    turned = joined * cos_part + swapped * sine_part
    queries = turned[0:4].reshape(ROWS, LANES).astype(bf16)
    new_key = turned[4][0:4].astype(bf16).astype(f32)
    new_key = jnp.concatenate([new_key, new_key], axis=0)
    new_value = joined[4][4:8].astype(bf16).astype(f32)
    new_value = jnp.concatenate([new_value, new_value], axis=0)

    scale = 1.0 / math.sqrt(HEAD_SIZE)
    tokens = SLOTS * PAGE_TOKENS
    scores = jnp.dot(queries, keys_turned[...], preferred_element_type=f32)
    live = live_buf[...] > 0.5
    masked = jnp.where(live, scores.reshape(4, 8, tokens) * scale, neg_fill)
    new_score = (
        jnp.sum(queries.astype(f32).reshape(4, 8, LANES) * new_key, axis=2, keepdims=True) * scale
    )
    peak = jnp.maximum(
        jnp.max(masked, axis=2, keepdims=True), jnp.where(mine, new_score, neg_fill)
    )
    weight = jnp.where(live, jnp.exp(masked - peak), 0.0)
    new_weight = jnp.where(mine, jnp.exp(new_score - peak), 0.0)
    denom = jnp.sum(weight, axis=2, keepdims=True) + new_weight
    accum = jnp.dot(
        weight.reshape(ROWS, tokens).astype(bf16),
        values[...].reshape(tokens, HEAD_SIZE),
        preferred_element_type=f32,
    ).reshape(4, 8, LANES)
    accum = accum + new_weight.astype(bf16).astype(f32) * new_value
    some = denom > 0.0
    safe = jnp.where(some, denom, 1.0)
    mean = (accum / safe).reshape(ROWS, LANES)
    lse = jnp.where(some, peak + jnp.log(safe), neg_fill).reshape(ROWS, 1)

    tiles = [slice(g * REQUESTS, (g + 1) * REQUESTS) for g in range(GROUP)]
    means = [mean[rows] for rows in tiles]
    column = lax.broadcasted_iota(jnp.int32, (REQUESTS, LANES), 1)
    stats = jnp.zeros((REQUESTS, LANES), f32)
    for g, rows in enumerate(tiles):
        stats = jnp.where(column == g, lse[rows], stats)

    def packed(means, stats):
        high = stats.astype(bf16).astype(f32)
        rest = stats - high
        middle = rest.astype(bf16).astype(f32)
        low = rest - middle
        side = high + pltpu.roll(middle, GROUP, 1) + pltpu.roll(low, 2 * GROUP, 1)
        return jnp.concatenate(means + [side], axis=1).astype(bf16)

    def merged(means, stats, arrived):
        blocks = [means]
        lses = [stats]
        for d in range(PEERS):
            block = arrived[d].astype(f32)
            blocks.append([block[:, g * LANES : (g + 1) * LANES] for g in range(GROUP)])
            side = block[:, GROUP * LANES :]
            side = side + pltpu.roll(side, LANES - GROUP, 1) + pltpu.roll(side, LANES - 2 * GROUP, 1)
            lses.append(jnp.where(column < GROUP, side, 0.0))
        best = functools.reduce(jnp.maximum, lses)
        factors = [jnp.exp(part - best) for part in lses]
        whole = functools.reduce(jnp.add, factors)
        factors = [factor / whole for factor in factors]
        means = [
            functools.reduce(
                jnp.add, [factor[:, g : g + 1] * block[g] for factor, block in zip(factors, blocks)]
            )
            for g in range(GROUP)
        ]
        return means, jnp.where(column < GROUP, best + jnp.log(whole), 0.0)

    part_out1[...] = packed(means, stats)
    exchange(2, first_peer, lambda o: part_out1, lambda d: part_in1.at[d - 1])
    loads["wout"].wait()
    loads["fgain"].wait()
    departed(1, qkv_in2)
    arrive(2, part_in1)
    means, stats = merged(means, stats, part_in1)
    part_out2[...] = packed(means, stats)
    exchange(3, second_peer, lambda o: part_out2, lambda d: part_in2.at[d - 1])
    loads["wgate"].wait()
    loads["wup"].wait()
    loads["wdown"].wait()
    departed(2, part_in1)
    arrive(3, part_in2)
    means, _ = merged(means, stats, part_in2)

    attention = jnp.concatenate(means, axis=1).astype(bf16)
    proj_buf[head] = jnp.dot(attention, wout[...], preferred_element_type=f32)
    exchange(4, head_peer, lambda o: proj_buf.at[head], lambda d: proj_buf.at[head])
    departed(3, part_in2)
    arrive(4, proj_buf)
    projected = proj_buf[0]
    for h in range(1, HEADS):
        projected = projected + proj_buf[h]
    attended = (stream + projected).astype(bf16)
    after = attended.astype(f32)
    ffn = (after * fgain[...].astype(f32)).astype(bf16)
    square = jnp.broadcast_to(jnp.sum(after * after, axis=1, keepdims=True), (REQUESTS, LANES))


    for away, distances in ((0, (4,)), (3, (3, 7)), (1, (5, 1)), (2, (6, 2))):
        wanted = lax.rem(first + away, CLASSES)
        span = pl.ds(pl.multiple_of(wanted * CHUNK, LANES), CHUNK)
        gate_part = jnp.dot(ffn, wgate[:, span], preferred_element_type=f32)
        up_part = jnp.dot(ffn, wup[:, span], preferred_element_type=f32)
        chunk = jnp.concatenate([gate_part, up_part, square], axis=1)
        chunk_out[away] = chunk.astype(bf16)
        if away == 0:
            chunk_sum[...] = chunk
        for d in distances:
            _, device = first_peer(d)
            pltpu.make_async_remote_copy(
                src_ref=chunk_out.at[away],
                dst_ref=chunk_in.at[d - 1],
                send_sem=send_sem.at[5],
                recv_sem=recv_sem.at[5],
                device_id=device,
                device_id_type=MESH,
            ).start()
    mine = lax.rem(first, CLASSES)
    total = chunk_sum[...]
    departed(4, proj_buf)
    arrive(5, chunk_in)
    for d in range(PEERS):
        total = total + chunk_in[d].astype(f32)
    piece_out[...] = total.astype(bf16)
    exchange(6, second_peer, lambda o: piece_out, lambda d: piece_in.at[d - 1])
    departed(5, chunk_in)
    arrive(6, piece_in)
    for d in range(PEERS):
        total = total + piece_in[d].astype(f32)
    inv_norm = lax.rsqrt(total[:, 2 * CHUNK : 2 * CHUNK + 1] / MODEL_WIDTH + epsilon)
    gate = total[:, :CHUNK] * inv_norm
    act = gate / (1.0 + jnp.exp(-gate)) * (total[:, CHUNK : 2 * CHUNK] * inv_norm)
    act_buf[mine] = act.astype(bf16)

    for k, d in enumerate((2, 1, SIDE - 1)):
        _, device = first_peer(d)
        pltpu.make_async_remote_copy(
            src_ref=act_buf.at[mine],
            dst_ref=act_buf.at[mine],
            send_sem=send_sem.at[7],
            recv_sem=act_sem.at[k],
            device_id=device,
            device_id_type=MESH,
        ).start()

    def down_of(owned):
        span = pl.ds(pl.multiple_of(owned * CHUNK, LANES), CHUNK)
        return jnp.dot(act_buf[owned], wdown[span, :], preferred_element_type=f32)

    part = down_of(mine)
    departed(6, piece_in)
    for k, d in ((1, 1), (2, SIDE - 1), (0, 2)):
        owned = lax.rem(first + SIDE - d, CLASSES)
        block = act_buf.at[owned]
        pltpu.make_async_copy(block, block, act_sem.at[k]).wait()
        part = part + down_of(owned)
    down_buf[head] = part
    exchange(8, head_peer, lambda o: down_buf.at[head], lambda d: down_buf.at[head])
    departed(7, act_buf, CLASSES - 1)
    arrive(8, down_buf)
    down = down_buf[0]
    for h in range(1, HEADS):
        down = down + down_buf[h]
    both_ref[...] = jnp.concatenate([after, after + down], axis=0).astype(bf16)
    departed(8, down_buf)


def on_device(
    hidden_state,
    attn_gain,
    query_key_value_weight,
    key_page_cache,
    value_page_cache,
    page_table,
    lengths,
    out_weight,
    ffn_gain,
    gate_weight,
    up_weight,
    down_weight,
):
    requests, width = hidden_state.shape
    arrays = (
        hidden_state,
        attn_gain.reshape(1, width),
        query_key_value_weight,
        key_page_cache,
        value_page_cache,
        page_table,
        out_weight,
        ffn_gain.reshape(1, width),
        gate_weight,
        up_weight,
        down_weight,
        lengths,
        jnp.asarray(rope_frequencies()),
    )
    hbm_spec = pl.BlockSpec(memory_space=pltpu.HBM)
    vmem_spec = pl.BlockSpec(memory_space=pltpu.VMEM)
    out = pltpu.VMEM((2 * requests, width), bf16)
    qkv_width, part_width = (GROUP + 3) * LANES, (GROUP + 1) * LANES
    both = pl.pallas_call(
        layer,
        out_shape=out,
        in_specs=[hbm_spec] * len(arrays),
        out_specs=vmem_spec,
        scratch_shapes=[
            pltpu.SMEM(a.shape, a.dtype) if a is lengths else pltpu.VMEM(a.shape, a.dtype) for a in arrays
        ]
        + [
            pltpu.SemaphoreType.DMA((len(arrays),)),
            pltpu.VMEM((requests, qkv_width), bf16),
            pltpu.VMEM((PEERS, requests, qkv_width), bf16),
            pltpu.VMEM((requests, qkv_width), bf16),
            pltpu.VMEM((PEERS, requests, qkv_width), bf16),
            pltpu.VMEM((8, SLOTS * PAGE_TOKENS), f32),
            pltpu.VMEM((HEAD_SIZE, SLOTS * PAGE_TOKENS), bf16),
            pltpu.VMEM((requests, part_width), bf16),
            pltpu.VMEM((PEERS, requests, part_width), bf16),
            pltpu.VMEM((requests, part_width), bf16),
            pltpu.VMEM((PEERS, requests, part_width), bf16),
            pltpu.VMEM((HEADS, REQUESTS, LANES), f32),
            pltpu.VMEM((REQUESTS, 2 * CHUNK + LANES), f32),
            pltpu.VMEM((CLASSES, REQUESTS, 2 * CHUNK + LANES), bf16),
            pltpu.VMEM((PEERS, REQUESTS, 2 * CHUNK + LANES), bf16),
            pltpu.VMEM((REQUESTS, 2 * CHUNK + LANES), bf16),
            pltpu.VMEM((PEERS, REQUESTS, 2 * CHUNK + LANES), bf16),
            pltpu.VMEM((CLASSES, REQUESTS, CHUNK), bf16),
            pltpu.VMEM((HEADS, REQUESTS, LANES), f32),
            pltpu.SemaphoreType.DMA((9,)),
            pltpu.SemaphoreType.DMA((9,)),
            pltpu.SemaphoreType.DMA((CLASSES - 1,)),
        ],
        compiler_params=pltpu.CompilerParams(
            collective_id=0, has_side_effects=True, vmem_limit_bytes=48 * 1024 * 1024
        ),
    )(*[pltpu.with_memory_space_constraint(a, pltpu.HBM) for a in arrays])
    return both[:requests], both[requests:]


def solution(mesh):
    in_specs = (
        P(None, "seq"),
        P("seq"),
        P("seq", "head"),
        P("seq", None, "head"),
        P("seq", None, "head"),
        P(),
        P(),
        P("head", "seq"),
        P("seq"),
        P("seq", "head"),
        P("seq", "head"),
        P("head", "seq"),
    )
    out_specs = (P(None, "seq"), P(None, "seq"))
    return jax.shard_map(
        on_device, mesh=mesh, in_specs=in_specs, out_specs=out_specs, check_vma=False
    )
```

```python
import functools
import math

import jax
import jax.numpy as jnp
import numpy as np
from jax import lax
from jax.experimental import pallas as pl
from jax.experimental.pallas import tpu as pltpu
from jax.sharding import PartitionSpec as P

MODEL_WIDTH = 8192
QUERY_HEADS = 64
KEY_VALUE_HEADS = 8
HEAD_SIZE = 128
PAGE_TOKENS = 128
REQUESTS = 4
GROUP = QUERY_HEADS // KEY_VALUE_HEADS
ROWS = GROUP * REQUESTS
SLOTS = 16
LANES = 128
SIDE = 8
HEADS = 8

epsilon = 1e-05
neg_fill = -1e30
MESH = pl.DeviceIdType.MESH
f32 = jnp.float32
bf16 = jnp.bfloat16

PEERS = 7
CLASSES = 4
CHUNK = 896

RING_ORDER = (4, 3, 5, 2, 6, 1, 7)


def rope_frequencies():
    index = np.arange(HEAD_SIZE // 2, dtype=np.float64)
    base = 500000.0 ** (-2.0 * index / HEAD_SIZE)
    ratio = 8192.0 * base / (2.0 * math.pi)
    smooth = np.clip((ratio - 1.0) / 3.0, 0.0, 1.0)
    frequency = (1.0 - smooth) * base / 8.0 + smooth * base
    return np.concatenate([frequency, frequency]).astype(np.float32)[None, :]


def layer(
    hidden_any,
    gain_any,
    wqkv_any,
    keys_any,
    values_any,
    table_any,
    wout_any,
    fgain_any,
    wgate_any,
    wup_any,
    wdown_any,
    len_any,
    freq_any,
    both_ref,
    hidden,
    gain,
    wqkv,
    keys,
    values,
    table,
    wout,
    fgain,
    wgate,
    wup,
    wdown,
    len_ref,
    freq_ref,
    load_sem,
    qkv_out1,
    qkv_in1,
    qkv_out2,
    qkv_in2,
    live_buf,
    keys_turned,
    part_out1,
    part_in1,
    part_out2,
    part_in2,
    proj_buf,
    chunk_sum,
    chunk_out,
    chunk_in,
    piece_out,
    piece_in,
    act_buf,
    down_buf,
    send_sem,
    recv_sem,
    act_sem,
):
    seq = lax.axis_index("seq")
    head = lax.axis_index("head")
    core = lax.rem(head, 2)
    row_y = seq // SIDE
    row_z = lax.rem(seq, SIDE)
    first = row_y + core * (row_z - row_y)
    second = row_z + core * (row_y - row_z)

    def seq_of(one, two):
        return one * (SIDE - (SIDE - 1) * core) + two * (1 + (SIDE - 1) * core)

    def first_peer(d):
        other = lax.rem(first + d, SIDE)
        return other, (seq_of(other, second), head)

    def second_peer(d):
        other = lax.rem(second + d, SIDE)
        return other, (seq_of(first, other), head)

    def head_peer(d):
        other = lax.rem(head + d, HEADS)
        return other, (seq, other)

    loads = {}

    def load(index, name, src, dst):
        loads[name] = pltpu.make_async_copy(src, dst, load_sem.at[index])
        loads[name].start()

    first_peers = {d: first_peer(d) for d in RING_ORDER}
    second_peers = {d: second_peer(d) for d in RING_ORDER}
    head_peers = {d: head_peer(d) for d in RING_ORDER}

    barrier = pltpu.get_barrier_semaphore()

    for d in RING_ORDER:
        pl.semaphore_signal(barrier, inc=1, device_id=first_peers[d][1], device_id_type=MESH)

    load(0, "hidden", hidden_any, hidden)
    load(1, "gain", gain_any, gain)
    load(2, "wqkv", wqkv_any, wqkv)
    load(3, "table", table_any, table)
    load(4, "lengths", len_any, len_ref)
    load(5, "freq", freq_any, freq_ref)

    for d in RING_ORDER:
        for peers in (second_peers, head_peers):
            pl.semaphore_signal(barrier, inc=1, device_id=peers[d][1], device_id_type=MESH)

    def exchange(step, peers, src_of, dst_of):
        for d in RING_ORDER:
            other, device = peers[d]
            pltpu.make_async_remote_copy(
                src_ref=src_of(other),
                dst_ref=dst_of(d),
                send_sem=send_sem.at[step],
                recv_sem=recv_sem.at[step],
                device_id=device,
                device_id_type=MESH,
            ).start()

    def arrive(step, blocks, count=PEERS):
        some = blocks.at[pl.ds(0, count)]
        pltpu.make_async_copy(some, some, recv_sem.at[step]).wait()

    def departed(step, blocks, count=PEERS):
        some = blocks.at[pl.ds(0, count)]
        pltpu.make_async_copy(some, some, send_sem.at[step]).wait()

    loads["hidden"].wait()
    loads["gain"].wait()
    stream = hidden[...].astype(f32)
    scaled = (stream * gain[...].astype(f32)).astype(bf16)
    square = jnp.broadcast_to(jnp.sum(stream * stream, axis=1, keepdims=True), (REQUESTS, LANES))
    loads["wqkv"].wait()
    part = jnp.dot(scaled, wqkv[...], preferred_element_type=f32)
    total = jnp.concatenate([part, square], axis=1)
    qkv_out1[...] = total.astype(bf16)

    pl.semaphore_wait(barrier, 21)
    exchange(0, first_peers, lambda o: qkv_out1, lambda d: qkv_in1.at[d - 1])

    load(6, "keys", keys_any, keys)
    load(7, "values", values_any, values)
    load(8, "wout", wout_any, wout)
    load(9, "fgain", fgain_any, fgain)
    load(10, "wgate", wgate_any, wgate)
    load(11, "wup", wup_any, wup)
    load(12, "wdown", wdown_any, wdown)

    sub = lax.broadcasted_iota(jnp.int32, (8, 1), 0)
    request = lax.rem(sub, REQUESTS)
    length = jnp.zeros((8, 1), jnp.int32)
    loads["lengths"].wait()
    for b in range(REQUESTS):
        length = jnp.where(request == b, len_ref[b], length)
    loads["table"].wait()
    pages = table[...]
    pages = jnp.concatenate([pages, pages], axis=0)
    page_count = pages.shape[1]
    page_index = lax.broadcasted_iota(jnp.int32, (8, page_count), 1)
    lane = lax.broadcasted_iota(jnp.int32, (8, LANES), 1)
    for j in range(SLOTS):
        hit = jnp.sum(
            jnp.where(pages == seq * SLOTS + j, (page_index + 1).astype(f32), 0.0), axis=1, keepdims=True
        ).astype(jnp.int32)
        limit = jnp.where(hit > 0, length - (hit - 1) * PAGE_TOKENS, 0)
        live_buf[:, j * LANES : (j + 1) * LANES] = jnp.where(lane < limit, 1.0, 0.0)
    mine_page = (page_index == length // PAGE_TOKENS) & (pages >= seq * SLOTS) & (pages < (seq + 1) * SLOTS)
    mine = jnp.sum(jnp.where(mine_page, 1.0, 0.0), axis=1, keepdims=True) > 0.5
    loads["freq"].wait()
    angle = length.astype(f32) * freq_ref[...]
    cos_part = jnp.cos(angle)
    sine_part = jnp.sin(angle)
    sine_part = jnp.where(lane < HEAD_SIZE // 2, -sine_part, sine_part)

    arrive(0, qkv_in1)
    for d in range(7):
        total = total + qkv_in1[d].astype(f32)
    qkv_out2[...] = total.astype(bf16)
    exchange(1, second_peers, lambda o: qkv_out2, lambda d: qkv_in2.at[d - 1])
    loads["keys"].wait()

    @pl.loop(0, SLOTS // 4)
    def turn(step):
        for k in range(4):
            j = step * 4 + k
            span = pl.ds(pl.multiple_of(j * PAGE_TOKENS, PAGE_TOKENS), PAGE_TOKENS)
            keys_turned[:, span] = keys[j].T

    loads["values"].wait()
    arrive(1, qkv_in2)
    for d in range(7):
        total = total + qkv_in2[d].astype(f32)

    inv_rms = lax.rsqrt(total[:, (GROUP + 2) * LANES :] / MODEL_WIDTH + epsilon)
    joined = jnp.concatenate(
        [total[:, t * LANES : (t + 1) * LANES] * inv_rms for t in range(GROUP + 2)], axis=0
    ).reshape(5, 8, LANES)
    swapped = pltpu.roll(joined.reshape(40, LANES), HEAD_SIZE // 2, 1).reshape(5, 8, LANES)
    turned = joined * cos_part + swapped * sine_part
    queries = turned[0:4].reshape(ROWS, LANES).astype(bf16)
    new_key = turned[4][0:4].astype(bf16).astype(f32)
    new_key = jnp.concatenate([new_key, new_key], axis=0)
    new_value = joined[4][4:8].astype(bf16).astype(f32)
    new_value = jnp.concatenate([new_value, new_value], axis=0)

    scale = 1.0 / math.sqrt(HEAD_SIZE)
    tokens = SLOTS * PAGE_TOKENS
    scores = jnp.dot(queries, keys_turned[...], preferred_element_type=f32)
    live = live_buf[...] > 0.5
    masked = jnp.where(live, scores.reshape(4, 8, tokens) * scale, neg_fill)
    new_score = (
        jnp.sum(queries.astype(f32).reshape(4, 8, LANES) * new_key, axis=2, keepdims=True) * scale
    )
    peak = jnp.maximum(
        jnp.max(masked, axis=2, keepdims=True), jnp.where(mine, new_score, neg_fill)
    )
    weight = jnp.where(live, jnp.exp(masked - peak), 0.0)
    new_weight = jnp.where(mine, jnp.exp(new_score - peak), 0.0)
    denom = jnp.sum(weight, axis=2, keepdims=True) + new_weight
    accum = jnp.dot(
        weight.reshape(ROWS, tokens).astype(bf16),
        values[...].reshape(tokens, HEAD_SIZE),
        preferred_element_type=f32,
    ).reshape(4, 8, LANES)
    accum = accum + new_weight.astype(bf16).astype(f32) * new_value
    some = denom > 0.0
    safe = jnp.where(some, denom, 1.0)
    mean = (accum / safe).reshape(ROWS, LANES)
    lse = jnp.where(some, peak + jnp.log(safe), neg_fill).reshape(ROWS, 1)

    tiles = [slice(g * REQUESTS, (g + 1) * REQUESTS) for g in range(GROUP)]
    means = [mean[rows] for rows in tiles]
    column = lax.broadcasted_iota(jnp.int32, (REQUESTS, LANES), 1)
    stats = jnp.zeros((REQUESTS, LANES), f32)
    for g, rows in enumerate(tiles):
        stats = jnp.where(column == g, lse[rows], stats)

    def packed(means, stats):
        high = stats.astype(bf16).astype(f32)
        rest = stats - high
        middle = rest.astype(bf16).astype(f32)
        low = rest - middle
        side = high + pltpu.roll(middle, GROUP, 1) + pltpu.roll(low, 2 * GROUP, 1)
        return jnp.concatenate(means + [side], axis=1).astype(bf16)

    def merged(means, stats, arrived):
        blocks = [means]
        lses = [stats]
        for d in range(PEERS):
            block = arrived[d].astype(f32)
            blocks.append([block[:, g * LANES : (g + 1) * LANES] for g in range(GROUP)])
            side = block[:, GROUP * LANES :]
            side = side + pltpu.roll(side, LANES - GROUP, 1) + pltpu.roll(side, LANES - 2 * GROUP, 1)
            lses.append(jnp.where(column < GROUP, side, 0.0))
        best = functools.reduce(jnp.maximum, lses)
        factors = [jnp.exp(part - best) for part in lses]
        whole = functools.reduce(jnp.add, factors)
        factors = [factor / whole for factor in factors]
        means = [
            functools.reduce(
                jnp.add, [factor[:, g : g + 1] * block[g] for factor, block in zip(factors, blocks)]
            )
            for g in range(GROUP)
        ]
        return means, jnp.where(column < GROUP, best + jnp.log(whole), 0.0)

    part_out1[...] = packed(means, stats)
    exchange(2, first_peers, lambda o: part_out1, lambda d: part_in1.at[d - 1])
    loads["wout"].wait()
    loads["fgain"].wait()
    arrive(2, part_in1)
    means, stats = merged(means, stats, part_in1)
    part_out2[...] = packed(means, stats)
    exchange(3, second_peers, lambda o: part_out2, lambda d: part_in2.at[d - 1])
    loads["wgate"].wait()
    loads["wup"].wait()
    loads["wdown"].wait()
    arrive(3, part_in2)
    means, _ = merged(means, stats, part_in2)

    attention = jnp.concatenate(means, axis=1).astype(bf16)
    proj_buf[head] = jnp.dot(attention, wout[...], preferred_element_type=f32)
    exchange(4, head_peers, lambda o: proj_buf.at[head], lambda d: proj_buf.at[head])
    arrive(4, proj_buf)
    projected = proj_buf[0]
    for h in range(1, HEADS):
        projected = projected + proj_buf[h]
    attended = (stream + projected).astype(bf16)
    after = attended.astype(f32)
    ffn = (after * fgain[...].astype(f32)).astype(bf16)
    square = jnp.broadcast_to(jnp.sum(after * after, axis=1, keepdims=True), (REQUESTS, LANES))


    for away, distances in ((0, (4,)), (3, (3, 7)), (1, (5, 1)), (2, (6, 2))):
        wanted = lax.rem(first + away, CLASSES)
        span = pl.ds(pl.multiple_of(wanted * CHUNK, LANES), CHUNK)
        gate_part = jnp.dot(ffn, wgate[:, span], preferred_element_type=f32)
        up_part = jnp.dot(ffn, wup[:, span], preferred_element_type=f32)
        chunk = jnp.concatenate([gate_part, up_part, square], axis=1)
        chunk_out[away] = chunk.astype(bf16)
        if away == 0:
            chunk_sum[...] = chunk
        for d in distances:
            _, device = first_peers[d]
            pltpu.make_async_remote_copy(
                src_ref=chunk_out.at[away],
                dst_ref=chunk_in.at[d - 1],
                send_sem=send_sem.at[5],
                recv_sem=recv_sem.at[5],
                device_id=device,
                device_id_type=MESH,
            ).start()
    mine = lax.rem(first, CLASSES)
    total = chunk_sum[...]
    arrive(5, chunk_in)
    for d in range(PEERS):
        total = total + chunk_in[d].astype(f32)
    piece_out[...] = total.astype(bf16)
    exchange(6, second_peers, lambda o: piece_out, lambda d: piece_in.at[d - 1])
    arrive(6, piece_in)
    for d in range(PEERS):
        total = total + piece_in[d].astype(f32)
    inv_norm = lax.rsqrt(total[:, 2 * CHUNK : 2 * CHUNK + 1] / MODEL_WIDTH + epsilon)
    gate = total[:, :CHUNK] * inv_norm
    act = gate / (1.0 + jnp.exp(-gate)) * (total[:, CHUNK : 2 * CHUNK] * inv_norm)
    act_buf[mine] = act.astype(bf16)

    for k, d in enumerate((2, 1, SIDE - 1)):
        _, device = first_peers[d]
        pltpu.make_async_remote_copy(
            src_ref=act_buf.at[mine],
            dst_ref=act_buf.at[mine],
            send_sem=send_sem.at[7],
            recv_sem=act_sem.at[k],
            device_id=device,
            device_id_type=MESH,
        ).start()

    def down_of(owned):
        span = pl.ds(pl.multiple_of(owned * CHUNK, LANES), CHUNK)
        return jnp.dot(act_buf[owned], wdown[span, :], preferred_element_type=f32)

    part = down_of(mine)
    for k, d in ((1, 1), (2, SIDE - 1), (0, 2)):
        owned = lax.rem(first + SIDE - d, CLASSES)
        block = act_buf.at[owned]
        pltpu.make_async_copy(block, block, act_sem.at[k]).wait()
        part = part + down_of(owned)
    down_buf[head] = part
    exchange(8, head_peers, lambda o: down_buf.at[head], lambda d: down_buf.at[head])
    arrive(8, down_buf)
    down = down_buf[0]
    for h in range(1, HEADS):
        down = down + down_buf[h]
    both_ref[...] = jnp.concatenate([after, after + down], axis=0).astype(bf16)
    departed(0, qkv_in1)
    departed(1, qkv_in2)
    departed(2, part_in1)
    departed(3, part_in2)
    departed(4, proj_buf)
    departed(5, chunk_in)
    departed(6, piece_in)
    departed(7, act_buf, CLASSES - 1)
    departed(8, down_buf)


def on_device(
    hidden_state,
    attn_gain,
    query_key_value_weight,
    key_page_cache,
    value_page_cache,
    page_table,
    lengths,
    out_weight,
    ffn_gain,
    gate_weight,
    up_weight,
    down_weight,
):
    requests, width = hidden_state.shape
    arrays = (
        hidden_state,
        attn_gain.reshape(1, width),
        query_key_value_weight,
        key_page_cache,
        value_page_cache,
        page_table,
        out_weight,
        ffn_gain.reshape(1, width),
        gate_weight,
        up_weight,
        down_weight,
        lengths,
        jnp.asarray(rope_frequencies()),
    )
    hbm_spec = pl.BlockSpec(memory_space=pltpu.HBM)
    vmem_spec = pl.BlockSpec(memory_space=pltpu.VMEM)
    out = pltpu.VMEM((2 * requests, width), bf16)
    qkv_width, part_width = (GROUP + 3) * LANES, (GROUP + 1) * LANES
    both = pl.pallas_call(
        layer,
        out_shape=out,
        in_specs=[hbm_spec] * len(arrays),
        out_specs=vmem_spec,
        scratch_shapes=[
            pltpu.SMEM(a.shape, a.dtype) if a is lengths else pltpu.VMEM(a.shape, a.dtype) for a in arrays
        ]
        + [
            pltpu.SemaphoreType.DMA((len(arrays),)),
            pltpu.VMEM((requests, qkv_width), bf16),
            pltpu.VMEM((PEERS, requests, qkv_width), bf16),
            pltpu.VMEM((requests, qkv_width), bf16),
            pltpu.VMEM((PEERS, requests, qkv_width), bf16),
            pltpu.VMEM((8, SLOTS * PAGE_TOKENS), f32),
            pltpu.VMEM((HEAD_SIZE, SLOTS * PAGE_TOKENS), bf16),
            pltpu.VMEM((requests, part_width), bf16),
            pltpu.VMEM((PEERS, requests, part_width), bf16),
            pltpu.VMEM((requests, part_width), bf16),
            pltpu.VMEM((PEERS, requests, part_width), bf16),
            pltpu.VMEM((HEADS, REQUESTS, LANES), f32),
            pltpu.VMEM((REQUESTS, 2 * CHUNK + LANES), f32),
            pltpu.VMEM((CLASSES, REQUESTS, 2 * CHUNK + LANES), bf16),
            pltpu.VMEM((PEERS, REQUESTS, 2 * CHUNK + LANES), bf16),
            pltpu.VMEM((REQUESTS, 2 * CHUNK + LANES), bf16),
            pltpu.VMEM((PEERS, REQUESTS, 2 * CHUNK + LANES), bf16),
            pltpu.VMEM((CLASSES, REQUESTS, CHUNK), bf16),
            pltpu.VMEM((HEADS, REQUESTS, LANES), f32),
            pltpu.SemaphoreType.DMA((9,)),
            pltpu.SemaphoreType.DMA((9,)),
            pltpu.SemaphoreType.DMA((CLASSES - 1,)),
        ],
        compiler_params=pltpu.CompilerParams(
            collective_id=0, has_side_effects=True, vmem_limit_bytes=48 * 1024 * 1024
        ),
    )(*[pltpu.with_memory_space_constraint(a, pltpu.HBM) for a in arrays])
    return both[:requests], both[requests:]


def solution(mesh):
    in_specs = (
        P(None, "seq"),
        P("seq"),
        P("seq", "head"),
        P("seq", None, "head"),
        P("seq", None, "head"),
        P(),
        P(),
        P("head", "seq"),
        P("seq"),
        P("seq", "head"),
        P("seq", "head"),
        P("head", "seq"),
    )
    out_specs = (P(None, "seq"), P(None, "seq"))
    return jax.shard_map(
        on_device, mesh=mesh, in_specs=in_specs, out_specs=out_specs, check_vma=False
    )
```

```python
import functools
import math

import jax
import jax.numpy as jnp
import numpy as np
from jax import lax
from jax.experimental import pallas as pl
from jax.experimental.pallas import tpu as pltpu
from jax.sharding import PartitionSpec as P

MODEL_WIDTH = 8192
QUERY_HEADS = 64
KEY_VALUE_HEADS = 8
HEAD_SIZE = 128
PAGE_TOKENS = 128
REQUESTS = 4
GROUP = QUERY_HEADS // KEY_VALUE_HEADS
ROWS = GROUP * REQUESTS
SLOTS = 16
LANES = 128
SIDE = 8
HEADS = 8

epsilon = 1e-05
neg_fill = -1e30
MESH = pl.DeviceIdType.MESH
f32 = jnp.float32
bf16 = jnp.bfloat16

PEERS = 7
OWNERS = 14
CHUNK = 256
DEVICES = 64


def near_half():
    chosen = []
    for dy in range(SIDE):
        for dz in range(SIDE):
            hops = min(dy, SIDE - dy) + min(dz, SIDE - dz)
            if hops < 4 or (hops == 4 and dy < 4):
                chosen.append((-hops, dy, dz))
    return [(dy, dz) for hops, dy, dz in sorted(chosen) if hops]


NEAR = near_half()


def ring_distance(i):
    return 4 + ((i + 1) // 2) * (1 - 2 * lax.rem(i, 2))


def rope_frequencies():
    index = np.arange(HEAD_SIZE // 2, dtype=np.float64)
    base = 500000.0 ** (-2.0 * index / HEAD_SIZE)
    ratio = 8192.0 * base / (2.0 * math.pi)
    smooth = np.clip((ratio - 1.0) / 3.0, 0.0, 1.0)
    frequency = (1.0 - smooth) * base / 8.0 + smooth * base
    return np.concatenate([frequency, frequency]).astype(np.float32)[None, :]


def layer(
    hidden_any,
    gain_any,
    wqkv_any,
    keys_any,
    values_any,
    table_any,
    wout_any,
    fgain_any,
    wgate_any,
    wup_any,
    wdown_any,
    len_any,
    freq_any,
    both_ref,
    hidden,
    gain,
    wqkv,
    keys,
    values,
    table,
    wout,
    fgain,
    wgate,
    wup,
    wdown,
    len_ref,
    freq_ref,
    load_sem,
    qkv_out1,
    qkv_in1,
    qkv_out2,
    qkv_in2,
    live_buf,
    keys_turned,
    part_out1,
    part_in1,
    part_out2,
    part_in2,
    proj_buf,
    chunk_sum,
    chunk_out,
    chunk_in,
    act_buf,
    down_buf,
    send_sem,
    recv_sem,
):
    seq = lax.axis_index("seq")
    head = lax.axis_index("head")
    core = lax.rem(head, 2)
    row_y = seq // SIDE
    row_z = lax.rem(seq, SIDE)
    first = row_y + core * (row_z - row_y)
    second = row_z + core * (row_y - row_z)

    def seq_of(one, two):
        return one * (SIDE - (SIDE - 1) * core) + two * (1 + (SIDE - 1) * core)

    def first_peer(d):
        other = lax.rem(first + d, SIDE)
        return other, (seq_of(other, second), head)

    def second_peer(d):
        other = lax.rem(second + d, SIDE)
        return other, (seq_of(first, other), head)

    def head_peer(d):
        other = lax.rem(head + d, HEADS)
        return other, (seq, other)

    loads = {}

    def load(index, name, src, dst):
        loads[name] = pltpu.make_async_copy(src, dst, load_sem.at[index])
        loads[name].start()

    barrier = pltpu.get_barrier_semaphore()

    @pl.loop(0, PEERS)
    def announce(i):
        pl.semaphore_signal(barrier, inc=1, device_id=first_peer(ring_distance(i))[1], device_id_type=MESH)

    load(0, "hidden", hidden_any, hidden)
    load(1, "gain", gain_any, gain)
    load(2, "wqkv", wqkv_any, wqkv)
    load(3, "table", table_any, table)
    load(4, "lengths", len_any, len_ref)
    load(5, "freq", freq_any, freq_ref)

    @pl.loop(0, PEERS)
    def announce_more(i):
        for peer in (second_peer, head_peer):
            pl.semaphore_signal(barrier, inc=1, device_id=peer(ring_distance(i))[1], device_id_type=MESH)

    def exchange(step, peer, src_of, dst_of):
        @pl.loop(0, PEERS)
        def send(i):
            d = ring_distance(i)
            other, device = peer(d)
            pltpu.make_async_remote_copy(
                src_ref=src_of(other),
                dst_ref=dst_of(d),
                send_sem=send_sem.at[step],
                recv_sem=recv_sem.at[step],
                device_id=device,
                device_id_type=MESH,
            ).start()

    def arrive(step, blocks, count=PEERS):
        some = blocks.at[pl.ds(0, count)]
        pltpu.make_async_copy(some, some, recv_sem.at[step]).wait()

    def departed(step, blocks, count=PEERS):
        some = blocks.at[pl.ds(0, count)]
        pltpu.make_async_copy(some, some, send_sem.at[step]).wait()

    loads["hidden"].wait()
    loads["gain"].wait()
    stream = hidden[...].astype(f32)
    scaled = (stream * gain[...].astype(f32)).astype(bf16)
    square = jnp.broadcast_to(jnp.sum(stream * stream, axis=1, keepdims=True), (REQUESTS, LANES))
    loads["wqkv"].wait()
    part = jnp.dot(scaled, wqkv[...], preferred_element_type=f32)
    total = jnp.concatenate([part, square], axis=1)
    qkv_out1[...] = total.astype(bf16)

    pl.semaphore_wait(barrier, 21)
    exchange(0, first_peer, lambda o: qkv_out1, lambda d: qkv_in1.at[d - 1])

    load(6, "keys", keys_any, keys)
    load(7, "values", values_any, values)
    load(8, "wout", wout_any, wout)
    load(9, "fgain", fgain_any, fgain)
    load(10, "wgate", wgate_any, wgate)
    load(11, "wup", wup_any, wup)
    load(12, "wdown", wdown_any, wdown)

    sub = lax.broadcasted_iota(jnp.int32, (8, 1), 0)
    request = lax.rem(sub, REQUESTS)
    length = jnp.zeros((8, 1), jnp.int32)
    loads["lengths"].wait()
    for b in range(REQUESTS):
        length = jnp.where(request == b, len_ref[b], length)
    loads["table"].wait()
    pages = table[...]
    pages = jnp.concatenate([pages, pages], axis=0)
    page_count = pages.shape[1]
    page_index = lax.broadcasted_iota(jnp.int32, (8, page_count), 1)
    lane = lax.broadcasted_iota(jnp.int32, (8, LANES), 1)
    for j in range(SLOTS):
        hit = jnp.sum(
            jnp.where(pages == seq * SLOTS + j, (page_index + 1).astype(f32), 0.0), axis=1, keepdims=True
        ).astype(jnp.int32)
        limit = jnp.where(hit > 0, length - (hit - 1) * PAGE_TOKENS, 0)
        live_buf[:, j * LANES : (j + 1) * LANES] = jnp.where(lane < limit, 1.0, 0.0)
    mine_page = (page_index == length // PAGE_TOKENS) & (pages >= seq * SLOTS) & (pages < (seq + 1) * SLOTS)
    mine = jnp.sum(jnp.where(mine_page, 1.0, 0.0), axis=1, keepdims=True) > 0.5
    loads["freq"].wait()
    angle = length.astype(f32) * freq_ref[...]
    cos_part = jnp.cos(angle)
    sine_part = jnp.sin(angle)
    sine_part = jnp.where(lane < HEAD_SIZE // 2, -sine_part, sine_part)

    arrive(0, qkv_in1)
    for d in range(7):
        total = total + qkv_in1[d].astype(f32)
    qkv_out2[...] = total.astype(bf16)
    exchange(1, second_peer, lambda o: qkv_out2, lambda d: qkv_in2.at[d - 1])
    loads["keys"].wait()

    @pl.loop(0, SLOTS // 4)
    def turn(step):
        for k in range(4):
            j = step * 4 + k
            span = pl.ds(pl.multiple_of(j * PAGE_TOKENS, PAGE_TOKENS), PAGE_TOKENS)
            keys_turned[:, span] = keys[j].T

    loads["values"].wait()
    departed(0, qkv_in1)
    arrive(1, qkv_in2)
    for d in range(7):
        total = total + qkv_in2[d].astype(f32)

    inv_rms = lax.rsqrt(total[:, (GROUP + 2) * LANES :] / MODEL_WIDTH + epsilon)
    joined = jnp.concatenate(
        [total[:, t * LANES : (t + 1) * LANES] * inv_rms for t in range(GROUP + 2)], axis=0
    ).reshape(5, 8, LANES)
    swapped = pltpu.roll(joined.reshape(40, LANES), HEAD_SIZE // 2, 1).reshape(5, 8, LANES)
    turned = joined * cos_part + swapped * sine_part
    queries = turned[0:4].reshape(ROWS, LANES).astype(bf16)
    new_key = turned[4][0:4].astype(bf16).astype(f32)
    new_key = jnp.concatenate([new_key, new_key], axis=0)
    new_value = joined[4][4:8].astype(bf16).astype(f32)
    new_value = jnp.concatenate([new_value, new_value], axis=0)

    scale = 1.0 / math.sqrt(HEAD_SIZE)
    tokens = SLOTS * PAGE_TOKENS
    scores = jnp.dot(queries, keys_turned[...], preferred_element_type=f32)
    live = live_buf[...] > 0.5
    masked = jnp.where(live, scores.reshape(4, 8, tokens) * scale, neg_fill)
    new_score = (
        jnp.sum(queries.astype(f32).reshape(4, 8, LANES) * new_key, axis=2, keepdims=True) * scale
    )
    peak = jnp.maximum(
        jnp.max(masked, axis=2, keepdims=True), jnp.where(mine, new_score, neg_fill)
    )
    weight = jnp.where(live, jnp.exp(masked - peak), 0.0)
    new_weight = jnp.where(mine, jnp.exp(new_score - peak), 0.0)
    denom = jnp.sum(weight, axis=2, keepdims=True) + new_weight
    accum = jnp.dot(
        weight.reshape(ROWS, tokens).astype(bf16),
        values[...].reshape(tokens, HEAD_SIZE),
        preferred_element_type=f32,
    ).reshape(4, 8, LANES)
    accum = accum + new_weight.astype(bf16).astype(f32) * new_value
    some = denom > 0.0
    safe = jnp.where(some, denom, 1.0)
    mean = (accum / safe).reshape(ROWS, LANES)
    lse = jnp.where(some, peak + jnp.log(safe), neg_fill).reshape(ROWS, 1)

    tiles = [slice(g * REQUESTS, (g + 1) * REQUESTS) for g in range(GROUP)]
    means = [mean[rows] for rows in tiles]
    column = lax.broadcasted_iota(jnp.int32, (REQUESTS, LANES), 1)
    stats = jnp.zeros((REQUESTS, LANES), f32)
    for g, rows in enumerate(tiles):
        stats = jnp.where(column == g, lse[rows], stats)

    def packed(means, stats):
        high = stats.astype(bf16).astype(f32)
        rest = stats - high
        middle = rest.astype(bf16).astype(f32)
        low = rest - middle
        side = high + pltpu.roll(middle, GROUP, 1) + pltpu.roll(low, 2 * GROUP, 1)
        return jnp.concatenate(means + [side], axis=1).astype(bf16)

    def merged(means, stats, arrived):
        blocks = [means]
        lses = [stats]
        for d in range(PEERS):
            block = arrived[d].astype(f32)
            blocks.append([block[:, g * LANES : (g + 1) * LANES] for g in range(GROUP)])
            side = block[:, GROUP * LANES :]
            side = side + pltpu.roll(side, LANES - GROUP, 1) + pltpu.roll(side, LANES - 2 * GROUP, 1)
            lses.append(jnp.where(column < GROUP, side, 0.0))
        best = functools.reduce(jnp.maximum, lses)
        factors = [jnp.exp(part - best) for part in lses]
        whole = functools.reduce(jnp.add, factors)
        factors = [factor / whole for factor in factors]
        means = [
            functools.reduce(
                jnp.add, [factor[:, g : g + 1] * block[g] for factor, block in zip(factors, blocks)]
            )
            for g in range(GROUP)
        ]
        return means, jnp.where(column < GROUP, best + jnp.log(whole), 0.0)

    part_out1[...] = packed(means, stats)
    exchange(2, first_peer, lambda o: part_out1, lambda d: part_in1.at[d - 1])
    loads["wout"].wait()
    loads["fgain"].wait()
    departed(1, qkv_in2)
    arrive(2, part_in1)
    means, stats = merged(means, stats, part_in1)
    part_out2[...] = packed(means, stats)
    exchange(3, second_peer, lambda o: part_out2, lambda d: part_in2.at[d - 1])
    loads["wgate"].wait()
    loads["wup"].wait()
    loads["wdown"].wait()
    departed(2, part_in1)
    arrive(3, part_in2)
    means, _ = merged(means, stats, part_in2)

    attention = jnp.concatenate(means, axis=1).astype(bf16)
    proj_buf[head] = jnp.dot(attention, wout[...], preferred_element_type=f32)
    exchange(4, head_peer, lambda o: proj_buf.at[head], lambda d: proj_buf.at[head])
    departed(3, part_in2)
    arrive(4, proj_buf)
    projected = proj_buf[0]
    for h in range(1, HEADS):
        projected = projected + proj_buf[h]
    attended = (stream + projected).astype(bf16)
    after = attended.astype(f32)
    ffn = (after * fgain[...].astype(f32)).astype(bf16)
    square = jnp.broadcast_to(jnp.sum(after * after, axis=1, keepdims=True), (REQUESTS, LANES))

    gate_part = jnp.dot(ffn, wgate[...], preferred_element_type=f32)
    up_part = jnp.dot(ffn, wup[...], preferred_element_type=f32)
    for p in range(OWNERS):
        span = slice(p * CHUNK, (p + 1) * CHUNK)
        chunk_out[p] = jnp.concatenate([gate_part[:, span], up_part[:, span], square], axis=1).astype(bf16)

    place = lax.rem(row_y, 4) * SIDE + lax.rem(row_z + 4 * (row_y // 4), SIDE)
    mine_p = place // 2
    owns = (lax.rem(place, 2) == core) & (mine_p < OWNERS)

    @pl.loop(0, 2 * OWNERS)
    def send_chunk(i):
        again = lax.rem(i, 2)
        p = lax.rem(mine_p + OWNERS // 2 + i // 2, OWNERS)
        spot = 2 * p + core
        owner = (spot // SIDE + 4 * again) * SIDE + lax.rem(spot + 4 * again, SIDE)

        @pl.when(owner != seq)
        def start():
            pltpu.make_async_remote_copy(
                src_ref=chunk_out.at[p],
                dst_ref=chunk_in.at[seq],
                send_sem=send_sem.at[5],
                recv_sem=recv_sem.at[5],
                device_id=(owner, head),
                device_id_type=MESH,
            ).start()

    departed(4, proj_buf)

    @pl.when(owns)
    def own_chunk():
        chunk_in[seq] = chunk_out[mine_p]
        chunk_sum[...] = jnp.zeros((REQUESTS, 2 * CHUNK + LANES), f32)
        arrive(5, chunk_in, DEVICES - 1)

        @pl.loop(0, DEVICES // 8)
        def add(i):
            total = chunk_sum[...]
            for k in range(8):
                total = total + chunk_in[i * 8 + k].astype(f32)
            chunk_sum[...] = total

        total = chunk_sum[...]
        inv_norm = lax.rsqrt(total[:, 2 * CHUNK : 2 * CHUNK + 1] / MODEL_WIDTH + epsilon)
        gate = total[:, :CHUNK] * inv_norm
        act = gate / (1.0 + jnp.exp(-gate)) * (total[:, CHUNK : 2 * CHUNK] * inv_norm)
        act_buf[mine_p] = act.astype(bf16)
        for dy, dz in NEAR:
            other = lax.rem(row_y + dy, SIDE) * SIDE + lax.rem(row_z + dz, SIDE)
            pltpu.make_async_remote_copy(
                src_ref=act_buf.at[mine_p],
                dst_ref=act_buf.at[mine_p],
                send_sem=send_sem.at[6],
                recv_sem=recv_sem.at[6],
                device_id=(other, head),
                device_id_type=MESH,
            ).start()
        departed(5, chunk_in, 2 * OWNERS - 1)
        arrive(6, act_buf, OWNERS - 1)

    @pl.when(jnp.logical_not(owns))
    def no_chunk():
        departed(5, chunk_in, 2 * OWNERS)
        arrive(6, act_buf, OWNERS)

    units = jnp.concatenate([act_buf[p] for p in range(OWNERS)], axis=1)
    down_buf[head] = jnp.dot(units, wdown[...], preferred_element_type=f32)
    exchange(7, head_peer, lambda o: down_buf.at[head], lambda d: down_buf.at[head])

    @pl.when(owns)
    def act_sent():
        departed(6, act_buf, len(NEAR))

    arrive(7, down_buf)
    down = down_buf[0]
    for h in range(1, HEADS):
        down = down + down_buf[h]
    both_ref[...] = jnp.concatenate([after, after + down], axis=0).astype(bf16)
    departed(7, down_buf)


def on_device(
    hidden_state,
    attn_gain,
    query_key_value_weight,
    key_page_cache,
    value_page_cache,
    page_table,
    lengths,
    out_weight,
    ffn_gain,
    gate_weight,
    up_weight,
    down_weight,
):
    requests, width = hidden_state.shape
    arrays = (
        hidden_state,
        attn_gain.reshape(1, width),
        query_key_value_weight,
        key_page_cache,
        value_page_cache,
        page_table,
        out_weight,
        ffn_gain.reshape(1, width),
        gate_weight,
        up_weight,
        down_weight,
        lengths,
        jnp.asarray(rope_frequencies()),
    )
    hbm_spec = pl.BlockSpec(memory_space=pltpu.HBM)
    vmem_spec = pl.BlockSpec(memory_space=pltpu.VMEM)
    out = pltpu.VMEM((2 * requests, width), bf16)
    qkv_width, part_width = (GROUP + 3) * LANES, (GROUP + 1) * LANES
    both = pl.pallas_call(
        layer,
        out_shape=out,
        in_specs=[hbm_spec] * len(arrays),
        out_specs=vmem_spec,
        scratch_shapes=[
            pltpu.SMEM(a.shape, a.dtype) if a is lengths else pltpu.VMEM(a.shape, a.dtype) for a in arrays
        ]
        + [
            pltpu.SemaphoreType.DMA((len(arrays),)),
            pltpu.VMEM((requests, qkv_width), bf16),
            pltpu.VMEM((PEERS, requests, qkv_width), bf16),
            pltpu.VMEM((requests, qkv_width), bf16),
            pltpu.VMEM((PEERS, requests, qkv_width), bf16),
            pltpu.VMEM((8, SLOTS * PAGE_TOKENS), f32),
            pltpu.VMEM((HEAD_SIZE, SLOTS * PAGE_TOKENS), bf16),
            pltpu.VMEM((requests, part_width), bf16),
            pltpu.VMEM((PEERS, requests, part_width), bf16),
            pltpu.VMEM((requests, part_width), bf16),
            pltpu.VMEM((PEERS, requests, part_width), bf16),
            pltpu.VMEM((HEADS, REQUESTS, LANES), f32),
            pltpu.VMEM((REQUESTS, 2 * CHUNK + LANES), f32),
            pltpu.VMEM((OWNERS, REQUESTS, 2 * CHUNK + LANES), bf16),
            pltpu.VMEM((DEVICES, REQUESTS, 2 * CHUNK + LANES), bf16),
            pltpu.VMEM((DEVICES // 2, REQUESTS, CHUNK), bf16),
            pltpu.VMEM((HEADS, REQUESTS, LANES), f32),
            pltpu.SemaphoreType.DMA((9,)),
            pltpu.SemaphoreType.DMA((9,)),
        ],
        compiler_params=pltpu.CompilerParams(
            collective_id=0, has_side_effects=True, vmem_limit_bytes=48 * 1024 * 1024
        ),
    )(*[pltpu.with_memory_space_constraint(a, pltpu.HBM) for a in arrays])
    return both[:requests], both[requests:]


def solution(mesh):
    in_specs = (
        P(None, "seq"),
        P("seq"),
        P("seq", "head"),
        P("seq", None, "head"),
        P("seq", None, "head"),
        P(),
        P(),
        P("head", "seq"),
        P("seq"),
        P("seq", "head"),
        P("seq", "head"),
        P("head", "seq"),
    )
    out_specs = (P(None, "seq"), P(None, "seq"))
    return jax.shard_map(
        on_device, mesh=mesh, in_specs=in_specs, out_specs=out_specs, check_vma=False
    )
```

```python
import functools
import math

import jax
import jax.numpy as jnp
import numpy as np
from jax import lax
from jax.experimental import pallas as pl
from jax.experimental.pallas import tpu as pltpu
from jax.sharding import PartitionSpec as P

MODEL_WIDTH = 8192
QUERY_HEADS = 64
KEY_VALUE_HEADS = 8
HEAD_SIZE = 128
PAGE_TOKENS = 128
REQUESTS = 4
GROUP = QUERY_HEADS // KEY_VALUE_HEADS
ROWS = GROUP * REQUESTS
SLOTS = 16
LANES = 128
SIDE = 8
HEADS = 8

epsilon = 1e-05
neg_fill = -1e30
MESH = pl.DeviceIdType.MESH
f32 = jnp.float32
bf16 = jnp.bfloat16

PEERS = 7
CLASSES = 4
CHUNK = 896


def ring_distance(i):
    return 4 + ((i + 1) // 2) * (1 - 2 * lax.rem(i, 2))


def rope_frequencies():
    index = np.arange(HEAD_SIZE // 2, dtype=np.float64)
    base = 500000.0 ** (-2.0 * index / HEAD_SIZE)
    ratio = 8192.0 * base / (2.0 * math.pi)
    smooth = np.clip((ratio - 1.0) / 3.0, 0.0, 1.0)
    frequency = (1.0 - smooth) * base / 8.0 + smooth * base
    return np.concatenate([frequency, frequency]).astype(np.float32)[None, :]


def layer(
    hidden_any,
    gain_any,
    wqkv_any,
    keys_any,
    values_any,
    table_any,
    wout_any,
    fgain_any,
    wgate_any,
    wup_any,
    wdown_any,
    len_any,
    freq_any,
    both_ref,
    hidden,
    gain,
    wqkv,
    keys,
    values,
    table,
    wout,
    fgain,
    wgate,
    wup,
    wdown,
    len_ref,
    freq_ref,
    load_sem,
    qkv_out1,
    qkv_in1,
    qkv_out2,
    qkv_in2,
    live_buf,
    part_out1,
    part_in1,
    part_out2,
    part_in2,
    proj_buf,
    chunk_out,
    chunk_in,
    piece_out,
    piece_in,
    act_buf,
    down_buf,
    send_sem,
    recv_sem,
):
    seq = lax.axis_index("seq")
    head = lax.axis_index("head")
    core = lax.rem(head, 2)
    row_y = seq // SIDE
    row_z = lax.rem(seq, SIDE)
    first = row_y + core * (row_z - row_y)
    second = row_z + core * (row_y - row_z)

    def seq_of(one, two):
        return one * (SIDE - (SIDE - 1) * core) + two * (1 + (SIDE - 1) * core)

    def first_peer(d):
        other = lax.rem(first + d, SIDE)
        return other, (seq_of(other, second), head)

    def second_peer(d):
        other = lax.rem(second + d, SIDE)
        return other, (seq_of(first, other), head)

    def head_peer(d):
        other = lax.rem(head + d, HEADS)
        return other, (seq, other)

    loads = {}

    def load(index, name, src, dst):
        loads[name] = pltpu.make_async_copy(src, dst, load_sem.at[index])
        loads[name].start()

    barrier = pltpu.get_barrier_semaphore()

    @pl.loop(0, PEERS)
    def announce(i):
        pl.semaphore_signal(barrier, inc=1, device_id=first_peer(ring_distance(i))[1], device_id_type=MESH)

    load(0, "hidden", hidden_any, hidden)
    load(1, "gain", gain_any, gain)
    load(2, "wqkv", wqkv_any, wqkv)
    load(3, "table", table_any, table)
    load(4, "lengths", len_any, len_ref)
    load(5, "freq", freq_any, freq_ref)

    @pl.loop(0, PEERS)
    def announce_more(i):
        for peer in (second_peer, head_peer):
            pl.semaphore_signal(barrier, inc=1, device_id=peer(ring_distance(i))[1], device_id_type=MESH)

    def exchange(step, peer, src_of, dst_of):
        @pl.loop(0, PEERS)
        def send(i):
            d = ring_distance(i)
            other, device = peer(d)
            pltpu.make_async_remote_copy(
                src_ref=src_of(other),
                dst_ref=dst_of(d),
                send_sem=send_sem.at[step],
                recv_sem=recv_sem.at[step],
                device_id=device,
                device_id_type=MESH,
            ).start()

    def arrive(step, blocks, count=PEERS):
        some = blocks.at[pl.ds(0, count)]
        pltpu.make_async_copy(some, some, recv_sem.at[step]).wait()

    def departed(step, blocks, count=PEERS):
        some = blocks.at[pl.ds(0, count)]
        pltpu.make_async_copy(some, some, send_sem.at[step]).wait()

    loads["hidden"].wait()
    loads["gain"].wait()
    stream = hidden[...].astype(f32)
    scaled = (stream * gain[...].astype(f32)).astype(bf16)
    square = jnp.broadcast_to(jnp.sum(stream * stream, axis=1, keepdims=True), (REQUESTS, LANES))
    loads["wqkv"].wait()
    part = jnp.dot(scaled, wqkv[...], preferred_element_type=f32)
    total = jnp.concatenate([part, square], axis=1)
    qkv_out1[...] = total.astype(bf16)

    pl.semaphore_wait(barrier, 21)
    exchange(0, first_peer, lambda o: qkv_out1, lambda d: qkv_in1.at[d - 1])

    load(6, "keys", keys_any, keys)
    load(7, "values", values_any, values)
    load(8, "wout", wout_any, wout)
    load(9, "fgain", fgain_any, fgain)
    load(10, "wgate", wgate_any, wgate)
    load(11, "wup", wup_any, wup)
    load(12, "wdown", wdown_any, wdown)

    sub = lax.broadcasted_iota(jnp.int32, (8, 1), 0)
    request = lax.rem(sub, REQUESTS)
    length = jnp.zeros((8, 1), jnp.int32)
    loads["lengths"].wait()
    for b in range(REQUESTS):
        length = jnp.where(request == b, len_ref[b], length)
    loads["table"].wait()
    pages = table[...]
    pages = jnp.concatenate([pages, pages], axis=0)
    page_count = pages.shape[1]
    page_index = lax.broadcasted_iota(jnp.int32, (8, page_count), 1)
    lane = lax.broadcasted_iota(jnp.int32, (8, LANES), 1)
    for j in range(SLOTS):
        hit = jnp.sum(
            jnp.where(pages == seq * SLOTS + j, (page_index + 1).astype(f32), 0.0), axis=1, keepdims=True
        ).astype(jnp.int32)
        limit = jnp.where(hit > 0, length - (hit - 1) * PAGE_TOKENS, 0)
        live_buf[:, j * LANES : (j + 1) * LANES] = jnp.where(lane < limit, 1.0, 0.0)
    mine_page = (page_index == length // PAGE_TOKENS) & (pages >= seq * SLOTS) & (pages < (seq + 1) * SLOTS)
    mine = jnp.sum(jnp.where(mine_page, 1.0, 0.0), axis=1, keepdims=True) > 0.5
    loads["freq"].wait()
    angle = length.astype(f32) * freq_ref[...]
    cos_part = jnp.cos(angle)
    sine_part = jnp.sin(angle)
    sine_part = jnp.where(lane < HEAD_SIZE // 2, -sine_part, sine_part)

    arrive(0, qkv_in1)
    for d in range(7):
        total = total + qkv_in1[d].astype(f32)
    qkv_out2[...] = total.astype(bf16)
    exchange(1, second_peer, lambda o: qkv_out2, lambda d: qkv_in2.at[d - 1])
    loads["keys"].wait()
    loads["values"].wait()
    arrive(1, qkv_in2)
    for d in range(7):
        total = total + qkv_in2[d].astype(f32)

    inv_rms = lax.rsqrt(total[:, (GROUP + 2) * LANES :] / MODEL_WIDTH + epsilon)
    joined = jnp.concatenate(
        [total[:, t * LANES : (t + 1) * LANES] * inv_rms for t in range(GROUP + 2)], axis=0
    ).reshape(5, 8, LANES)
    swapped = pltpu.roll(joined.reshape(40, LANES), HEAD_SIZE // 2, 1).reshape(5, 8, LANES)
    turned = joined * cos_part + swapped * sine_part
    queries = turned[0:4].reshape(ROWS, LANES).astype(bf16)
    new_key = turned[4][0:4].astype(bf16).astype(f32)
    new_key = jnp.concatenate([new_key, new_key], axis=0)
    new_value = joined[4][4:8].astype(bf16).astype(f32)
    new_value = jnp.concatenate([new_value, new_value], axis=0)

    scale = 1.0 / math.sqrt(HEAD_SIZE)
    tokens = SLOTS * PAGE_TOKENS
    scores = lax.dot_general(
        queries,
        keys[...].reshape(tokens, HEAD_SIZE),
        (((1,), (1,)), ((), ())),
        preferred_element_type=f32,
    )
    live = live_buf[...] > 0.5
    masked = jnp.where(live, scores.reshape(4, 8, tokens) * scale, neg_fill)
    new_score = (
        jnp.sum(queries.astype(f32).reshape(4, 8, LANES) * new_key, axis=2, keepdims=True) * scale
    )
    peak = jnp.maximum(
        jnp.max(masked, axis=2, keepdims=True), jnp.where(mine, new_score, neg_fill)
    )
    weight = jnp.where(live, jnp.exp(masked - peak), 0.0)
    new_weight = jnp.where(mine, jnp.exp(new_score - peak), 0.0)
    denom = jnp.sum(weight, axis=2, keepdims=True) + new_weight
    accum = jnp.dot(
        weight.reshape(ROWS, tokens).astype(bf16),
        values[...].reshape(tokens, HEAD_SIZE),
        preferred_element_type=f32,
    ).reshape(4, 8, LANES)
    accum = accum + new_weight.astype(bf16).astype(f32) * new_value
    some = denom > 0.0
    safe = jnp.where(some, denom, 1.0)
    mean = (accum / safe).reshape(ROWS, LANES)
    lse = jnp.where(some, peak + jnp.log(safe), neg_fill).reshape(ROWS, 1)

    tiles = [slice(g * REQUESTS, (g + 1) * REQUESTS) for g in range(GROUP)]
    means = [mean[rows] for rows in tiles]
    column = lax.broadcasted_iota(jnp.int32, (REQUESTS, LANES), 1)
    stats = jnp.zeros((REQUESTS, LANES), f32)
    for g, rows in enumerate(tiles):
        stats = jnp.where(column == g, lse[rows], stats)

    def packed(means, stats):
        high = stats.astype(bf16).astype(f32)
        rest = stats - high
        middle = rest.astype(bf16).astype(f32)
        low = rest - middle
        side = high + pltpu.roll(middle, GROUP, 1) + pltpu.roll(low, 2 * GROUP, 1)
        return jnp.concatenate(means + [side], axis=1).astype(bf16)

    def merged(means, stats, arrived):
        blocks = [means]
        lses = [stats]
        for d in range(PEERS):
            block = arrived[d].astype(f32)
            blocks.append([block[:, g * LANES : (g + 1) * LANES] for g in range(GROUP)])
            side = block[:, GROUP * LANES :]
            side = side + pltpu.roll(side, LANES - GROUP, 1) + pltpu.roll(side, LANES - 2 * GROUP, 1)
            lses.append(jnp.where(column < GROUP, side, 0.0))
        best = functools.reduce(jnp.maximum, lses)
        factors = [jnp.exp(part - best) for part in lses]
        whole = functools.reduce(jnp.add, factors)
        factors = [factor / whole for factor in factors]
        means = [
            functools.reduce(
                jnp.add, [factor[:, g : g + 1] * block[g] for factor, block in zip(factors, blocks)]
            )
            for g in range(GROUP)
        ]
        return means, jnp.where(column < GROUP, best + jnp.log(whole), 0.0)

    part_out1[...] = packed(means, stats)
    exchange(2, first_peer, lambda o: part_out1, lambda d: part_in1.at[d - 1])
    loads["wout"].wait()
    loads["fgain"].wait()
    arrive(2, part_in1)
    means, stats = merged(means, stats, part_in1)
    part_out2[...] = packed(means, stats)
    exchange(3, second_peer, lambda o: part_out2, lambda d: part_in2.at[d - 1])
    loads["wgate"].wait()
    loads["wup"].wait()
    loads["wdown"].wait()
    arrive(3, part_in2)
    means, _ = merged(means, stats, part_in2)

    attention = jnp.concatenate(means, axis=1).astype(bf16)
    proj_buf[head] = jnp.dot(attention, wout[...], preferred_element_type=f32)
    exchange(4, head_peer, lambda o: proj_buf.at[head], lambda d: proj_buf.at[head])
    arrive(4, proj_buf)
    projected = proj_buf[0]
    for h in range(1, HEADS):
        projected = projected + proj_buf[h]
    attended = (stream + projected).astype(bf16)
    after = attended.astype(f32)
    ffn = (after * fgain[...].astype(f32)).astype(bf16)
    square = jnp.broadcast_to(jnp.sum(after * after, axis=1, keepdims=True), (REQUESTS, LANES))

    gate_part = jnp.dot(ffn, wgate[...], preferred_element_type=f32)
    up_part = jnp.dot(ffn, wup[...], preferred_element_type=f32)
    for c in range(CLASSES):
        span = slice(c * CHUNK, (c + 1) * CHUNK)
        chunk_out[c] = jnp.concatenate([gate_part[:, span], up_part[:, span], square], axis=1).astype(bf16)

    exchange(
        5, first_peer, lambda o: chunk_out.at[lax.rem(o, CLASSES)], lambda d: chunk_in.at[d - 1]
    )
    mine = lax.rem(first, CLASSES)
    total = chunk_out[mine].astype(f32)
    arrive(5, chunk_in)
    for d in range(PEERS):
        total = total + chunk_in[d].astype(f32)
    piece_out[...] = total.astype(bf16)
    exchange(6, second_peer, lambda o: piece_out, lambda d: piece_in.at[d - 1])
    arrive(6, piece_in)
    for d in range(PEERS):
        total = total + piece_in[d].astype(f32)
    inv_norm = lax.rsqrt(total[:, 2 * CHUNK : 2 * CHUNK + 1] / MODEL_WIDTH + epsilon)
    gate = total[:, :CHUNK] * inv_norm
    act = gate / (1.0 + jnp.exp(-gate)) * (total[:, CHUNK : 2 * CHUNK] * inv_norm)
    act_buf[mine] = act.astype(bf16)

    for d in (2, 1, SIDE - 1):
        _, device = first_peer(d)
        pltpu.make_async_remote_copy(
            src_ref=act_buf.at[mine],
            dst_ref=act_buf.at[mine],
            send_sem=send_sem.at[7],
            recv_sem=recv_sem.at[7],
            device_id=device,
            device_id_type=MESH,
        ).start()
    arrive(7, act_buf, CLASSES - 1)
    units = jnp.concatenate([act_buf[c] for c in range(CLASSES)], axis=1)
    down_buf[head] = jnp.dot(units, wdown[...], preferred_element_type=f32)
    exchange(8, head_peer, lambda o: down_buf.at[head], lambda d: down_buf.at[head])
    arrive(8, down_buf)
    down = down_buf[0]
    for h in range(1, HEADS):
        down = down + down_buf[h]
    both_ref[...] = jnp.concatenate([after, after + down], axis=0).astype(bf16)
    departed(0, qkv_in1)
    departed(1, qkv_in2)
    departed(2, part_in1)
    departed(3, part_in2)
    departed(4, proj_buf)
    departed(5, chunk_in)
    departed(6, piece_in)
    departed(7, act_buf, CLASSES - 1)
    departed(8, down_buf)


def on_device(
    hidden_state,
    attn_gain,
    query_key_value_weight,
    key_page_cache,
    value_page_cache,
    page_table,
    lengths,
    out_weight,
    ffn_gain,
    gate_weight,
    up_weight,
    down_weight,
):
    requests, width = hidden_state.shape
    arrays = (
        hidden_state,
        attn_gain.reshape(1, width),
        query_key_value_weight,
        key_page_cache,
        value_page_cache,
        page_table,
        out_weight,
        ffn_gain.reshape(1, width),
        gate_weight,
        up_weight,
        down_weight,
        lengths,
        jnp.asarray(rope_frequencies()),
    )
    hbm_spec = pl.BlockSpec(memory_space=pltpu.HBM)
    vmem_spec = pl.BlockSpec(memory_space=pltpu.VMEM)
    out = pltpu.VMEM((2 * requests, width), bf16)
    qkv_width, part_width = (GROUP + 3) * LANES, (GROUP + 1) * LANES
    both = pl.pallas_call(
        layer,
        out_shape=out,
        in_specs=[hbm_spec] * len(arrays),
        out_specs=vmem_spec,
        scratch_shapes=[
            pltpu.SMEM(a.shape, a.dtype) if a is lengths else pltpu.VMEM(a.shape, a.dtype) for a in arrays
        ]
        + [
            pltpu.SemaphoreType.DMA((len(arrays),)),
            pltpu.VMEM((requests, qkv_width), bf16),
            pltpu.VMEM((PEERS, requests, qkv_width), bf16),
            pltpu.VMEM((requests, qkv_width), bf16),
            pltpu.VMEM((PEERS, requests, qkv_width), bf16),
            pltpu.VMEM((8, SLOTS * PAGE_TOKENS), f32),
            pltpu.VMEM((requests, part_width), bf16),
            pltpu.VMEM((PEERS, requests, part_width), bf16),
            pltpu.VMEM((requests, part_width), bf16),
            pltpu.VMEM((PEERS, requests, part_width), bf16),
            pltpu.VMEM((HEADS, REQUESTS, LANES), f32),
            pltpu.VMEM((CLASSES, REQUESTS, 2 * CHUNK + LANES), bf16),
            pltpu.VMEM((PEERS, REQUESTS, 2 * CHUNK + LANES), bf16),
            pltpu.VMEM((REQUESTS, 2 * CHUNK + LANES), bf16),
            pltpu.VMEM((PEERS, REQUESTS, 2 * CHUNK + LANES), bf16),
            pltpu.VMEM((CLASSES, REQUESTS, CHUNK), bf16),
            pltpu.VMEM((HEADS, REQUESTS, LANES), f32),
            pltpu.SemaphoreType.DMA((9,)),
            pltpu.SemaphoreType.DMA((9,)),
        ],
        compiler_params=pltpu.CompilerParams(
            collective_id=0, has_side_effects=True, vmem_limit_bytes=48 * 1024 * 1024
        ),
    )(*[pltpu.with_memory_space_constraint(a, pltpu.HBM) for a in arrays])
    return both[:requests], both[requests:]


def solution(mesh):
    in_specs = (
        P(None, "seq"),
        P("seq"),
        P("seq", "head"),
        P("seq", None, "head"),
        P("seq", None, "head"),
        P(),
        P(),
        P("head", "seq"),
        P("seq"),
        P("seq", "head"),
        P("seq", "head"),
        P("head", "seq"),
    )
    out_specs = (P(None, "seq"), P(None, "seq"))
    return jax.shard_map(
        on_device, mesh=mesh, in_specs=in_specs, out_specs=out_specs, check_vma=False
    )
```
